32 devices in a mesh: dp: 8 (over y, x, core), tensor: 4 (over z).
Axes of the slice: x: 2, y: 2, z: 4, core: 2. Of those that a mesh axis runs over, the one named last changes fastest.
Arguments:
- tokens: bfloat16 [8, 1032, 1024], P('dp', 'tensor'), may hold values from -6 to 6
- cotangent: bfloat16 [8, 1032, 1024], P('dp', 'tensor'), may hold values from -6 to 6
- w_qkv: bfloat16 [3, 1024, 1024], P(None, 'dp', 'tensor'), may hold values from -0.1875 to 0.1875
- w_o: bfloat16 [1024, 1024], P('tensor', 'dp'), may hold values from -0.1875 to 0.1875
- w_gu: bfloat16 [2, 1024, 2736], P(None, 'dp', 'tensor'), may hold values from -0.1875 to 0.1875
- w_down: bfloat16 [2736, 1024], P('tensor', 'dp'), may hold values from -0.109375 to 0.109375
- norm_params: float32 [6, 1024], replicated, may hold values from -1.5 to 1.65, as said below
- head_params: float32 [4, 1024], replicated, may hold values from -1.5 to 1.65, as said below
- ffn_params: float32 [4, 2736], replicated, may hold values from -1.5 to 1.65, as said below
- token_mask: int32 [8, 1032], P('dp'), may hold values from 0 to 1, as said below
- empty_flag: int32 [8], P('dp'), may hold values from 0 to 1, as said below
- coords: int32 [8, 2, 1032], P('dp'), may hold values from 0 to 31, as said below
Outputs:
- layer_out: bfloat16 [8, 1032, 1024], P('dp', 'tensor')
- d_tokens: float32 [8, 1032, 1024], P('dp', 'tensor')
- d_w_qkv: float32 [3, 1024, 1024], P(None, 'dp', 'tensor')
- d_w_o: float32 [1024, 1024], P('tensor', 'dp')
- d_w_gu: float32 [2, 1024, 2736], P(None, 'dp', 'tensor')
- d_w_down: float32 [2736, 1024], P('tensor', 'dp')
- d_norm_params: float32 [6, 1024], replicated
- d_head_params: float32 [4, 1024], replicated
- d_ffn_params: float32 [4, 2736], replicated
The draws below stay inside these ranges and needn't reach their ends.
Inputs may be any that keep to these rules, and one draw needn't show every extreme that they name: `token_mask`: in every image slot 0 (the class token) is 1, the patch slots 1 to 1024 are 1 or 0, and the later slots are 0. `empty_flag`: at least one image is flagged. `coords`: row 0 holds grid rows, row 1 grid columns; the patch slots of an image hold every position of the 32 x 32 grid once, in an order drawn per image; slot 0 and the later slots hold 0. `norm_params`: gain rows lie within 0.6 to 1.65, the other rows within -1.5 to 1.5. `head_params`: gain rows lie within 0.6 to 1.65, the other rows within -1.5 to 1.5. `ffn_params`: gain rows lie within 0.6 to 1.65, the other rows within -1.5 to 1.5.
All inputs are finite; a program needn't handle non-finite values.
Results may differ from the reference program's by a relative error of at most 0.015.
Values may be sent and summed in bfloat16 or wider, within the bound.
No kernel may reach another device: no remote copies, remote signals or barrier semaphores. Data moves between devices by JAX's collectives and lax.ppermute only.
A program may use at most 192 MiB of HBM per device.

```python
import math
import jax
import jax.numpy as jnp
from jax import lax

D = 1024
H = 16
FF = 2730
HD = 64
FF_PAD = 2736
GRID = 32
SEQ = 1032
IMAGES = 8


def small_rows(key, row_kinds, full_width):
    stacked = []
    for index_r, row_kind in enumerate(row_kinds):
        sub_key = jax.random.fold_in(key, index_r + 11)
        if row_kind == 'gain':
            stacked.append(jnp.exp(jax.random.uniform(sub_key, (full_width,), jnp.float32, -0.5, 0.5)))
        else:
            stacked.append(jnp.clip(0.5 * jax.random.normal(sub_key, (full_width,), jnp.float32), -1.5, 1.5))
    return jnp.stack(stacked)


def draw_norm_params(key, part):
    return small_rows(key, ('gain', 'shift', 'gain', 'shift', 'shift', 'shift'), D)


def draw_head_params(key, part):
    return small_rows(key, ('shift', 'shift', 'gain', 'shift'), D)


def draw_ffn_params(key, part):
    return small_rows(key, ('shift', 'shift', 'gain', 'shift'), FF_PAD)


def draw_token_mask(key, part):
    rolls = jax.random.randint(key, (IMAGES, SEQ), 0, 16)
    slot_ids = jnp.arange(SEQ)[None, :]
    patch_kept = (rolls > 0).astype(jnp.int32)
    kept = jnp.where(slot_ids == 0, 1, jnp.where(slot_ids <= GRID * GRID, patch_kept, 0))
    return kept.astype(jnp.int32)


def draw_empty_flag(key, part):
    chosen = jax.random.randint(jax.random.fold_in(key, 5), (), 0, IMAGES)
    extra = jax.random.randint(jax.random.fold_in(key, 7), (IMAGES,), 0, 4)
    flagged = jnp.logical_or(jnp.arange(IMAGES) == chosen, extra == 0)
    return flagged.astype(jnp.int32)


def draw_coords(key, part):
    key_list = jax.random.split(key, IMAGES)

    def one_order(sub_key):
        return jax.random.permutation(sub_key, GRID * GRID).astype(jnp.int32)
    orders = jax.vmap(one_order)(key_list)
    slots_full = jnp.zeros((IMAGES, SEQ), jnp.int32)
    slots_full = slots_full.at[:, 1:1 + GRID * GRID].set(orders)
    return jnp.stack([slots_full // GRID, slots_full % GRID], axis=1).astype(jnp.int32)


def levels(rng, extent, cuts, low, high):
    level = 1.0
    for dim, blocks in cuts:
        draws = jax.random.uniform(jax.random.fold_in(jax.random.fold_in(rng, 6), dim), (blocks,), jnp.float32, low / len(cuts), high / len(cuts))
        level = level * jnp.repeat(jnp.exp(draws), extent[dim] // blocks).reshape((-1,) + (1,) * (len(extent) - 1 - dim))
    return level


def normal_values(own_key, shape, spread, bound, cuts=(), held_as=jnp.bfloat16):
    entries = spread * jax.random.normal(own_key, shape, jnp.float32)
    if cuts:
        entries = entries * levels(own_key, shape, cuts, -0.22, 0.18)
    return jnp.clip(entries, -bound, bound).astype(held_as)


def setup_inputs(seed: int = 0) -> dict:
    keys = jax.random.split(jax.random.key(seed), 13)
    return {
        "tokens": normal_values(keys[0], (IMAGES, SEQ, D), 1.0, 6.0, ((0, 8), (1, 4))),
        "cotangent": normal_values(keys[1], (IMAGES, SEQ, D), 1.0, 6.0, ((0, 8), (1, 4))),
        "w_qkv": normal_values(keys[2], (3, D, D), D ** -0.5, 0.1875, ((1, 8), (2, 4))),
        "w_o": normal_values(keys[3], (D, D), D ** -0.5, 0.1875, ((0, 4), (1, 8))),
        "w_gu": normal_values(keys[4], (2, D, FF_PAD), D ** -0.5, 0.1875, ((1, 8), (2, 4))),
        "w_down": normal_values(keys[5], (FF_PAD, D), FF ** -0.5, 0.109375, ((0, 4), (1, 8))),
        "norm_params": draw_norm_params(jax.random.fold_in(keys[12], 71), 0),
        "head_params": draw_head_params(jax.random.fold_in(keys[12], 71), 0),
        "ffn_params": draw_ffn_params(jax.random.fold_in(keys[12], 71), 0),
        "token_mask": draw_token_mask(jax.random.fold_in(keys[12], 71), 0),
        "empty_flag": draw_empty_flag(jax.random.fold_in(keys[12], 71), 0),
        "coords": draw_coords(jax.random.fold_in(keys[12], 71), 0),
    }


@jax.custom_vjp
def low(v):
    return lax.optimization_barrier(v.astype(jnp.bfloat16)).astype(jnp.float32)

@jax.custom_vjp
def low_back(v):
    return v

def low_keep(v):
    return (low(v), None)

def low_pass(kept, grad):
    return (grad,)

def back_keep(v):
    return (v, None)

def back_low(kept, grad):
    return (low(grad),)
low.defvjp(low_keep, low_pass)
low_back.defvjp(back_keep, back_low)

def layer_norm(values_in, gain_vec, shift_vec, mask_vec, unit_count):
    mean_row = lax.optimization_barrier(jnp.sum(values_in * mask_vec, axis=-1, keepdims=True)) / unit_count
    power_row = lax.optimization_barrier(jnp.sum(values_in * values_in * mask_vec, axis=-1, keepdims=True)) / unit_count
    unit_value = (values_in - mean_row) * lax.rsqrt(power_row - mean_row * mean_row + 1e-06)
    return mask_vec * (unit_value * gain_vec + shift_vec)

def rope_tables(coord_pair):
    half_dim = HD // 2
    index_j = jnp.arange(half_dim // 2).astype(jnp.float32)
    frequency = jnp.repeat(jnp.exp(index_j * (-2.0 * math.log(10000.0) / half_dim)), 2)
    places = coord_pair.astype(jnp.float32) * 0.5
    angles = jnp.concatenate([places[0][:, None] * frequency[None, :], places[1][:, None] * frequency[None, :]], axis=1)
    return (jnp.cos(angles)[:, None, :], jnp.sin(angles)[:, None, :])

def rotate(heads_in, cosine, sine_tab):
    pair_view = heads_in.reshape(heads_in.shape[:-1] + (heads_in.shape[-1] // 2, 2))
    turned = jnp.stack([-pair_view[..., 1], pair_view[..., 0]], axis=-1).reshape(heads_in.shape)
    return heads_in * cosine + turned * sine_tab

def block(params, image_rows, mask_row, empty_one, coord_pair):
    w_qkv, w_o, w_gu, w_down, norm_params, head_params, ffn_params = params
    highest = lax.Precision.HIGHEST
    keep_rows = (mask_row.astype(jnp.float32) * (1.0 - empty_one.astype(jnp.float32)))[:, None]
    valid_keys = mask_row > 0
    cosine, sine_tab = rope_tables(coord_pair)
    ones_vec = jnp.ones((D,), jnp.float32)
    normed = low(layer_norm(image_rows, norm_params[0], norm_params[1], ones_vec, D))
    query_pre = low_back(jnp.dot(normed, w_qkv[0], precision=highest) + head_params[0])
    key_pre = low_back(jnp.dot(normed, w_qkv[1], precision=highest))
    value_pre = low_back(jnp.dot(normed, w_qkv[2], precision=highest) + head_params[1])
    query_heads = low(rotate(query_pre.reshape(SEQ, H, HD), cosine, sine_tab))
    key_heads = low(rotate(key_pre.reshape(SEQ, H, HD), cosine, sine_tab))
    value_heads = low(value_pre.reshape(SEQ, H, HD))
    scores = low_back(jnp.einsum('qhd,khd->hqk', query_heads, key_heads, precision=highest) * HD ** (-0.5))
    scores = jnp.where(valid_keys[None, None, :], scores, -1e+30)
    row_max = lax.optimization_barrier(jnp.max(scores, axis=-1, keepdims=True))
    exp_score = jnp.exp(scores - row_max)
    attn_probs = low(exp_score / lax.optimization_barrier(jnp.sum(exp_score, axis=-1, keepdims=True)))
    mixed_heads = low_back(jnp.einsum('hqk,khd->qhd', attn_probs, value_heads, precision=highest).reshape(SEQ, D))
    inner_normed = low(layer_norm(mixed_heads, head_params[2], head_params[3], ones_vec, D))
    branch = low_back(jnp.dot(inner_normed, w_o, precision=highest) + norm_params[4])
    middle = image_rows + keep_rows * branch
    normed_two = low(layer_norm(middle, norm_params[2], norm_params[3], ones_vec, D))
    gate_act = low_back(jnp.dot(normed_two, w_gu[0], precision=highest) + ffn_params[0])
    up_act = low_back(jnp.dot(normed_two, w_gu[1], precision=highest) + ffn_params[1])
    hidden = gate_act / (1.0 + jnp.exp(-gate_act)) * up_act
    unit_mask = (jnp.arange(FF_PAD) < FF).astype(jnp.float32)
    ffn_normed = low(layer_norm(hidden, ffn_params[2], ffn_params[3], unit_mask, FF))
    branch_two = low_back(jnp.dot(ffn_normed, w_down, precision=highest) + norm_params[5])
    return middle + keep_rows * branch_two

def reference(tokens, cotangent, w_qkv, w_o, w_gu, w_down, norm_params, head_params, ffn_params, token_mask, empty_flag, coords):
    params = (w_qkv.astype(jnp.float32), w_o.astype(jnp.float32), w_gu.astype(jnp.float32), w_down.astype(jnp.float32), norm_params.astype(jnp.float32), head_params.astype(jnp.float32), ffn_params.astype(jnp.float32))

    def whole_layer(params, images_in):

        def one_image(item_pack):
            image_rows, mask_row, empty_one, coord_pair = item_pack
            return block(params, image_rows, mask_row, empty_one, coord_pair)
        return lax.map(jax.checkpoint(one_image), (images_in, token_mask, empty_flag, coords))
    layer_out, pull_back = jax.vjp(whole_layer, params, tokens.astype(jnp.float32))
    weight_grads, d_tokens = pull_back(cotangent.astype(jnp.float32))
    return (layer_out.astype(jnp.bfloat16), d_tokens, weight_grads[0], weight_grads[1], weight_grads[2], weight_grads[3], weight_grads[4], weight_grads[5], weight_grads[6])
```

```python
import functools
import math

import jax
import jax.numpy as jnp
from jax import lax
from jax.experimental import pallas as pl
from jax.experimental.pallas import tpu as pltpu
from jax.sharding import PartitionSpec as P

FF = 2730
HD = 64
FF_PAD = 2736
LANES = 128
EPS = 1e-06
VMEM_LIMIT = 44 * 2**20
BF = jnp.bfloat16
F32 = jnp.float32
NT = (((1,), (1,)), ((), ()))
TN = (((0,), (0,)), ((), ()))


def ring_up(value, size):
    return lax.ppermute(value, "tensor", [(j, (j + 1) % size) for j in range(size)])


def ring_down(value, size):
    return lax.ppermute(value, "tensor", [(j, (j - 1) % size) for j in range(size)])


def ring_offsets(size):
    ups = size // 2
    return [0] + [-s for s in range(1, ups + 1)] + [s for s in range(1, size - ups)]


def ring_gather(own, size):
    ups = size // 2
    downs = size - 1 - ups
    upper, lower = [], []
    up_now, down_now = own, own
    for s in range(ups):
        up_now = ring_up(up_now, size)
        upper.append(up_now)
        if s < downs:
            down_now = ring_down(down_now, size)
            lower.append(down_now)
    return [own] + upper + lower


def add_low(left, right):
    return (left.astype(F32) + right.astype(F32)).astype(BF)


def ring_scatter(pieces, size):
    ups = size // 2
    downs = size - 1 - ups
    if size == 1:
        return pieces
    place = {offset % size: at for at, offset in enumerate(ring_offsets(size))}
    up_now = pieces[place[ups % size]]
    down_now = pieces[place[-downs % size]] if downs else None
    for s in range(ups, 0, -1):
        up_now = ring_up(up_now, size)
        if s > 1:
            up_now = add_low(up_now, pieces[place[s - 1]])
        if s <= downs:
            down_now = ring_down(down_now, size)
            if s > 1:
                down_now = add_low(down_now, pieces[place[(1 - s) % size]])
    return [pieces[0], up_now] + ([down_now] if downs else [])


def dp_bits(size):
    bits = []
    step = 2
    while step < size:
        bits.append(step)
        step *= 2
    return bits + ([1] if size > 1 else [])


def flip(value, bit, size):
    return lax.ppermute(value, "dp", [(j, j ^ bit) for j in range(size)])


def dp_gather(block, size):
    stacked = block[None]
    for bit in dp_bits(size):
        stacked = jnp.concatenate([stacked, flip(stacked, bit, size)], axis=0)
    return stacked


def dp_order(size):
    order = [0]
    for bit in dp_bits(size):
        order = order + [at ^ bit for at in order]
    return jnp.array(order, jnp.int32) ^ lax.axis_index("dp")


def dp_scatter(blocks, size):
    if size == 1:
        return blocks[0].astype(F32)
    parity = lax.axis_index("dp") % 2
    pairs = blocks.reshape((size // 2, 2) + blocks.shape[1:])
    away = lax.dynamic_index_in_dim(pairs, 1 - parity, 1, keepdims=False)
    kept = lax.dynamic_index_in_dim(pairs, parity, 1, keepdims=False)
    merged = add_low(kept, flip(away, 1, size))
    groups = [[j for j in range(size) if j % 2 == c] for c in range(2)]
    parts = lax.all_to_all(
        merged, "dp", split_axis=0, concat_axis=0, tiled=True, axis_index_groups=groups
    )
    return jnp.sum(parts.astype(F32), axis=0)


def sum_everywhere(value, dp_size, tensor_size):
    for bit in reversed(dp_bits(dp_size)):
        value = value + flip(value, bit, dp_size)
    step = 1
    while step < tensor_size:
        value = value + lax.ppermute(
            value, "tensor", [(j, j ^ step) for j in range(tensor_size)]
        )
        step *= 2
    return value


def whole(shape):
    return pl.BlockSpec(shape, lambda *_: (0,) * len(shape))


def lead(shape):
    return pl.BlockSpec((1,) + shape, lambda s, *_: (s,) + (0,) * len(shape))


def ordered(shape):
    return pl.BlockSpec((1,) + shape, lambda s, order: (order[s],) + (0,) * len(shape))


def call(body, args, specs, outs, out_specs, grid, scratch=(), prefetch=0, flops=0):
    moved = sum(a.size * a.dtype.itemsize for a in args)
    moved += sum(math.prod(o.shape) * jnp.dtype(o.dtype).itemsize for o in outs)
    return pl.pallas_call(
        body,
        out_shape=outs,
        grid_spec=pltpu.PrefetchScalarGridSpec(
            num_scalar_prefetch=prefetch,
            grid=grid,
            in_specs=specs,
            out_specs=out_specs,
            scratch_shapes=list(scratch),
        ),
        compiler_params=pltpu.CompilerParams(vmem_limit_bytes=VMEM_LIMIT),
        cost_estimate=pl.CostEstimate(
            flops=int(flops), bytes_accessed=int(moved), transcendentals=0
        ),
    )(*args)


def sds(shape, dtype):
    return jax.ShapeDtypeStruct(shape, dtype)


def row_stats(rows, count):
    mean = jnp.sum(rows, axis=1, keepdims=True) / count
    power = jnp.sum(rows * rows, axis=1, keepdims=True) / count
    return mean, lax.rsqrt(power - mean * mean + EPS)


def rows_back(upstream, gain, unit, inv, count):
    scaled = upstream * gain
    first = jnp.sum(scaled, axis=1, keepdims=True) / count
    second = jnp.sum(scaled * unit, axis=1, keepdims=True) / count
    return inv * (scaled - first - unit * second)


def down_sum(rows):
    return jnp.sum(rows, axis=0, keepdims=True)


def put_back_body(order_ref, in_ref, out_ref):
    out_ref[...] = in_ref[0]


def put_back(order, stacked, axis):
    size = stacked.shape[0]
    block = stacked.shape[1:]
    shape = tuple(n * size if at == axis else n for at, n in enumerate(block))
    if block[axis] % (LANES if axis == len(block) - 1 else 16):
        placed = jnp.zeros_like(stacked).at[order].set(stacked)
        return jnp.moveaxis(placed, 0, axis).reshape(shape)
    return call(
        put_back_body,
        (order, stacked),
        [pl.BlockSpec((1,) + block, lambda r, order: (r,) + (0,) * len(block))],
        [sds(shape, stacked.dtype)],
        [
            pl.BlockSpec(
                block,
                lambda r, order: tuple(order[r] if at == axis else 0 for at in range(len(block))),
            )
        ],
        (size,),
        prefetch=1,
    )[0]


def first_norm_body(tokens_ref, dy_ref, keep_ref, norm_ref, normed_ref, low_ref):
    rows = tokens_ref[...].astype(F32)
    mean, inv = row_stats(rows, rows.shape[1])
    normed_ref[...] = ((rows - mean) * inv * norm_ref[0:1, :] + norm_ref[1:2, :]).astype(BF)
    low_ref[...] = (keep_ref[...] * dy_ref[...].astype(F32)).astype(BF)


def spread(table, width):
    return table if width == LANES else jnp.concatenate([table] * (width // LANES), axis=1)


def turn_pairs(rows):
    width = rows.shape[1]
    even = lax.broadcasted_iota(jnp.int32, (1, width), 1) % 2 == 0
    return jnp.where(even, -pltpu.roll(rows, width - 1, 1), pltpu.roll(rows, 1, 1))


def project_body(count, *refs):
    chunk_refs = refs[:count]
    w_ref, head_ref, cos_ref, sin_ref, q_ref, k_ref, v_ref, held = refs[count:]
    for at in range(count):

        @pl.when(pl.program_id(0) == at)
        def _():
            held[...] = chunk_refs[at][...]

    rows = held[...]
    width = w_ref.shape[2]
    cosine, sine = spread(cos_ref[0], width), spread(sin_ref[0], width)
    query = jnp.dot(rows, w_ref[0], preferred_element_type=F32) + head_ref[0:1, :]
    key = jnp.dot(rows, w_ref[1], preferred_element_type=F32)
    value = jnp.dot(rows, w_ref[2], preferred_element_type=F32) + head_ref[1:2, :]
    query_low = (query * cosine + turn_pairs(query) * sine).astype(BF)
    q_ref[0] = (query_low.astype(F32) * HD ** (-0.5)).astype(BF)
    k_ref[0] = (key * cosine + turn_pairs(key) * sine).astype(BF)
    v_ref[0] = value.astype(BF)


def head_lanes(width, head):
    lane = lax.broadcasted_iota(jnp.int32, (1, width), 1)
    return (lane >= head * HD) & (lane < (head + 1) * HD)


def attend_body(order_ref, q_ref, k_ref, v_ref, bias_ref, mixed_ref, lse_ref):
    query, keys, values, bias = q_ref[...], k_ref[...], v_ref[...], bias_ref[...]
    length, width = query.shape
    total = jnp.zeros((length, width), F32)
    for head in range(width // HD):
        mine = head_lanes(width, head)
        query_h = jnp.where(mine, query, jnp.zeros_like(query))
        scores = lax.dot_general(query_h, keys, NT, preferred_element_type=F32) + bias
        row_max = jnp.max(scores, axis=1, keepdims=True)
        exp_score = jnp.exp(scores - row_max)
        row_total = jnp.sum(exp_score, axis=1, keepdims=True)
        out = jnp.dot(exp_score.astype(BF), values, preferred_element_type=F32)
        total = jnp.where(mine, out * (1.0 / row_total), total)
        lse_ref[0, head : head + 1, :] = (row_max + jnp.log(row_total)).reshape(1, length)
    rows = mixed_ref.shape[1]
    for part in range(length // rows):
        at = order_ref[pl.program_id(0) * (length // rows) + part]
        mixed_ref[at] = total[part * rows : (part + 1) * rows].astype(BF)


def attend_back_body(
    order_ref,
    q_ref,
    dmix_ref,
    lse_ref,
    k_ref,
    v_ref,
    bias_ref,
    cos_ref,
    sin_ref,
    coss_ref,
    sins_ref,
    dq_ref,
    dk_ref,
    dv_ref,
    sums_ref,
    dk_sum,
    dv_sum,
):
    step = pl.program_id(0)

    @pl.when(step == 0)
    def _():
        dk_sum[...] = jnp.zeros_like(dk_sum)
        dv_sum[...] = jnp.zeros_like(dv_sum)
        sums_ref[...] = jnp.zeros_like(sums_ref)

    query, keys, values, bias = q_ref[...], k_ref[...], v_ref[...], bias_ref[...]
    length, width = query.shape
    rows = dmix_ref.shape[1]
    parts = length // rows
    d_mixed = jnp.concatenate([dmix_ref[order_ref[step * parts + p]] for p in range(parts)], axis=0)
    total = jnp.zeros((length, width), F32)
    for head in range(width // HD):
        mine = head_lanes(width, head)
        zero = jnp.zeros_like(query)
        query_h, d_mixed_h = jnp.where(mine, query, zero), jnp.where(mine, d_mixed, zero)
        scores = lax.dot_general(keys, query_h, NT, preferred_element_type=F32) + bias
        probs = jnp.exp(scores - lse_ref[0, head : head + 1, :])
        d_probs = lax.dot_general(values, d_mixed_h, NT, preferred_element_type=F32)
        d_scores = (probs * (d_probs - down_sum(probs * d_probs))).astype(BF)
        dv_sum[...] += jnp.dot(probs.astype(BF), d_mixed_h, preferred_element_type=F32)
        dk_sum[...] += jnp.dot(d_scores, query_h, preferred_element_type=F32)
        d_query = lax.dot_general(d_scores, keys, TN, preferred_element_type=F32)
        total = jnp.where(mine, d_query, total)
    total = total * HD ** (-0.5)
    cosine, sine = spread(cos_ref[...], width), spread(sin_ref[...], width)
    d_query_pre = (total * cosine - turn_pairs(total) * sine).astype(BF)
    dq_ref[...] = d_query_pre
    sums_ref[0:1, :] += down_sum(d_query_pre.astype(F32))

    @pl.when(step == pl.num_programs(0) - 1)
    def _():
        d_key = dk_sum[...]
        all_cos, all_sin = spread(coss_ref[...], width), spread(sins_ref[...], width)
        dk_ref[...] = (d_key * all_cos - turn_pairs(d_key) * all_sin).astype(BF)
        d_value_pre = dv_sum[...].astype(BF)
        dv_ref[...] = d_value_pre
        sums_ref[1:2, :] = down_sum(d_value_pre.astype(F32))


def mixed_rows(mixed_ref):
    parts = mixed_ref.shape[0]
    return jnp.concatenate([mixed_ref[p] for p in range(parts)], axis=1).astype(F32)


def middle_body(
    mixed_ref, tokens_ref, keep_ref, w_ref, norm_ref, head_ref, inner_ref, middle_ref, normed_ref
):
    mixed = mixed_rows(mixed_ref)
    mean, inv = row_stats(mixed, mixed.shape[1])
    inner = ((mixed - mean) * inv * head_ref[2:3, :] + head_ref[3:4, :]).astype(BF)
    inner_ref[...] = inner
    branch = jnp.dot(inner, w_ref[...], preferred_element_type=F32) + norm_ref[4:5, :]
    middle = tokens_ref[...].astype(F32) + keep_ref[...] * branch
    middle_ref[...] = middle
    mean, inv = row_stats(middle, middle.shape[1])
    normed_ref[...] = ((middle - mean) * inv * norm_ref[2:3, :] + norm_ref[3:4, :]).astype(BF)


def sigmoid(gate):
    return 1.0 / (1.0 + jnp.exp(-gate))


def ffn_body(count, order_ref, *refs):
    x_refs, e_refs = refs[:count], refs[count : 2 * count]
    (w_gu_ref, w_down_ref, ffn_ref, unit_ref, gate_ref, up_ref, d_ref, stats_ref, x_held, e_held) = (
        refs[2 * count :]
    )
    for at in range(count):

        @pl.when(pl.program_id(0) == at)
        def _():
            x_held[...] = x_refs[at][...]
            e_held[...] = e_refs[at][...]

    rows = x_held[...]
    gate = jnp.dot(rows, w_gu_ref[0], preferred_element_type=F32) + ffn_ref[0:1, :]
    up = jnp.dot(rows, w_gu_ref[1], preferred_element_type=F32) + ffn_ref[1:2, :]
    d_ffn = lax.dot_general(e_held[...], w_down_ref[...], NT, preferred_element_type=F32)
    gate_ref[0], up_ref[0], d_ref[0] = gate, up, d_ffn
    unit = unit_ref[...]
    hidden = gate * sigmoid(gate) * up
    masked = hidden * unit
    scaled = d_ffn * ffn_ref[2:3, :] * unit
    length = rows.shape[0]
    for at, term in enumerate((masked, masked * hidden, scaled, scaled * hidden)):
        stats_ref[0, at : at + 1, :] = jnp.sum(term, axis=1, keepdims=True).reshape(1, length)


def ffn_back_body(count, order_ref, *refs):
    gate_ref, up_ref, d_ref, stats_ref, w_gu_ref, ffn_ref, unit_ref = refs[:7]
    low_ref, dgate_ref, dup_ref, sums_ref = refs[7:11]
    out_refs = refs[11:]
    step = pl.program_id(0)

    @pl.when(step == 0)
    def _():
        sums_ref[...] = jnp.zeros_like(sums_ref)

    gate, up, d_ffn, unit = gate_ref[0], up_ref[0], d_ref[0], unit_ref[...]
    gain = ffn_ref[2:3, :]
    stats = stats_ref[0]
    mean = stats[:, 0:1] / FF
    inv = lax.rsqrt(stats[:, 1:2] / FF - mean * mean + EPS)
    first = stats[:, 2:3]
    second = inv * (stats[:, 3:4] - mean * first)
    sig = sigmoid(gate)
    silu = gate * sig
    unit_value = (silu * up - mean) * inv
    low_ref[0] = (unit * (unit_value * gain + ffn_ref[3:4, :])).astype(BF)
    d_hidden = unit * inv * (d_ffn * gain * unit - first / FF - unit_value * (second / FF))
    d_gate = (d_hidden * up * sig * (1.0 + gate * (1.0 - sig))).astype(BF)
    d_up = (d_hidden * silu).astype(BF)
    dgate_ref[0], dup_ref[0] = d_gate, d_up
    d_masked = d_ffn * unit
    sums_ref[0:1, :] += down_sum(d_gate.astype(F32))
    sums_ref[1:2, :] += down_sum(d_up.astype(F32))
    sums_ref[2:3, :] += down_sum(d_masked * unit_value)
    sums_ref[3:4, :] += down_sum(d_masked)
    out = lax.dot_general(d_gate, w_gu_ref[0], NT, preferred_element_type=F32)
    out += lax.dot_general(d_up, w_gu_ref[1], NT, preferred_element_type=F32)
    for at in range(count):

        @pl.when(step == at)
        def _():
            out_refs[at][...] = out.astype(BF)


def down_body(count, low_ref, w_ref, *out_refs):
    out = jnp.dot(low_ref[0], w_ref[...], preferred_element_type=F32)
    for at in range(count):

        @pl.when(pl.program_id(0) == at)
        def _():
            out_refs[at][...] = out.astype(BF)


def spread_back_body(count, dq_ref, dk_ref, dv_ref, w_ref, *out_refs):
    out = lax.dot_general(dq_ref[...], w_ref[0], NT, preferred_element_type=F32)
    out += lax.dot_general(dk_ref[...], w_ref[1], NT, preferred_element_type=F32)
    out += lax.dot_general(dv_ref[...], w_ref[2], NT, preferred_element_type=F32)
    for at in range(count):

        @pl.when(pl.program_id(0) == at)
        def _():
            out_refs[at][...] = out.astype(BF)


def add_terms(term_refs):
    total = term_refs[0][...].astype(F32)
    for ref in term_refs[1:]:
        total += ref[...].astype(F32)
    return total


def middle_back_body(count, *refs):
    upstream = add_terms(refs[:count])
    middle_ref, dy_ref, low_ref, keep_ref, mixed_ref, w_ref, norm_ref, head_ref = refs[
        count : count + 8
    ]
    dmid_ref, dbranch_ref, dmix_ref, sums_ref = refs[count + 8 :]
    middle = middle_ref[...]
    width = middle.shape[1]
    mean, inv = row_stats(middle, width)
    unit = (middle - mean) * inv
    d_middle = dy_ref[...].astype(F32) + rows_back(upstream, norm_ref[2:3, :], unit, inv, width)
    dmid_ref[...] = d_middle
    sums_ref[0:1, :] = down_sum(upstream * unit)
    sums_ref[1:2, :] = down_sum(upstream)
    d_branch = (keep_ref[...] * d_middle).astype(BF)
    dbranch_ref[...] = d_branch
    sums_ref[2:3, :] = down_sum(d_branch.astype(F32))
    sums_ref[3:4, :] = down_sum(low_ref[...].astype(F32))
    d_inner = lax.dot_general(d_branch, w_ref[...], NT, preferred_element_type=F32)
    mixed = mixed_rows(mixed_ref)
    mean, inv = row_stats(mixed, width)
    unit = (mixed - mean) * inv
    d_mixed = rows_back(d_inner, head_ref[2:3, :], unit, inv, width).astype(BF)
    part = mixed_ref.shape[2]
    for at in range(mixed_ref.shape[0]):
        dmix_ref[at] = d_mixed[:, at * part : (at + 1) * part]
    sums_ref[4:5, :] = down_sum(d_inner * unit)
    sums_ref[5:6, :] = down_sum(d_inner)
    sums_ref[6:8, :] = jnp.zeros((2, width), F32)


def first_back_body(count, *refs):
    upstream = add_terms(refs[:count])
    tokens_ref, dmid_ref, norm_ref, out_ref, sums_ref = refs[count:]
    rows = tokens_ref[...].astype(F32)
    width = rows.shape[1]
    mean, inv = row_stats(rows, width)
    unit = (rows - mean) * inv
    d_tokens = dmid_ref[...] + rows_back(upstream, norm_ref[0:1, :], unit, inv, width)
    out_ref[...] = d_tokens[: out_ref.shape[0]]
    sums_ref[0:1, :] = down_sum(upstream * unit)
    sums_ref[1:2, :] = down_sum(upstream)


def layer_out_body(count, *refs):
    branch = add_terms(refs[:count])
    middle_ref, keep_ref, norm_ref, out_ref = refs[count:]
    out = middle_ref[...] + keep_ref[...] * (branch + norm_ref[5:6, :])
    out_ref[...] = out[: out_ref.shape[0]].astype(BF)


def rope_tables(coords):
    half_dim = HD // 2
    index_j = jnp.arange(half_dim // 2).astype(F32)
    frequency = jnp.repeat(jnp.exp(index_j * (-2.0 * math.log(10000.0) / half_dim)), 2)
    frequency = jnp.tile(frequency, LANES // half_dim)
    second = (jnp.arange(LANES) // half_dim) % 2 == 1
    places = coords.astype(F32) * 0.5
    angles = jnp.where(second, places[1][..., None], places[0][..., None]) * frequency
    return jnp.cos(angles), jnp.sin(angles)


def pad_to(value, axis, size):
    widths = [(0, 0)] * value.ndim
    widths[axis] = (0, size - value.shape[axis])
    return jnp.pad(value, widths)


def ceil_to(value, unit):
    return -(-value // unit) * unit


def on_device(
    n_dp,
    n_tp,
    tokens,
    cotangent,
    w_qkv,
    w_o,
    w_gu,
    w_down,
    norm_params,
    head_params,
    ffn_params,
    token_mask,
    empty_flag,
    coords,
):
    tp_index = lax.axis_index("tensor")
    own_rows, width = tokens.shape[1:]
    local = w_qkv.shape[2]
    units = w_gu.shape[2]
    heads = local // HD
    rows = ceil_to(own_rows, 16)
    seq = rows * n_tp
    lanes = ceil_to(units, LANES)
    step_rows = 2 * rows if n_tp % 2 == 0 else rows
    steps = seq // step_rows
    offsets = ring_offsets(n_tp)
    order = (jnp.array(offsets, jnp.int32) + tp_index) % n_tp

    slots = jnp.concatenate([token_mask, coords[0]], axis=0).reshape(3, n_tp, own_rows)
    slots = pad_to(slots, 2, rows)
    slots = jnp.stack(
        [lax.dynamic_index_in_dim(slots, order[at], 1, keepdims=False) for at in range(n_tp)], 1
    )
    mask = slots[0]
    bias = jnp.where(mask > 0, 0.0, -1e30).astype(F32)
    bias_row, bias_col = bias.reshape(1, seq), bias.reshape(seq, 1)
    keep = (mask[0].astype(F32) * (1.0 - empty_flag[0].astype(F32)))[:, None]
    cosine, sine = rope_tables(slots[1:])
    cos_all, sin_all = cosine.reshape(seq, LANES), sine.reshape(seq, LANES)

    head_local = lax.dynamic_slice_in_dim(head_params, tp_index * local, local, 1)
    ffn_local = pad_to(
        lax.dynamic_slice_in_dim(ffn_params, tp_index * units, units, 1), 1, lanes
    )
    lane_at = jnp.arange(lanes)
    unit_row = ((lane_at < units) & (tp_index * units + lane_at < FF)).astype(F32)[None]

    tokens_own = pad_to(tokens[0], 0, rows)
    dy_own = pad_to(cotangent[0], 0, rows)

    normed, d_low = call(
        first_norm_body,
        (tokens_own, dy_own, keep, norm_params),
        [whole((rows, width))] * 2 + [whole((rows, 1)), whole(norm_params.shape)],
        [sds((rows, width), BF)] * 2,
        [whole((rows, width))] * 2,
        (1,),
    )
    normed_parts = ring_gather(normed, n_tp)

    w_order = dp_order(n_dp)
    full_qkv = put_back(w_order, dp_gather(w_qkv, n_dp), 1)
    o_parts = lax.all_gather(w_o, "tensor", axis=0, tiled=True)
    full_o = put_back(w_order, dp_gather(o_parts, n_dp), 1)
    full_gu = put_back(w_order, dp_gather(pad_to(w_gu, 2, lanes), n_dp), 1)
    full_down = put_back(w_order, dp_gather(pad_to(w_down, 0, lanes), n_dp), 1)

    query, key, value = call(
        functools.partial(project_body, n_tp),
        (*normed_parts, full_qkv, head_local, cosine, sine),
        [whole((rows, width))] * n_tp
        + [whole(full_qkv.shape), whole(head_local.shape)]
        + [lead((rows, LANES))] * 2,
        [sds((n_tp, rows, local), BF)] * 3,
        [lead((rows, local))] * 3,
        (n_tp,),
        scratch=[pltpu.VMEM((rows, width), BF)],
        flops=2 * seq * width * 3 * local,
    )
    query, key, value = (part.reshape(seq, local) for part in (query, key, value))
    strip = pl.BlockSpec((step_rows, local), lambda s, *_: (s, 0))
    mixed_heads, lse = call(
        attend_body,
        (order, query, key, value, bias_row),
        [strip, whole((seq, local)), whole((seq, local)), whole((1, seq))],
        [sds((n_tp, rows, local), BF), sds((steps, heads, step_rows), F32)],
        [whole((n_tp, rows, local)), lead((heads, step_rows))],
        (steps,),
        prefetch=1,
        flops=4 * seq * seq * local * 4,
    )
    mixed = lax.all_to_all(mixed_heads, "tensor", split_axis=0, concat_axis=0, tiled=True)
    d_low_parts = ring_gather(d_low, n_tp)

    own = whole((rows, width))
    inner_low, middle, normed_two = call(
        middle_body,
        (mixed, tokens_own, keep, full_o, norm_params, head_params),
        [
            whole(mixed.shape),
            own,
            whole((rows, 1)),
            whole(full_o.shape),
            whole(norm_params.shape),
            whole(head_params.shape),
        ],
        [sds((rows, width), BF), sds((rows, width), F32), sds((rows, width), BF)],
        [own] * 3,
        (1,),
        flops=2 * rows * width * width,
    )
    two_parts = ring_gather(normed_two, n_tp)

    hidden_block = lead((rows, lanes))
    gate, up, d_ffn, stats = call(
        functools.partial(ffn_body, n_tp),
        (order, *two_parts, *d_low_parts, full_gu, full_down, ffn_local, unit_row),
        [own] * (2 * n_tp)
        + [
            whole(full_gu.shape),
            whole(full_down.shape),
            whole(ffn_local.shape),
            whole(unit_row.shape),
        ],
        [sds((n_tp, rows, lanes), F32)] * 3 + [sds((n_tp, 4, rows), F32)],
        [hidden_block] * 3 + [ordered((4, rows))],
        (n_tp,),
        scratch=[pltpu.VMEM((rows, width), BF)] * 2,
        prefetch=1,
        flops=6 * seq * width * lanes,
    )
    stats = jnp.swapaxes(lax.psum(stats, "tensor"), 1, 2)
    outs = call(
        functools.partial(ffn_back_body, n_tp),
        (order, gate, up, d_ffn, stats, full_gu, ffn_local, unit_row),
        [hidden_block] * 3
        + [
            ordered((rows, 4)),
            whole(full_gu.shape),
            whole(ffn_local.shape),
            whole(unit_row.shape),
        ],
        [sds((n_tp, rows, lanes), BF)] * 3
        + [sds((4, lanes), F32)]
        + [sds((rows, width), BF)] * n_tp,
        [hidden_block] * 3 + [whole((4, lanes))] + [own] * n_tp,
        (n_tp,),
        prefetch=1,
        flops=4 * seq * width * lanes,
    )
    ffn_low, d_gate, d_up, ffn_sums = outs[:4]
    d_two_terms = ring_scatter(outs[4:], n_tp)
    branch_parts = call(
        functools.partial(down_body, n_tp),
        (ffn_low, full_down),
        [hidden_block, whole(full_down.shape)],
        [sds((rows, width), BF)] * n_tp,
        [own] * n_tp,
        (n_tp,),
        flops=2 * seq * width * lanes,
    )

    n_terms = len(d_two_terms)
    d_middle, d_branch, d_mixed_rows, mid_sums = call(
        functools.partial(middle_back_body, n_terms),
        (*d_two_terms, middle, dy_own, d_low, keep, mixed, full_o, norm_params, head_params),
        [own] * n_terms
        + [own] * 3
        + [
            whole((rows, 1)),
            whole(mixed.shape),
            whole(full_o.shape),
            whole(norm_params.shape),
            whole(head_params.shape),
        ],
        [
            sds((rows, width), F32),
            sds((rows, width), BF),
            sds((n_tp, rows, local), BF),
            sds((8, width), F32),
        ],
        [own, own, whole((n_tp, rows, local)), whole((8, width))],
        (1,),
        flops=2 * rows * width * width,
    )
    d_mixed = lax.all_to_all(d_mixed_rows, "tensor", split_axis=0, concat_axis=0, tiled=True)
    branch_terms = ring_scatter(branch_parts, n_tp)
    layer_out = call(
        functools.partial(layer_out_body, n_terms),
        (*branch_terms, middle, keep, norm_params),
        [own] * n_terms + [own, whole((rows, 1)), whole(norm_params.shape)],
        [sds((own_rows, width), BF)],
        [whole((own_rows, width))],
        (1,),
    )[0]

    table = pl.BlockSpec((step_rows, LANES), lambda s, *_: (s, 0))
    all_rows = whole((seq, local))
    d_query, d_key, d_value, head_sums = call(
        attend_back_body,
        (
            order,
            query,
            d_mixed,
            lse,
            key,
            value,
            bias_col,
            cos_all,
            sin_all,
            cos_all,
            sin_all,
        ),
        [
            strip,
            whole(d_mixed.shape),
            lead((heads, step_rows)),
            all_rows,
            all_rows,
            whole((seq, 1)),
            table,
            table,
            whole((seq, LANES)),
            whole((seq, LANES)),
        ],
        [sds((seq, local), BF)] * 3 + [sds((8, local), F32)],
        [strip, all_rows, all_rows, whole((8, local))],
        (steps,),
        scratch=[pltpu.VMEM((seq, local), F32)] * 2,
        prefetch=1,
        flops=10 * seq * seq * local * 4,
    )
    chunk = pl.BlockSpec((rows, local), lambda s, *_: (s, 0))
    d_one_parts = call(
        functools.partial(spread_back_body, n_tp),
        (d_query, d_key, d_value, full_qkv),
        [chunk] * 3 + [whole(full_qkv.shape)],
        [sds((rows, width), BF)] * n_tp,
        [own] * n_tp,
        (n_tp,),
        flops=2 * seq * width * 3 * local,
    )
    d_one_terms = ring_scatter(d_one_parts, n_tp)
    d_tokens, one_sums = call(
        functools.partial(first_back_body, n_terms),
        (*d_one_terms, tokens_own, d_middle, norm_params),
        [own] * n_terms + [own, own, whole(norm_params.shape)],
        [sds((own_rows, width), F32), sds((2, width), F32)],
        [whole((own_rows, width)), whole((2, width))],
        (1,),
    )

    def product(left, right):
        out = lax.dot_general(left, right, TN, preferred_element_type=F32).astype(BF)
        return out.reshape(n_dp, width // n_dp, out.shape[1])

    two_all = jnp.concatenate(two_parts, axis=0)
    low_all = jnp.concatenate(d_low_parts, axis=0)
    hidden_rows = [part.reshape(seq, lanes) for part in (d_gate, d_up, ffn_low)]
    grad_ffn = jnp.concatenate(
        [
            product(two_all, hidden_rows[0]),
            product(two_all, hidden_rows[1]),
            product(low_all, hidden_rows[2]),
        ],
        axis=2,
    )
    grad_ffn = dp_scatter(grad_ffn, n_dp)
    grad_gu = jnp.stack([grad_ffn[:, :units], grad_ffn[:, lanes : lanes + units]])
    grad_down = grad_ffn[:, 2 * lanes : 2 * lanes + units].T
    grad_o = dp_scatter(product(d_branch, inner_low), n_dp).astype(BF)
    grad_o = lax.all_to_all(
        grad_o.reshape(grad_o.shape[0], n_tp, local).swapaxes(0, 1),
        "tensor",
        split_axis=0,
        concat_axis=0,
        tiled=True,
    )
    grad_o = jnp.sum(grad_o.astype(F32), axis=0).T
    normed_all = jnp.concatenate(normed_parts, axis=0)
    d_proj = jnp.concatenate([d_query, d_key, d_value], axis=1)
    grad_qkv = dp_scatter(product(normed_all, d_proj), n_dp)
    grad_qkv = grad_qkv.reshape(-1, 3, local).swapaxes(0, 1)

    ffn_canvas = lax.dynamic_update_slice(
        jnp.zeros((4, FF_PAD), F32), ffn_sums[:, :units], (0, tp_index * units)
    )
    early = jnp.concatenate([mid_sums[:6].reshape(-1), ffn_canvas.reshape(-1)])
    early_len = early.shape[0]
    early = pad_to(early, 0, ceil_to(early_len, 8 * LANES)).reshape(-1, LANES)
    early = sum_everywhere(early, n_dp, n_tp).reshape(-1)
    mid_total = early[: 6 * width].reshape(6, width)
    ffn_total = early[6 * width : early_len].reshape(4, FF_PAD)
    head_canvas = lax.dynamic_update_slice(
        jnp.zeros((2, width), F32), head_sums[:2], (0, tp_index * local)
    )
    late = sum_everywhere(jnp.concatenate([one_sums, head_canvas], axis=0), n_dp, n_tp)
    norm_total = jnp.concatenate([late[:2], mid_total[:4]], axis=0)
    head_total = jnp.concatenate([late[2:], mid_total[4:]], axis=0)
    return (
        layer_out[None],
        d_tokens[None],
        grad_qkv,
        grad_o,
        grad_gu,
        grad_down,
        norm_total,
        head_total,
        ffn_total,
    )


def solution(mesh):
    placed = (
        P("dp", "tensor", None),
        P("dp", "tensor", None),
        P(None, "dp", "tensor"),
        P("tensor", "dp"),
        P(None, "dp", "tensor"),
        P("tensor", "dp"),
        P(),
        P(),
        P(),
        P("dp", None),
        P("dp"),
        P("dp", None, None),
    )
    return jax.shard_map(
        functools.partial(on_device, mesh.shape["dp"], mesh.shape["tensor"]),
        mesh=mesh,
        in_specs=placed,
        out_specs=(
            P("dp", "tensor", None),
            P("dp", "tensor", None),
            P(None, "dp", "tensor"),
            P("tensor", "dp"),
            P(None, "dp", "tensor"),
            P("tensor", "dp"),
            P(),
            P(),
            P(),
        ),
        check_vma=False,
    )
```

```python
import functools
import math

import jax
import jax.numpy as jnp
from jax import lax
from jax.experimental import pallas as pl
from jax.experimental.pallas import tpu as pltpu
from jax.sharding import PartitionSpec as P

FF = 2730
HD = 64
FF_PAD = 2736
GRID_SIDE = 32
LANES = 128
EPS = 1e-06
VMEM_LIMIT = 44 * 2**20
COST_SCALE = 4.0
BF = jnp.bfloat16
F32 = jnp.float32
NT = (((1,), (1,)), ((), ()))
TN = (((0,), (0,)), ((), ()))


def ring_up(value, size):
    return lax.ppermute(value, "tensor", [(j, (j + 1) % size) for j in range(size)])


def ring_down(value, size):
    return lax.ppermute(value, "tensor", [(j, (j - 1) % size) for j in range(size)])


def ring_offsets(size):
    ups = size // 2
    return [0] + [-s for s in range(1, ups + 1)] + [s for s in range(1, size - ups)]


def gather_rest(own, first, size, late=None):
    ups = size // 2
    downs = size - 1 - ups
    upper, lower = first[:1], first[1:]
    for s in range(1, ups):
        up_now = upper[-1] if late is None else after(upper[-1], late)
        upper.append(ring_up(up_now, size))
        if s < downs:
            down_now = lower[-1] if late is None else after(lower[-1], late)
            lower.append(ring_down(down_now, size))
    return [own] + upper + lower


def ring_gather(own, size):
    return gather_rest(own, [ring_up(own, size), ring_down(own, size)], size)


def after(value, *others):
    return lax.optimization_barrier((value,) + others)[0]


def sum_shifts(value, size):
    total = value
    for s in range(1, size):
        total = total + lax.ppermute(
            value, "tensor", [(j, (j + s) % size) for j in range(size)]
        )
    return total


def in_device_order(own, arrived, size):
    index = lax.axis_index("tensor")
    stacked = jnp.stack([own] + arrived)
    doubled = jnp.concatenate([stacked, stacked], axis=0)
    turned = lax.dynamic_slice_in_dim(doubled, (index + 1) % size, size, 0)
    return turned[::-1]


def gather_small(value, size):
    arrived = [
        lax.ppermute(value, "tensor", [(j, (j + s) % size) for j in range(size)])
        for s in range(1, size)
    ]
    return in_device_order(value, arrived, size)


def swap_small(blocks, size):
    index = lax.axis_index("tensor")

    def block_for(s):
        return lax.dynamic_index_in_dim(blocks, (index + s) % size, 0, keepdims=False)

    arrived = [
        lax.ppermute(block_for(s), "tensor", [(j, (j + s) % size) for j in range(size)])
        for s in range(1, size)
    ]
    return in_device_order(block_for(0), arrived, size)


def add_low(left, right):
    return (left.astype(F32) + right.astype(F32)).astype(BF)


def scatter_first(pieces, size):
    place = {offset % size: at for at, offset in enumerate(ring_offsets(size))}
    ups = size // 2
    arrived = []
    if size > 1:
        arrived.append(ring_up(pieces[place[ups % size]], size))
    if ups == size - 1 - ups:
        arrived.append(ring_down(pieces[place[-ups % size]], size))
    elif size > 2:
        arrived.append(ring_down(pieces[place[(1 - ups) % size]], size))
    return arrived


def scatter_rest(pieces, arrived, size):
    place = {offset % size: at for at, offset in enumerate(ring_offsets(size))}
    ups = size // 2
    downs = size - 1 - ups
    up_now = arrived[0]
    for s in range(ups - 1, 0, -1):
        up_now = ring_up(add_low(up_now, pieces[place[s]]), size)
    terms = [pieces[0], up_now]
    if downs:
        down_now = arrived[1]
        for s in range(downs - 1, 0, -1):
            down_now = ring_down(add_low(down_now, pieces[place[-s % size]]), size)
        terms.append(down_now)
    return terms


def dp_bits(size):
    bits = []
    step = 2
    while step < size:
        bits.append(step)
        step *= 2
    return bits + ([1] if size > 1 else [])


def flip(value, bit, size):
    return lax.ppermute(value, "dp", [(j, j ^ bit) for j in range(size)])


def dp_gather(block, size, late=None):
    stacked = block[None]
    bits = dp_bits(size)
    for bit in bits[:-1]:
        other = flip(stacked, bit, size)
        if late is not None and bit == bits[-2]:
            other = after(other, late)
        stacked = jnp.concatenate([stacked, other], axis=0)
    return [stacked] + [flip(stacked, bit, size) for bit in bits[-1:]]


def dp_order(size):
    order = [0]
    for bit in dp_bits(size):
        order = order + [at ^ bit for at in order]
    return jnp.array(order, jnp.int32) ^ lax.axis_index("dp")


def pair_sum(halves, size):
    kept, away = halves
    return add_low(kept, flip(away, 1, size))


def dp_scatter(merged, size):
    groups = [[j for j in range(size) if j % 2 == c] for c in range(2)]
    return lax.all_to_all(
        merged, "dp", split_axis=0, concat_axis=0, tiled=True, axis_index_groups=groups
    )


def sum_parts(parts):
    return jnp.sum(parts.astype(F32), axis=0)


def sum_over(value, axis, size):
    copies = jnp.broadcast_to(value[None], (size,) + value.shape)
    return jnp.sum(lax.all_to_all(copies, axis, split_axis=0, concat_axis=0, tiled=True), axis=0)


def whole(shape):
    return pl.BlockSpec(shape, lambda *_: (0,) * len(shape))


def lead(shape):
    return pl.BlockSpec((1,) + shape, lambda s, *_: (s,) + (0,) * len(shape))


def placed(shape):
    return pl.BlockSpec((1,) + shape, lambda s, place, *_: (place[s],) + (0,) * len(shape))


def ordered(shape):
    return pl.BlockSpec(
        (1,) + shape, lambda s, place, order: (order[place[s]],) + (0,) * len(shape)
    )


def call(
    body, args, specs, outs, out_specs, grid, scratch=(), prefetch=0, held=(), us=1.0
):
    first_held = len(args)
    args = tuple(args) + tuple(held)
    specs = list(specs) + [pl.BlockSpec(memory_space=pl.ANY)] * len(held)
    return pl.pallas_call(
        body,
        out_shape=outs,
        grid_spec=pltpu.PrefetchScalarGridSpec(
            num_scalar_prefetch=prefetch,
            grid=grid,
            in_specs=specs,
            out_specs=out_specs,
            scratch_shapes=list(scratch),
        ),
        input_output_aliases={first_held + at: at for at in range(len(held))},
        compiler_params=pltpu.CompilerParams(vmem_limit_bytes=VMEM_LIMIT),
        cost_estimate=pl.CostEstimate(
            flops=int(us * COST_SCALE * 1e9), bytes_accessed=1, transcendentals=0
        ),
    )(*args)


def sds(shape, dtype):
    return jax.ShapeDtypeStruct(shape, dtype)


def row_stats(rows, count):
    mean = jnp.sum(rows, axis=1, keepdims=True) / count
    power = jnp.sum(rows * rows, axis=1, keepdims=True) / count
    return mean, lax.rsqrt(power - mean * mean + EPS)


def rows_back(upstream, gain, unit, inv, count):
    scaled = upstream * gain
    first = jnp.sum(scaled, axis=1, keepdims=True) / count
    second = jnp.sum(scaled * unit, axis=1, keepdims=True) / count
    return inv * (scaled - first - unit * second)


def down_sum(rows):
    return jnp.sum(rows, axis=0, keepdims=True)


def put_back_body(count, near, *refs):
    in_refs, out_ref = refs[1:-1], refs[-1]
    for at in range(count):

        @pl.when(pl.program_id(0) // near == at)
        def _():
            out_ref[...] = in_refs[at][(0,) * (len(in_refs[at].shape) - len(out_ref.shape))]


def put_back(order, stacks, axis):
    count, near, block = len(stacks), stacks[0].shape[0], stacks[0].shape[1:]
    size = count * near
    shape = tuple(n * size if at == axis else n for at, n in enumerate(block))
    if block[axis] % (LANES if axis == len(block) - 1 else 16):
        stacked = jnp.concatenate(stacks, axis=0)
        placed = jnp.zeros_like(stacked).at[order].set(stacked)
        return jnp.moveaxis(placed, 0, axis).reshape(shape)

    def taken(at):
        return pl.BlockSpec(
            (1,) + block,
            lambda r, order: (jnp.clip(r - at * near, 0, near - 1),) + (0,) * len(block),
        )

    return call(
        functools.partial(put_back_body, count, near),
        (order, *stacks),
        [taken(at) for at in range(count)],
        [sds(shape, stacks[0].dtype)],
        [
            pl.BlockSpec(
                block,
                lambda r, order: tuple(order[r] if at == axis else 0 for at in range(len(block))),
            )
        ],
        (size,),
        prefetch=1,
        us=size * math.prod(block) / 2**19,
    )[0]


def first_norm_body(tokens_ref, norm_ref, normed_ref):
    rows = tokens_ref[...].astype(F32)
    length, width = rows.shape
    mean, inv = row_stats(rows, width)
    normed_ref[:length] = ((rows - mean) * inv * norm_ref[0:1, :] + norm_ref[1:2, :]).astype(BF)
    normed_ref[length:] = jnp.zeros((normed_ref.shape[0] - length, width), BF)


def lay_body(order_ref, *refs):
    out_ref = refs[-1]
    for at, ref in enumerate(refs[:-1]):
        piece = ref[...].astype(F32).T.astype(BF)
        out_ref[order_ref[at]] = piece


def spread(table, width):
    return table if width == LANES else jnp.concatenate([table] * (width // LANES), axis=1)


def turn_pairs(rows):
    width = rows.shape[1]
    even = lax.broadcasted_iota(jnp.int32, (1, width), 1) % 2 == 0
    return jnp.where(even, -pltpu.roll(rows, width - 1, 1), pltpu.roll(rows, 1, 1))


def pick(held, chunk_refs):
    for at, ref in enumerate(chunk_refs):

        @pl.when(pl.program_id(0) == at)
        def _():
            held[...] = ref[...]

    return held[...]


def project_body(count, place_ref, *refs):
    chunk_refs = refs[:count]
    w_ref, head_ref, cos_ref, sin_ref = refs[count : count + 4]
    q_ref, k_ref, v_ref, held = refs[-4:]
    rows = pick(held, chunk_refs)
    width = w_ref.shape[2]
    cosine, sine = spread(cos_ref[...], width), spread(sin_ref[...], width)
    query = jnp.dot(rows, w_ref[0], preferred_element_type=F32) + head_ref[0:1, :]
    key = jnp.dot(rows, w_ref[1], preferred_element_type=F32)
    value = jnp.dot(rows, w_ref[2], preferred_element_type=F32) + head_ref[1:2, :]
    query_low = (query * cosine + turn_pairs(query) * sine).astype(BF)
    q_ref[0] = (query_low.astype(F32) * HD ** (-0.5)).astype(BF)
    k_ref[0] = (key * cosine + turn_pairs(key) * sine).astype(BF)
    v_ref[0] = value.astype(BF)


def head_lanes(width, head):
    lane = lax.broadcasted_iota(jnp.int32, (1, width), 1)
    return (lane >= head * HD) & (lane < (head + 1) * HD)


def attend_body(order_ref, q_ref, k_ref, v_ref, bias_ref, mixed_ref, lse_ref):
    query, keys, values, bias = q_ref[...], k_ref[...], v_ref[...], bias_ref[...]
    length, width = query.shape
    total = jnp.zeros((length, width), F32)
    for head in range(width // HD):
        mine = head_lanes(width, head)
        query_h = jnp.where(mine, query, jnp.zeros_like(query))
        scores = lax.dot_general(query_h, keys, NT, preferred_element_type=F32) + bias
        row_max = jnp.max(scores, axis=1, keepdims=True)
        exp_score = jnp.exp(scores - row_max)
        row_total = jnp.sum(exp_score, axis=1, keepdims=True)
        out = jnp.dot(exp_score.astype(BF), values, preferred_element_type=F32)
        total = jnp.where(mine, out * (1.0 / row_total), total)
        lse_ref[0, head : head + 1, :] = (row_max + jnp.log(row_total)).reshape(1, length)
    rows = mixed_ref.shape[1]
    for part in range(length // rows):
        at = order_ref[pl.program_id(0) * (length // rows) + part]
        mixed_ref[at] = total[part * rows : (part + 1) * rows].astype(BF)


def attend_back_body(
    order_ref,
    q_ref,
    dmix_ref,
    lse_ref,
    k_ref,
    v_ref,
    bias_ref,
    cos_ref,
    sin_ref,
    coss_ref,
    sins_ref,
    dq_ref,
    dk_ref,
    dv_ref,
    sums_ref,
    dk_sum,
    dv_sum,
):
    step = pl.program_id(0)

    @pl.when(step == 0)
    def _():
        dk_sum[...] = jnp.zeros_like(dk_sum)
        dv_sum[...] = jnp.zeros_like(dv_sum)
        sums_ref[...] = jnp.zeros_like(sums_ref)

    query, keys, values, bias = q_ref[...], k_ref[...], v_ref[...], bias_ref[...]
    length, width = query.shape
    rows = dmix_ref.shape[1]
    parts = length // rows
    d_mixed = jnp.concatenate([dmix_ref[order_ref[step * parts + p]] for p in range(parts)], axis=0)
    total = jnp.zeros((length, width), F32)
    for head in range(width // HD):
        mine = head_lanes(width, head)
        zero = jnp.zeros_like(query)
        query_h, d_mixed_h = jnp.where(mine, query, zero), jnp.where(mine, d_mixed, zero)
        scores = lax.dot_general(keys, query_h, NT, preferred_element_type=F32) + bias
        probs = jnp.exp(scores - lse_ref[0, head : head + 1, :])
        d_probs = lax.dot_general(values, d_mixed_h, NT, preferred_element_type=F32)
        d_scores = (probs * (d_probs - down_sum(probs * d_probs))).astype(BF)
        dv_sum[...] += jnp.dot(probs.astype(BF), d_mixed_h, preferred_element_type=F32)
        dk_sum[...] += jnp.dot(d_scores, query_h, preferred_element_type=F32)
        d_query = lax.dot_general(d_scores, keys, TN, preferred_element_type=F32)
        total = jnp.where(mine, d_query, total)
    total = total * HD ** (-0.5)
    cosine, sine = spread(cos_ref[...], width), spread(sin_ref[...], width)
    d_query_pre = (total * cosine - turn_pairs(total) * sine).astype(BF)
    dq_ref[...] = d_query_pre
    sums_ref[0:1, :] += down_sum(d_query_pre.astype(F32))

    @pl.when(step == pl.num_programs(0) - 1)
    def _():
        d_key = dk_sum[...]
        all_cos, all_sin = spread(coss_ref[...], width), spread(sins_ref[...], width)
        d_key_pre = (d_key * all_cos - turn_pairs(d_key) * all_sin).astype(BF)
        dk_ref[...] = d_key_pre
        sums_ref[1:2, :] = down_sum(d_key_pre.astype(F32))
        d_value_pre = dv_sum[...].astype(BF)
        dv_ref[...] = d_value_pre
        sums_ref[2:3, :] = down_sum(d_value_pre.astype(F32))


def mixed_rows(mixed_ref):
    parts = mixed_ref.shape[0]
    return jnp.concatenate([mixed_ref[p] for p in range(parts)], axis=1).astype(F32)


def middle_body(
    mixed_ref, tokens_ref, keep_ref, w_ref, norm_ref, head_ref, inner_ref, middle_ref, normed_ref
):
    mixed = mixed_rows(mixed_ref)
    mean, inv = row_stats(mixed, mixed.shape[1])
    inner = ((mixed - mean) * inv * head_ref[2:3, :] + head_ref[3:4, :]).astype(BF)
    inner_ref[...] = inner
    branch = lax.dot_general(inner, w_ref[...], NT, preferred_element_type=F32)
    branch += norm_ref[4:5, :]
    middle = tokens_ref[...].astype(F32) + keep_ref[...] * branch
    middle_ref[...] = middle
    mean, inv = row_stats(middle, middle.shape[1])
    normed_ref[...] = ((middle - mean) * inv * norm_ref[2:3, :] + norm_ref[3:4, :]).astype(BF)


def sigmoid(gate):
    return 1.0 / (1.0 + jnp.exp(-gate))


def d_ffn_body(count, *refs):
    w_ref, out_ref, held = refs[count:]
    out_ref[0] = jnp.dot(pick(held, refs[:count]), w_ref[0], preferred_element_type=F32)


def ffn_body(count, place_ref, order_ref, *refs):
    d_ref, w_gu_ref, ffn_ref, unit_ref = refs[count : count + 4]
    gate_ref, up_ref, stats_ref, held = refs[-4:]
    rows = pick(held, refs[:count])
    gate = jnp.dot(rows, w_gu_ref[0], preferred_element_type=F32) + ffn_ref[0:1, :]
    up = jnp.dot(rows, w_gu_ref[1], preferred_element_type=F32) + ffn_ref[1:2, :]
    gate_ref[0], up_ref[0] = gate, up
    unit = unit_ref[...]
    hidden = gate * sigmoid(gate) * up
    masked = hidden * unit
    scaled = d_ref[0] * ffn_ref[2:3, :] * unit
    length = rows.shape[0]
    for at, term in enumerate((masked, masked * hidden, scaled, scaled * hidden)):
        stats_ref[0, at : at + 1, :] = jnp.sum(term, axis=1, keepdims=True).reshape(1, length)


def ffn_back_body(count, place_ref, order_ref, *refs):
    gate_ref, up_ref, d_ref, stats_ref, w_gu_ref, ffn_ref, unit_ref = refs[:7]
    low_ref, dgate_ref, dup_ref, sums_ref = refs[-4 - count : -count]
    out_refs = refs[-count:]
    step = pl.program_id(0)

    @pl.when(step == 0)
    def _():
        sums_ref[...] = jnp.zeros_like(sums_ref)

    gate, up, d_ffn, unit = gate_ref[0], up_ref[0], d_ref[0], unit_ref[...]
    gain = ffn_ref[2:3, :]
    stats = stats_ref[0]
    mean = stats[:, 0:1] / FF
    inv = lax.rsqrt(stats[:, 1:2] / FF - mean * mean + EPS)
    first = stats[:, 2:3]
    second = inv * (stats[:, 3:4] - mean * first)
    sig = sigmoid(gate)
    silu = gate * sig
    unit_value = (silu * up - mean) * inv
    low_ref[0] = (unit * (unit_value * gain + ffn_ref[3:4, :])).astype(BF)
    d_hidden = unit * inv * (d_ffn * gain * unit - first / FF - unit_value * (second / FF))
    d_gate = (d_hidden * up * sig * (1.0 + gate * (1.0 - sig))).astype(BF)
    d_up = (d_hidden * silu).astype(BF)
    dgate_ref[0], dup_ref[0] = d_gate, d_up
    d_masked = d_ffn * unit
    sums_ref[0:1, :] += down_sum(d_gate.astype(F32))
    sums_ref[1:2, :] += down_sum(d_up.astype(F32))
    sums_ref[2:3, :] += down_sum(d_masked * unit_value)
    sums_ref[3:4, :] += down_sum(d_masked)
    out = lax.dot_general(d_gate, w_gu_ref[0], NT, preferred_element_type=F32)
    out += lax.dot_general(d_up, w_gu_ref[1], NT, preferred_element_type=F32)
    for at in range(count):

        @pl.when(step == at)
        def _():
            out_refs[at][...] = out.astype(BF)


def down_body(count, low_ref, w_ref, *out_refs):
    out = lax.dot_general(low_ref[0], w_ref[0], NT, preferred_element_type=F32)
    for at in range(count):

        @pl.when(pl.program_id(0) == at)
        def _():
            out_refs[at][...] = out.astype(BF)


def spread_back_body(count, place_ref, dq_ref, dk_ref, dv_ref, w_ref, *out_refs):
    out = lax.dot_general(dq_ref[...], w_ref[0], NT, preferred_element_type=F32)
    out += lax.dot_general(dk_ref[...], w_ref[1], NT, preferred_element_type=F32)
    out += lax.dot_general(dv_ref[...], w_ref[2], NT, preferred_element_type=F32)
    for at in range(count):

        @pl.when(pl.program_id(0) == at)
        def _():
            out_refs[at][...] = out.astype(BF)


def product_body(n_left, sizes, block, parity_ref, *refs):
    lefts, at = [], 0
    for count in n_left:
        lefts.append(jnp.concatenate([ref[...] for ref in refs[at : at + count]], axis=0))
        at += count
    rights = []
    for size in sizes:
        rights.append([ref[...] for ref in refs[at : at + size]])
        at += size
    w_refs = refs[at:-3] if len(refs) - at > 2 else []
    kept_ref, away_ref = refs[at + len(w_refs) : at + len(w_refs) + 2]
    parity = parity_ref[0]
    column, along = 0, 0.0
    for left, group in zip(lefts, rights):
        for right in group:
            out = lax.dot_general(left, right, TN, preferred_element_type=F32)
            width = right.shape[1]
            if w_refs:
                part = w_refs[0][column // width].astype(F32)
                along = along + jnp.sum(out * part, axis=1, keepdims=True)
            low = out.astype(BF)
            for pair in range(out.shape[0] // (2 * block)):
                first = low[2 * pair * block : (2 * pair + 1) * block]
                second = low[(2 * pair + 1) * block : (2 * pair + 2) * block]
                mine = jnp.where(parity == 0, first, second)
                other = jnp.where(parity == 0, second, first)
                kept_ref[pair, :, column : column + width] = mine
                away_ref[pair, :, column : column + width] = other
            column += width
    if w_refs:
        refs[-1][0] = along.reshape(1, along.shape[0])


def product(lefts, rights, parity, block, weights=None):
    width = lefts[0][0].shape[1]
    step = max(256, 2 * block)
    pairs = step // (2 * block)
    columns = sum(right.shape[1] for group in rights for right in group)
    args = [left for group in lefts for left in group]
    specs = [
        pl.BlockSpec((left.shape[0], step), lambda m, *_: (0, m)) for group in lefts for left in group
    ]
    for group in rights:
        args += group
        specs += [whole(right.shape) for right in group]
    outs = [sds((width // (2 * block), block, columns), BF)] * 2
    out_specs = [pl.BlockSpec((pairs, block, columns), lambda m, *_: (m, 0, 0))] * 2
    if weights is not None:
        args.append(weights)
        specs.append(
            pl.BlockSpec((weights.shape[0], step, weights.shape[2]), lambda m, *_: (0, m, 0))
        )
        outs.append(sds((width // step, 1, step), F32))
        out_specs.append(lead((1, step)))
    return call(
        functools.partial(
            product_body, [len(g) for g in lefts], [len(g) for g in rights], block
        ),
        (parity, *args),
        specs,
        outs,
        out_specs,
        (width // step,),
        prefetch=1,
        us=columns / 250,
    )


def add_terms(term_refs):
    total = term_refs[0][...].astype(F32)
    for ref in term_refs[1:]:
        total += ref[...].astype(F32)
    return total


def middle_back_body(count, *refs):
    upstream = add_terms(refs[:count])
    middle_ref, dy_ref, low_ref, keep_ref, mixed_ref, w_ref, norm_ref, head_ref = refs[
        count : count + 8
    ]
    dmid_ref, dbranch_ref, dmix_ref, sums_ref = refs[count + 8 :]
    middle = middle_ref[...]
    width = middle.shape[1]
    mean, inv = row_stats(middle, width)
    unit = (middle - mean) * inv
    d_middle = dy_ref[...].astype(F32) + rows_back(upstream, norm_ref[2:3, :], unit, inv, width)
    dmid_ref[...] = d_middle
    sums_ref[0:1, :] = down_sum(upstream * unit)
    sums_ref[1:2, :] = down_sum(upstream)
    d_branch = (keep_ref[...] * d_middle).astype(BF)
    dbranch_ref[...] = d_branch
    sums_ref[2:3, :] = down_sum(d_branch.astype(F32))
    sums_ref[3:4, :] = down_sum(low_ref[...].astype(F32))
    d_inner = jnp.dot(d_branch, w_ref[...], preferred_element_type=F32)
    mixed = mixed_rows(mixed_ref)
    mean, inv = row_stats(mixed, width)
    unit = (mixed - mean) * inv
    d_mixed = rows_back(d_inner, head_ref[2:3, :], unit, inv, width).astype(BF)
    part = mixed_ref.shape[2]
    for at in range(mixed_ref.shape[0]):
        dmix_ref[at] = d_mixed[:, at * part : (at + 1) * part]
    sums_ref[4:5, :] = down_sum(d_inner * unit)
    sums_ref[5:6, :] = down_sum(d_inner)
    sums_ref[6:8, :] = jnp.zeros((2, width), F32)


def first_back_body(count, *refs):
    upstream = add_terms(refs[:count])
    tokens_ref, dmid_ref, norm_ref, out_ref = refs[count:]
    rows = tokens_ref[...].astype(F32)
    length, width = rows.shape
    mean, inv = row_stats(rows, width)
    unit = (rows - mean) * inv
    d_in = rows_back(upstream[:length], norm_ref[0:1, :], unit, inv, width)
    out_ref[...] = dmid_ref[:length] + d_in


def layer_out_body(count, *refs):
    branch = add_terms(refs[:count])
    middle_ref, keep_ref, norm_ref, out_ref = refs[count:]
    out = middle_ref[...] + keep_ref[...] * (branch + norm_ref[5:6, :])
    out_ref[...] = out[: out_ref.shape[0]].astype(BF)


def rope_tables(coords):
    half_dim = HD // 2
    index_j = jnp.arange(half_dim // 2).astype(F32)
    frequency = jnp.repeat(jnp.exp(index_j * (-2.0 * math.log(10000.0) / half_dim)), 2)
    spots = jnp.arange(GRID_SIDE)
    angles = (spots.astype(F32) * 0.5)[:, None] * frequency
    lane_half = jnp.arange(LANES) // half_dim % 2
    tables = jnp.stack([jnp.cos(angles), jnp.sin(angles)])
    tables = jnp.tile(tables, (1, 1, LANES // half_dim))
    tables = jnp.concatenate([tables * (lane_half == half) for half in range(2)], axis=1)
    chosen = jnp.concatenate(
        [(coords[half][:, None] == spots).astype(F32) for half in range(2)], axis=1
    )
    both = jnp.dot(
        chosen,
        jnp.concatenate([tables[0], tables[1]], axis=1),
        precision=lax.Precision.HIGHEST,
    )
    return both[:, :LANES], both[:, LANES:]


def pad_to(value, axis, size):
    widths = [(0, 0)] * value.ndim
    widths[axis] = (0, size - value.shape[axis])
    return jnp.pad(value, widths)


def ceil_to(value, unit):
    return -(-value // unit) * unit


def on_device(
    n_dp,
    n_tp,
    tokens,
    cotangent,
    w_qkv,
    w_o,
    w_gu,
    w_down,
    norm_params,
    head_params,
    ffn_params,
    token_mask,
    empty_flag,
    coords,
):
    tp_index = lax.axis_index("tensor")
    own_rows, width = tokens.shape[1:]
    local = w_qkv.shape[2]
    units = w_gu.shape[2]
    heads = local // HD
    rows = ceil_to(own_rows, 16)
    seq = rows * n_tp
    lanes = ceil_to(units, LANES)
    step_rows = 2 * rows if n_tp % 2 == 0 else rows
    steps = seq // step_rows
    offsets = ring_offsets(n_tp)
    order = (jnp.array(offsets, jnp.int32) + tp_index) % n_tp
    place = {offset % n_tp: at for at, offset in enumerate(offsets)}
    own = whole((rows, width))

    normed = call(
        first_norm_body,
        (tokens[0], norm_params),
        [whole((own_rows, width)), whole(norm_params.shape)],
        [sds((rows, width), BF)],
        [own],
        (1,),
        us=1.2,
    )[0]
    normed_parts = ring_gather(normed, n_tp)

    ups = n_tp // 2
    arrivals = [[0]]
    for s in range(1, ups + 1):
        arrivals.append(sorted({place[-s % n_tp], place[s % n_tp]}))
    leaving = sorted({place[ups % n_tp], place[-1 % n_tp]})
    staying = [at for at in range(n_tp) if at not in leaving]
    leavings = [group for group in (leaving, staying) if group]

    slots = jnp.concatenate([token_mask, coords[0]], axis=0).reshape(3, n_tp, own_rows)
    slots = pad_to(slots, 2, rows)
    slots = jnp.stack(
        [lax.dynamic_index_in_dim(slots, order[at], 1, keepdims=False) for at in range(n_tp)], 1
    )
    mask = slots[0]
    bias = jnp.where(mask > 0, 0.0, -1e30).astype(F32)
    bias_row, bias_col = bias.reshape(1, seq), bias.reshape(seq, 1)
    keep = (mask[0].astype(F32) * (1.0 - empty_flag[0].astype(F32)))[:, None]
    cos_all, sin_all = rope_tables(slots[1:].reshape(2, seq))

    head_local = lax.dynamic_slice_in_dim(head_params, tp_index * local, local, 1)
    ffn_local = pad_to(
        lax.dynamic_slice_in_dim(ffn_params, tp_index * units, units, 1), 1, lanes
    )
    lane_at = jnp.arange(lanes)
    unit_row = ((lane_at < units) & (tp_index * units + lane_at < FF)).astype(F32)[None]

    tokens_own = pad_to(tokens[0], 0, rows)
    dy_own = pad_to(cotangent[0], 0, rows)
    d_low = (keep * dy_own.astype(F32)).astype(BF)

    w_order = dp_order(n_dp)
    full_qkv = put_back(w_order, dp_gather(w_qkv, n_dp), 1)
    filled = ()
    for turn, group in enumerate(arrivals):
        if turn > 1:
            normed_parts[group[0]] = after(normed_parts[group[0]], filled[0])
        filled = call(
            functools.partial(project_body, len(group)),
            (
                jnp.array(group, jnp.int32),
                *(normed_parts[at] for at in group),
                full_qkv,
                head_local,
                cos_all,
                sin_all,
            ),
            [own] * len(group)
            + [whole(full_qkv.shape), whole(head_local.shape)]
            + [pl.BlockSpec((rows, LANES), lambda s, place, *_: (place[s], 0))] * 2,
            [sds((n_tp, rows, local), BF)] * 3,
            [placed((rows, local))] * 3,
            (len(group),),
            scratch=[pltpu.VMEM((rows, width), BF)],
            prefetch=1,
            held=filled,
            us=2.0 * len(group),
        )
    query, key, value = (part.reshape(seq, local) for part in filled)
    d_low_late = after(d_low, normed_parts[-1], normed_parts[ups])
    d_low_first = [ring_up(d_low_late, n_tp), ring_down(d_low_late, n_tp)]
    strip = pl.BlockSpec((step_rows, local), lambda s, *_: (s, 0))
    mixed_heads, lse = call(
        attend_body,
        (order, query, key, value, bias_row),
        [strip, whole((seq, local)), whole((seq, local)), whole((1, seq))],
        [sds((n_tp, rows, local), BF), sds((steps, heads, step_rows), F32)],
        [whole((n_tp, rows, local)), lead((heads, step_rows))],
        (steps,),
        prefetch=1,
        us=10,
    )
    mixed_heads = after(mixed_heads, *d_low_first)
    mixed = lax.all_to_all(mixed_heads, "tensor", split_axis=0, concat_axis=0, tiled=True)

    w_o_late = after(w_o, normed_parts[1])
    o_parts = call(
        lay_body,
        (order, *ring_gather(w_o_late, n_tp)),
        [whole(w_o.shape)] * n_tp,
        [sds((n_tp,) + w_o.shape[::-1], BF)],
        [whole((n_tp,) + w_o.shape[::-1])],
        (1,),
        prefetch=1,
        us=0.7,
    )[0]
    o_parts = jnp.concatenate([o_parts[at] for at in range(n_tp)], axis=1)
    full_o = put_back(w_order, dp_gather(o_parts, n_dp), 0)
    w_ffn = pad_to(jnp.concatenate([w_gu, w_down.T[None]], axis=0), 2, lanes)
    w_ffn = after(w_ffn, normed_parts[1])
    full_ffn = put_back(w_order, dp_gather(w_ffn, n_dp, mixed), 1)

    inner_low, middle, normed_two = call(
        middle_body,
        (mixed, tokens_own, keep, full_o, norm_params, head_params),
        [
            whole(mixed.shape),
            own,
            whole((rows, 1)),
            whole(full_o.shape),
            whole(norm_params.shape),
            whole(head_params.shape),
        ],
        [sds((rows, width), BF), sds((rows, width), F32), sds((rows, width), BF)],
        [own] * 3,
        (1,),
        us=3,
    )
    two_parts = ring_gather(normed_two, n_tp)
    d_low_parts = gather_rest(d_low, d_low_first, n_tp, two_parts[1])

    hidden_shape = (n_tp, rows, lanes)
    gu_block = pl.BlockSpec((2, width, lanes), lambda *_: (0, 0, 0))
    down_block = pl.BlockSpec((1, width, lanes), lambda *_: (2, 0, 0))
    d_ffn = call(
        functools.partial(d_ffn_body, n_tp),
        (*d_low_parts, full_ffn),
        [own] * n_tp + [down_block],
        [sds(hidden_shape, F32)],
        [lead((rows, lanes))],
        (n_tp,),
        scratch=[pltpu.VMEM((rows, width), BF)],
        us=5.6,
    )[0]
    hidden_block = placed((rows, lanes))
    filled = ()
    for turn, group in enumerate(arrivals):
        if turn > 1:
            two_parts[group[0]] = after(two_parts[group[0]], filled[0])
        filled = call(
            functools.partial(ffn_body, len(group)),
            (
                jnp.array(group, jnp.int32),
                order,
                *(two_parts[at] for at in group),
                d_ffn,
                full_ffn,
                ffn_local,
                unit_row,
            ),
            [own] * len(group)
            + [hidden_block, gu_block, whole(ffn_local.shape), whole(unit_row.shape)],
            [sds(hidden_shape, F32)] * 2 + [sds((n_tp, 4, rows), F32)],
            [hidden_block] * 2 + [ordered((4, rows))],
            (len(group),),
            scratch=[pltpu.VMEM((rows, width), BF)],
            prefetch=2,
            held=filled,
            us=1.2 + 2.2 * len(group),
        )
    gate, up, stats = filled
    stats = jnp.swapaxes(sum_shifts(stats, n_tp), 1, 2)
    filled, ffn_sums, d_two_parts = (), 0.0, [None] * n_tp
    for group in leavings:
        outs = call(
            functools.partial(ffn_back_body, len(group)),
            (
                jnp.array(group, jnp.int32),
                order,
                gate,
                up,
                d_ffn,
                stats,
                full_ffn,
                ffn_local,
                unit_row,
            ),
            [hidden_block] * 3
            + [
                ordered((rows, 4)),
                gu_block,
                whole(ffn_local.shape),
                whole(unit_row.shape),
            ],
            [sds(hidden_shape, BF)] * 3
            + [sds((4, lanes), F32)]
            + [sds((rows, width), BF)] * len(group),
            [hidden_block] * 3 + [whole((4, lanes))] + [own] * len(group),
            (len(group),),
            prefetch=2,
            held=filled,
            us=3.7 * len(group),
        )
        filled = outs[:3]
        ffn_sums = ffn_sums + outs[3]
        for at, piece in zip(group, outs[4:]):
            d_two_parts[at] = piece
    ffn_low, d_gate, d_up = filled
    d_two_terms = scatter_rest(d_two_parts, scatter_first(d_two_parts, n_tp), n_tp)
    branch_parts = call(
        functools.partial(down_body, n_tp),
        (ffn_low, full_ffn),
        [lead((rows, lanes)), down_block],
        [sds((rows, width), BF)] * n_tp,
        [own] * n_tp,
        (n_tp,),
        us=2.8,
    )

    parity = (lax.axis_index("dp") % 2).astype(jnp.int32)[None]
    block = width // n_dp
    hidden_rows = [part.reshape(seq, lanes) for part in (d_gate, d_up, ffn_low)]
    grad_ffn = product([two_parts, d_low_parts], [hidden_rows[:2], hidden_rows[2:]], parity, block)
    grad_ffn = pair_sum(grad_ffn, n_dp)


    n_terms = len(d_two_terms)
    d_middle, d_branch, d_mixed_rows, mid_sums = call(
        functools.partial(middle_back_body, n_terms),
        (*d_two_terms, middle, dy_own, d_low, keep, mixed, full_o, norm_params, head_params),
        [own] * n_terms
        + [own] * 3
        + [
            whole((rows, 1)),
            whole(mixed.shape),
            whole(full_o.shape),
            whole(norm_params.shape),
            whole(head_params.shape),
        ],
        [
            sds((rows, width), F32),
            sds((rows, width), BF),
            sds((n_tp, rows, local), BF),
            sds((8, width), F32),
        ],
        [own, own, whole((n_tp, rows, local)), whole((8, width))],
        (1,),
        us=3.6,
    )
    d_mixed = lax.all_to_all(d_mixed_rows, "tensor", split_axis=0, concat_axis=0, tiled=True)
    grad_o = pair_sum(product([[d_branch]], [[inner_low]], parity, block), n_dp)
    grad_early = jnp.concatenate([grad_ffn, grad_o], axis=2)
    d_mixed = after(d_mixed, grad_early)
    grad_early = dp_scatter(grad_early, n_dp)
    branch_parts = [after(part, d_mixed) for part in branch_parts]
    branch_first = scatter_first(branch_parts, n_tp)

    table = pl.BlockSpec((step_rows, LANES), lambda s, *_: (s, 0))
    all_rows = whole((seq, local))
    d_query, d_key, d_value, head_sums = call(
        attend_back_body,
        (
            order,
            query,
            d_mixed,
            lse,
            key,
            value,
            bias_col,
            cos_all,
            sin_all,
            cos_all,
            sin_all,
        ),
        [
            strip,
            whole(d_mixed.shape),
            lead((heads, step_rows)),
            all_rows,
            all_rows,
            whole((seq, 1)),
            table,
            table,
            whole((seq, LANES)),
            whole((seq, LANES)),
        ],
        [sds((seq, local), BF)] * 3 + [sds((8, local), F32)],
        [strip, all_rows, all_rows, whole((8, local))],
        (steps,),
        scratch=[pltpu.VMEM((seq, local), F32)] * 2,
        prefetch=1,
        us=24,
    )
    d_query = after(d_query, *branch_first)
    chunk = pl.BlockSpec((rows, local), lambda s, place, *_: (place[s], 0))
    d_one_parts = [None] * n_tp
    for group in leavings:
        outs = call(
            functools.partial(spread_back_body, len(group)),
            (jnp.array(group, jnp.int32), d_query, d_key, d_value, full_qkv),
            [chunk] * 3 + [whole(full_qkv.shape)],
            [sds((rows, width), BF)] * len(group),
            [own] * len(group),
            (len(group),),
            prefetch=1,
            us=1.0 * len(group),
        )
        for at, piece in zip(group, outs):
            d_one_parts[at] = piece
    d_proj = [after(part, *[d_one_parts[at] for at in leaving]) for part in (d_query, d_key, d_value)]
    *grad_qkv, along_normed = product([normed_parts], [d_proj], parity, block, full_qkv)
    along_normed = along_normed.reshape(-1)
    shift_one = sum(
        jnp.sum(full_qkv[at].astype(F32) * head_sums[at : at + 1], axis=1) for at in range(3)
    )
    grad_qkv = pair_sum(grad_qkv, n_dp)

    d_one_first = scatter_first(d_one_parts, n_tp)
    arrived = [after(d_one_first[0], grad_qkv)] + d_one_first[1:]
    d_one_terms = scatter_rest(d_one_parts, arrived, n_tp)

    small = [along_normed, shift_one, mid_sums[:6].reshape(-1)]
    small += [head_sums[0], head_sums[2], ffn_sums[:, :units].reshape(-1)]
    small = jnp.concatenate(small)
    small_len = small.shape[0]
    small = pad_to(small, 0, ceil_to(small_len, 8 * LANES)).reshape(-1, LANES)
    grad_qkv = dp_scatter(after(grad_qkv, grad_early), n_dp)
    small = sum_over(after(small, grad_qkv), "dp", n_dp)
    small = gather_small(small, n_tp).reshape(n_tp, -1)
    head_at = 8 * width
    ffn_at = head_at + 2 * local
    norm_sums = jnp.sum(small[:, :head_at], axis=0).reshape(8, width)
    head_bias = small[:, head_at:ffn_at].reshape(n_tp, 2, local).swapaxes(0, 1)
    ffn_total = small[:, ffn_at:small_len].reshape(n_tp, 4, units).swapaxes(0, 1)
    ffn_total = ffn_total.reshape(4, n_tp * units)
    gain_one = (norm_sums[0:1] - norm_params[1:2] * norm_sums[1:2]) / norm_params[0:1]
    norm_total = jnp.concatenate([gain_one, norm_sums[1:6]], axis=0)
    head_total = jnp.concatenate([head_bias.reshape(2, width), norm_sums[6:8]], axis=0)

    grad_early = sum_parts(grad_early)
    grad_o = grad_early[:, 3 * lanes :].astype(BF).reshape(-1, n_tp, local).swapaxes(0, 1)
    grad_o = jnp.sum(swap_small(grad_o, n_tp).astype(F32), axis=0).T
    grad_gu = jnp.stack([grad_early[:, :units], grad_early[:, lanes : lanes + units]])
    grad_down = grad_early[:, 2 * lanes : 2 * lanes + units].T
    grad_qkv = sum_parts(grad_qkv).reshape(-1, 3, local).swapaxes(0, 1)

    branch_first = [after(branch_first[0], d_one_first[0])] + branch_first[1:]
    branch_terms = scatter_rest(branch_parts, branch_first, n_tp)
    layer_out = call(
        functools.partial(layer_out_body, n_terms),
        (*branch_terms, middle, keep, norm_params),
        [own] * n_terms + [own, whole((rows, 1)), whole(norm_params.shape)],
        [sds((own_rows, width), BF)],
        [whole((own_rows, width))],
        (1,),
        us=2,
    )[0]
    d_one_terms[0] = after(d_one_terms[0], grad_qkv, norm_total, ffn_total)
    d_tokens = call(
        functools.partial(first_back_body, n_terms),
        (*d_one_terms, tokens[0], d_middle, norm_params),
        [own] * n_terms + [whole((own_rows, width)), own, whole(norm_params.shape)],
        [sds((own_rows, width), F32)],
        [whole((own_rows, width))],
        (1,),
        us=1.5,
    )[0]

    return (
        layer_out[None],
        d_tokens[None],
        grad_qkv,
        grad_o,
        grad_gu,
        grad_down,
        norm_total,
        head_total,
        ffn_total,
    )


def solution(mesh):
    placed = (
        P("dp", "tensor", None),
        P("dp", "tensor", None),
        P(None, "dp", "tensor"),
        P("tensor", "dp"),
        P(None, "dp", "tensor"),
        P("tensor", "dp"),
        P(),
        P(),
        P(),
        P("dp", None),
        P("dp"),
        P("dp", None, None),
    )
    return jax.shard_map(
        functools.partial(on_device, mesh.shape["dp"], mesh.shape["tensor"]),
        mesh=mesh,
        in_specs=placed,
        out_specs=(
            P("dp", "tensor", None),
            P("dp", "tensor", None),
            P(None, "dp", "tensor"),
            P("tensor", "dp"),
            P(None, "dp", "tensor"),
            P("tensor", "dp"),
            P(),
            P(),
            P(),
        ),
        check_vma=False,
    )
```

```python
import functools
import math

import jax
import jax.numpy as jnp
from jax import lax
from jax.experimental import pallas as pl
from jax.experimental.pallas import tpu as pltpu
from jax.sharding import PartitionSpec as P

FF = 2730
HD = 64
FF_PAD = 2736
GRID_SIDE = 32
LANES = 128
EPS = 1e-06
VMEM_LIMIT = 44 * 2**20
COST_SCALE = 4.0
BF = jnp.bfloat16
F32 = jnp.float32
NT = (((1,), (1,)), ((), ()))
TN = (((0,), (0,)), ((), ()))


def ring_up(value, size):
    return lax.ppermute(value, "tensor", [(j, (j + 1) % size) for j in range(size)])


def ring_down(value, size):
    return lax.ppermute(value, "tensor", [(j, (j - 1) % size) for j in range(size)])


def ring_offsets(size):
    ups = size // 2
    return [0] + [-s for s in range(1, ups + 1)] + [s for s in range(1, size - ups)]


def gather_rest(own, first, size, late=None):
    ups = size // 2
    downs = size - 1 - ups
    upper, lower = first[:1], first[1:]
    for s in range(1, ups):
        up_now = upper[-1] if late is None else after(upper[-1], late)
        upper.append(ring_up(up_now, size))
        if s < downs:
            down_now = lower[-1] if late is None else after(lower[-1], late)
            lower.append(ring_down(down_now, size))
    return [own] + upper + lower


def ring_gather(own, size):
    return gather_rest(own, [ring_up(own, size), ring_down(own, size)], size)


def after(value, *others):
    return lax.optimization_barrier((value,) + others)[0]


def sum_shifts(value, size):
    total = value
    for s in range(1, size):
        total = total + lax.ppermute(
            value, "tensor", [(j, (j + s) % size) for j in range(size)]
        )
    return total


def gather_small(value, size):
    return [value] + [
        lax.ppermute(value, "tensor", [(j, (j + s) % size) for j in range(size)])
        for s in range(1, size)
    ]


def sum_alike(terms):
    while len(terms) > 1 and len(terms) % 2 == 0:
        half = len(terms) // 2
        terms = [terms[s] + terms[s + half] for s in range(half)]
    return functools.reduce(jnp.add, terms)


def swap_sum(blocks, size):
    index = lax.axis_index("tensor")

    def block_for(s):
        return lax.dynamic_index_in_dim(blocks, (index + s) % size, 0, keepdims=False)

    total = block_for(0).astype(F32)
    for s in range(1, size):
        came = lax.ppermute(block_for(s), "tensor", [(j, (j + s) % size) for j in range(size)])
        total = total + came.astype(F32)
    return total


def add_low(left, right):
    return (left.astype(F32) + right.astype(F32)).astype(BF)


def scatter_first(pieces, size):
    place = {offset % size: at for at, offset in enumerate(ring_offsets(size))}
    ups = size // 2
    arrived = []
    if size > 1:
        arrived.append(ring_up(pieces[place[ups % size]], size))
    if ups == size - 1 - ups:
        arrived.append(ring_down(pieces[place[-ups % size]], size))
    elif size > 2:
        arrived.append(ring_down(pieces[place[(1 - ups) % size]], size))
    return arrived


def scatter_rest(pieces, arrived, size, sent=None):
    place = {offset % size: at for at, offset in enumerate(ring_offsets(size))}
    ups = size // 2
    downs = size - 1 - ups
    up_now = arrived[0]
    for s in range(ups - 1, 0, -1):
        up_now = add_low(up_now, pieces[place[s]])
        if sent is not None:
            sent.append(up_now)
        up_now = ring_up(up_now, size)
    terms = [pieces[0], up_now]
    if downs:
        down_now = arrived[1]
        for s in range(downs - 1, 0, -1):
            down_now = ring_down(add_low(down_now, pieces[place[-s % size]]), size)
        terms.append(down_now)
    return terms


def dp_bits(size):
    bits = []
    step = 2
    while step < size:
        bits.append(step)
        step *= 2
    return bits + ([1] if size > 1 else [])


def flip(value, bit, size):
    return lax.ppermute(value, "dp", [(j, j ^ bit) for j in range(size)])


def dp_gather(block, size, late=None):
    stacked = block[None]
    bits = dp_bits(size)
    for bit in bits[:-1]:
        other = flip(stacked, bit, size)
        if late is not None and bit == bits[-2]:
            other = after(other, late)
        stacked = jnp.concatenate([stacked, other], axis=0)
    return [stacked] + [flip(stacked, bit, size) for bit in bits[-1:]]


def dp_order(size):
    order = [0]
    for bit in dp_bits(size):
        order = order + [at ^ bit for at in order]
    return jnp.array(order, jnp.int32) ^ lax.axis_index("dp")


def pair_sum(halves, size):
    kept, away = halves
    return add_low(kept, flip(away, 1, size))


def dp_scatter(merged, size):
    groups = [[j for j in range(size) if j % 2 == c] for c in range(2)]
    return lax.all_to_all(
        merged, "dp", split_axis=0, concat_axis=0, tiled=True, axis_index_groups=groups
    )


def sum_parts(parts):
    return jnp.sum(parts.astype(F32), axis=0)


def sum_over(value, axis, size):
    copies = jnp.broadcast_to(value[None], (size,) + value.shape)
    return jnp.sum(lax.all_to_all(copies, axis, split_axis=0, concat_axis=0, tiled=True), axis=0)


def whole(shape):
    return pl.BlockSpec(shape, lambda *_: (0,) * len(shape))


def lead(shape):
    return pl.BlockSpec((1,) + shape, lambda s, *_: (s,) + (0,) * len(shape))


def placed(shape):
    return pl.BlockSpec((1,) + shape, lambda s, place, *_: (place[s],) + (0,) * len(shape))


def ordered(shape):
    return pl.BlockSpec(
        (1,) + shape, lambda s, place, order: (order[place[s]],) + (0,) * len(shape)
    )


def call(
    body, args, specs, outs, out_specs, grid, scratch=(), prefetch=0, held=(), us=1.0
):
    first_held = len(args)
    args = tuple(args) + tuple(held)
    specs = list(specs) + [pl.BlockSpec(memory_space=pl.ANY)] * len(held)
    return pl.pallas_call(
        body,
        out_shape=outs,
        grid_spec=pltpu.PrefetchScalarGridSpec(
            num_scalar_prefetch=prefetch,
            grid=grid,
            in_specs=specs,
            out_specs=out_specs,
            scratch_shapes=list(scratch),
        ),
        input_output_aliases={first_held + at: at for at in range(len(held))},
        compiler_params=pltpu.CompilerParams(vmem_limit_bytes=VMEM_LIMIT),
        cost_estimate=pl.CostEstimate(
            flops=int(us * COST_SCALE * 1e9), bytes_accessed=1, transcendentals=0
        ),
    )(*args)


def sds(shape, dtype):
    return jax.ShapeDtypeStruct(shape, dtype)


def row_stats(rows, count):
    mean = jnp.sum(rows, axis=1, keepdims=True) / count
    power = jnp.sum(rows * rows, axis=1, keepdims=True) / count
    return mean, lax.rsqrt(power - mean * mean + EPS)


def rows_back(upstream, gain, unit, inv, count):
    scaled = upstream * gain
    first = jnp.sum(scaled, axis=1, keepdims=True) / count
    second = jnp.sum(scaled * unit, axis=1, keepdims=True) / count
    return inv * (scaled - first - unit * second)


def down_sum(rows):
    return jnp.sum(rows, axis=0, keepdims=True)


def put_back_body(count, near, *refs):
    in_refs, out_ref = refs[1:-1], refs[-1]
    for at in range(count):

        @pl.when(pl.program_id(0) // near == at)
        def _():
            out_ref[...] = in_refs[at][(0,) * (len(in_refs[at].shape) - len(out_ref.shape))]


def put_back(order, stacks, axis):
    count, near, block = len(stacks), stacks[0].shape[0], stacks[0].shape[1:]
    size = count * near
    shape = tuple(n * size if at == axis else n for at, n in enumerate(block))
    if block[axis] % (LANES if axis == len(block) - 1 else 16):
        stacked = jnp.concatenate(stacks, axis=0)
        placed = jnp.zeros_like(stacked).at[order].set(stacked)
        return jnp.moveaxis(placed, 0, axis).reshape(shape)

    def taken(at):
        return pl.BlockSpec(
            (1,) + block,
            lambda r, order: (jnp.clip(r - at * near, 0, near - 1),) + (0,) * len(block),
        )

    return call(
        functools.partial(put_back_body, count, near),
        (order, *stacks),
        [taken(at) for at in range(count)],
        [sds(shape, stacks[0].dtype)],
        [
            pl.BlockSpec(
                block,
                lambda r, order: tuple(order[r] if at == axis else 0 for at in range(len(block))),
            )
        ],
        (size,),
        prefetch=1,
        us=size * math.prod(block) / 2**19,
    )[0]


def first_norm_body(tokens_ref, norm_ref, normed_ref):
    rows = tokens_ref[...].astype(F32)
    length, width = rows.shape
    mean, inv = row_stats(rows, width)
    normed_ref[:length] = ((rows - mean) * inv * norm_ref[0:1, :] + norm_ref[1:2, :]).astype(BF)
    normed_ref[length:] = jnp.zeros((normed_ref.shape[0] - length, width), BF)


def lay_body(order_ref, *refs):
    out_ref = refs[-1]
    for at, ref in enumerate(refs[:-1]):
        piece = ref[...].astype(F32).T.astype(BF)
        out_ref[order_ref[at]] = piece


def spread(table, width):
    return table if width == LANES else jnp.concatenate([table] * (width // LANES), axis=1)


def turn_pairs(rows):
    width = rows.shape[1]
    even = lax.broadcasted_iota(jnp.int32, (1, width), 1) % 2 == 0
    return jnp.where(even, -pltpu.roll(rows, width - 1, 1), pltpu.roll(rows, 1, 1))


def pick(held, chunk_refs):
    for at, ref in enumerate(chunk_refs):

        @pl.when(pl.program_id(0) == at)
        def _():
            held[...] = ref[...]

    return held[...]


def project_body(count, place_ref, *refs):
    chunk_refs = refs[:count]
    w_ref, head_ref, cos_ref, sin_ref = refs[count : count + 4]
    q_ref, k_ref, v_ref, held = refs[-4:]
    rows = pick(held, chunk_refs)
    width = w_ref.shape[2]
    cosine, sine = spread(cos_ref[...], width), spread(sin_ref[...], width)
    query = jnp.dot(rows, w_ref[0], preferred_element_type=F32) + head_ref[0:1, :]
    key = jnp.dot(rows, w_ref[1], preferred_element_type=F32)
    value = jnp.dot(rows, w_ref[2], preferred_element_type=F32) + head_ref[1:2, :]
    query_low = (query * cosine + turn_pairs(query) * sine).astype(BF)
    q_ref[0] = (query_low.astype(F32) * HD ** (-0.5)).astype(BF)
    k_ref[0] = (key * cosine + turn_pairs(key) * sine).astype(BF)
    v_ref[0] = value.astype(BF)


def head_lanes(width, head):
    lane = lax.broadcasted_iota(jnp.int32, (1, width), 1)
    return (lane >= head * HD) & (lane < (head + 1) * HD)


def attend_body(order_ref, q_ref, k_ref, v_ref, bias_ref, mixed_ref, lse_ref):
    query, keys, values, bias = q_ref[...], k_ref[...], v_ref[...], bias_ref[...]
    length, width = query.shape
    total = jnp.zeros((length, width), F32)
    for head in range(width // HD):
        mine = head_lanes(width, head)
        query_h = jnp.where(mine, query, jnp.zeros_like(query))
        scores = lax.dot_general(query_h, keys, NT, preferred_element_type=F32) + bias
        row_max = jnp.max(scores, axis=1, keepdims=True)
        exp_score = jnp.exp(scores - row_max)
        row_total = jnp.sum(exp_score, axis=1, keepdims=True)
        out = jnp.dot(exp_score.astype(BF), values, preferred_element_type=F32)
        total = jnp.where(mine, out * (1.0 / row_total), total)
        lse_ref[0, head : head + 1, :] = (row_max + jnp.log(row_total)).reshape(1, length)
    rows = mixed_ref.shape[1]
    for part in range(length // rows):
        at = order_ref[pl.program_id(0) * (length // rows) + part]
        mixed_ref[at] = total[part * rows : (part + 1) * rows].astype(BF)


def attend_back_body(
    order_ref,
    q_ref,
    dmix_ref,
    lse_ref,
    k_ref,
    v_ref,
    bias_ref,
    cos_ref,
    sin_ref,
    coss_ref,
    sins_ref,
    dq_ref,
    dk_ref,
    dv_ref,
    sums_ref,
    dk_sum,
    dv_sum,
):
    step = pl.program_id(0)

    @pl.when(step == 0)
    def _():
        dk_sum[...] = jnp.zeros_like(dk_sum)
        dv_sum[...] = jnp.zeros_like(dv_sum)
        sums_ref[...] = jnp.zeros_like(sums_ref)

    query, keys, values, bias = q_ref[...], k_ref[...], v_ref[...], bias_ref[...]
    length, width = query.shape
    rows = dmix_ref.shape[1]
    parts = length // rows
    d_mixed = jnp.concatenate([dmix_ref[order_ref[step * parts + p]] for p in range(parts)], axis=0)
    total = jnp.zeros((length, width), F32)
    for head in range(width // HD):
        mine = head_lanes(width, head)
        zero = jnp.zeros_like(query)
        query_h, d_mixed_h = jnp.where(mine, query, zero), jnp.where(mine, d_mixed, zero)
        scores = lax.dot_general(keys, query_h, NT, preferred_element_type=F32) + bias
        probs = jnp.exp(scores - lse_ref[0, head : head + 1, :])
        d_probs = lax.dot_general(values, d_mixed_h, NT, preferred_element_type=F32)
        d_scores = (probs * (d_probs - down_sum(probs * d_probs))).astype(BF)
        dv_sum[...] += jnp.dot(probs.astype(BF), d_mixed_h, preferred_element_type=F32)
        dk_sum[...] += jnp.dot(d_scores, query_h, preferred_element_type=F32)
        d_query = lax.dot_general(d_scores, keys, TN, preferred_element_type=F32)
        total = jnp.where(mine, d_query, total)
    total = total * HD ** (-0.5)
    cosine, sine = spread(cos_ref[...], width), spread(sin_ref[...], width)
    d_query_pre = (total * cosine - turn_pairs(total) * sine).astype(BF)
    dq_ref[...] = d_query_pre
    sums_ref[0:1, :] += down_sum(d_query_pre.astype(F32))

    @pl.when(step == pl.num_programs(0) - 1)
    def _():
        d_key = dk_sum[...]
        all_cos, all_sin = spread(coss_ref[...], width), spread(sins_ref[...], width)
        d_key_pre = (d_key * all_cos - turn_pairs(d_key) * all_sin).astype(BF)
        dk_ref[...] = d_key_pre
        sums_ref[1:2, :] = down_sum(d_key_pre.astype(F32))
        d_value_pre = dv_sum[...].astype(BF)
        dv_ref[...] = d_value_pre
        sums_ref[2:3, :] = down_sum(d_value_pre.astype(F32))


def mixed_rows(mixed_ref):
    parts = mixed_ref.shape[0]
    return jnp.concatenate([mixed_ref[p] for p in range(parts)], axis=1).astype(F32)


def middle_body(
    mixed_ref, tokens_ref, keep_ref, w_ref, norm_ref, head_ref, inner_ref, middle_ref, normed_ref
):
    mixed = mixed_rows(mixed_ref)
    mean, inv = row_stats(mixed, mixed.shape[1])
    inner = ((mixed - mean) * inv * head_ref[2:3, :] + head_ref[3:4, :]).astype(BF)
    inner_ref[...] = inner
    branch = lax.dot_general(inner, w_ref[...], NT, preferred_element_type=F32)
    branch += norm_ref[4:5, :]
    middle = tokens_ref[...].astype(F32) + keep_ref[...] * branch
    middle_ref[...] = middle
    mean, inv = row_stats(middle, middle.shape[1])
    normed_ref[...] = ((middle - mean) * inv * norm_ref[2:3, :] + norm_ref[3:4, :]).astype(BF)


def sigmoid(gate):
    return 1.0 / (1.0 + jnp.exp(-gate))


def d_ffn_body(count, *refs):
    w_ref, out_refs, held = refs[count], refs[count + 1 : -1], refs[-1]
    out = jnp.dot(pick(held, refs[:count]), w_ref[0], preferred_element_type=F32)
    for at in range(count):

        @pl.when(pl.program_id(0) == at)
        def _():
            out_refs[at][...] = out


def ffn_body(count, place_ref, order_ref, *refs):
    w_gu_ref, ffn_ref, unit_ref = refs[2 * count : 2 * count + 3]
    gate_ref, up_ref, stats_ref, held, d_held = refs[-5:]
    rows = pick(held, refs[:count])
    d_ffn = pick(d_held, refs[count : 2 * count])
    gate = jnp.dot(rows, w_gu_ref[0], preferred_element_type=F32) + ffn_ref[0:1, :]
    up = jnp.dot(rows, w_gu_ref[1], preferred_element_type=F32) + ffn_ref[1:2, :]
    gate_ref[0], up_ref[0] = gate, up
    unit = unit_ref[...]
    hidden = gate * sigmoid(gate) * up
    masked = hidden * unit
    scaled = d_ffn * ffn_ref[2:3, :] * unit
    length = rows.shape[0]
    for at, term in enumerate((masked, masked * hidden, scaled, scaled * hidden)):
        stats_ref[0, at : at + 1, :] = jnp.sum(term, axis=1, keepdims=True).reshape(1, length)


def ffn_back_body(count, place_ref, order_ref, *refs):
    gate_ref, up_ref = refs[:2]
    stats_ref, w_gu_ref, ffn_ref, unit_ref = refs[2 + count : 6 + count]
    low_ref, dgate_ref, dup_ref, sums_ref = refs[-5 - count : -1 - count]
    out_refs = refs[-1 - count : -1]
    d_ffn = pick(refs[-1], refs[2 : 2 + count])
    step = pl.program_id(0)

    @pl.when(step == 0)
    def _():
        sums_ref[...] = jnp.zeros_like(sums_ref)

    gate, up, unit = gate_ref[0], up_ref[0], unit_ref[...]
    gain = ffn_ref[2:3, :]
    stats = stats_ref[0]
    mean = stats[:, 0:1] / FF
    inv = lax.rsqrt(stats[:, 1:2] / FF - mean * mean + EPS)
    first = stats[:, 2:3]
    second = inv * (stats[:, 3:4] - mean * first)
    sig = sigmoid(gate)
    silu = gate * sig
    unit_value = (silu * up - mean) * inv
    low_ref[0] = (unit * (unit_value * gain + ffn_ref[3:4, :])).astype(BF)
    d_hidden = unit * inv * (d_ffn * gain * unit - first / FF - unit_value * (second / FF))
    d_gate = (d_hidden * up * sig * (1.0 + gate * (1.0 - sig))).astype(BF)
    d_up = (d_hidden * silu).astype(BF)
    dgate_ref[0], dup_ref[0] = d_gate, d_up
    d_masked = d_ffn * unit
    sums_ref[0:1, :] += down_sum(d_gate.astype(F32))
    sums_ref[1:2, :] += down_sum(d_up.astype(F32))
    sums_ref[2:3, :] += down_sum(d_masked * unit_value)
    sums_ref[3:4, :] += down_sum(d_masked)
    out = lax.dot_general(d_gate, w_gu_ref[0], NT, preferred_element_type=F32)
    out += lax.dot_general(d_up, w_gu_ref[1], NT, preferred_element_type=F32)
    for at in range(count):

        @pl.when(step == at)
        def _():
            out_refs[at][...] = out.astype(BF)


def down_body(count, low_ref, w_ref, *out_refs):
    out = lax.dot_general(low_ref[0], w_ref[0], NT, preferred_element_type=F32)
    for at in range(count):

        @pl.when(pl.program_id(0) == at)
        def _():
            out_refs[at][...] = out.astype(BF)


def spread_back_body(count, place_ref, dq_ref, dk_ref, dv_ref, w_ref, *out_refs):
    out = lax.dot_general(dq_ref[...], w_ref[0], NT, preferred_element_type=F32)
    out += lax.dot_general(dk_ref[...], w_ref[1], NT, preferred_element_type=F32)
    out += lax.dot_general(dv_ref[...], w_ref[2], NT, preferred_element_type=F32)
    for at in range(count):

        @pl.when(pl.program_id(0) == at)
        def _():
            out_refs[at][...] = out.astype(BF)


def product_body(n_left, sizes, block, parity_ref, *refs):
    lefts, at = [], 0
    for count in n_left:
        lefts.append(jnp.concatenate([ref[...] for ref in refs[at : at + count]], axis=0))
        at += count
    rights = []
    for size in sizes:
        rights.append([ref[...] for ref in refs[at : at + size]])
        at += size
    w_refs = refs[at:-3] if len(refs) - at > 2 else []
    kept_ref, away_ref = refs[at + len(w_refs) : at + len(w_refs) + 2]
    parity = parity_ref[0]
    column, along = 0, 0.0
    for left, group in zip(lefts, rights):
        for right in group:
            out = lax.dot_general(left, right, TN, preferred_element_type=F32)
            width = right.shape[1]
            if w_refs and column < w_refs[0].shape[0] * w_refs[0].shape[2]:
                part = w_refs[0][column // width].astype(F32)
                along = along + jnp.sum(out * part, axis=1, keepdims=True)
            low = out.astype(BF)
            for pair in range(out.shape[0] // (2 * block)):
                first = low[2 * pair * block : (2 * pair + 1) * block]
                second = low[(2 * pair + 1) * block : (2 * pair + 2) * block]
                mine = jnp.where(parity == 0, first, second)
                other = jnp.where(parity == 0, second, first)
                kept_ref[pair, :, column : column + width] = mine
                away_ref[pair, :, column : column + width] = other
            column += width
    if w_refs:
        refs[-1][0] = along.reshape(1, along.shape[0])


def product(lefts, rights, parity, block, weights=None):
    width = lefts[0][0].shape[1]
    step = max(256, 2 * block)
    pairs = step // (2 * block)
    columns = sum(right.shape[1] for group in rights for right in group)
    args = [left for group in lefts for left in group]
    specs = [
        pl.BlockSpec((left.shape[0], step), lambda m, *_: (0, m)) for group in lefts for left in group
    ]
    for group in rights:
        args += group
        specs += [whole(right.shape) for right in group]
    outs = [sds((width // (2 * block), block, columns), BF)] * 2
    out_specs = [pl.BlockSpec((pairs, block, columns), lambda m, *_: (m, 0, 0))] * 2
    if weights is not None:
        args.append(weights)
        specs.append(
            pl.BlockSpec((weights.shape[0], step, weights.shape[2]), lambda m, *_: (0, m, 0))
        )
        outs.append(sds((width // step, 1, step), F32))
        out_specs.append(lead((1, step)))
    return call(
        functools.partial(
            product_body, [len(g) for g in lefts], [len(g) for g in rights], block
        ),
        (parity, *args),
        specs,
        outs,
        out_specs,
        (width // step,),
        prefetch=1,
        us=columns / 250,
    )


def add_terms(term_refs):
    total = term_refs[0][...].astype(F32)
    for ref in term_refs[1:]:
        total += ref[...].astype(F32)
    return total


def middle_back_body(count, *refs):
    upstream = add_terms(refs[:count])
    middle_ref, dy_ref, low_ref, keep_ref, mixed_ref, w_ref, norm_ref, head_ref = refs[
        count : count + 8
    ]
    dmid_ref, dbranch_ref, dmix_ref, sums_ref = refs[count + 8 :]
    middle = middle_ref[...]
    width = middle.shape[1]
    mean, inv = row_stats(middle, width)
    unit = (middle - mean) * inv
    d_middle = dy_ref[...].astype(F32) + rows_back(upstream, norm_ref[2:3, :], unit, inv, width)
    dmid_ref[...] = d_middle
    sums_ref[0:1, :] = down_sum(upstream * unit)
    sums_ref[1:2, :] = down_sum(upstream)
    d_branch = (keep_ref[...] * d_middle).astype(BF)
    dbranch_ref[...] = d_branch
    sums_ref[2:3, :] = down_sum(d_branch.astype(F32))
    sums_ref[3:4, :] = down_sum(low_ref[...].astype(F32))
    d_inner = jnp.dot(d_branch, w_ref[...], preferred_element_type=F32)
    mixed = mixed_rows(mixed_ref)
    mean, inv = row_stats(mixed, width)
    unit = (mixed - mean) * inv
    d_mixed = rows_back(d_inner, head_ref[2:3, :], unit, inv, width).astype(BF)
    part = mixed_ref.shape[2]
    for at in range(mixed_ref.shape[0]):
        dmix_ref[at] = d_mixed[:, at * part : (at + 1) * part]
    sums_ref[4:5, :] = down_sum(d_inner * unit)
    sums_ref[5:6, :] = down_sum(d_inner)
    sums_ref[6:8, :] = jnp.zeros((2, width), F32)


def first_back_body(count, *refs):
    upstream = add_terms(refs[:count])
    tokens_ref, dmid_ref, norm_ref, out_ref = refs[count:]
    rows = tokens_ref[...].astype(F32)
    length, width = rows.shape
    mean, inv = row_stats(rows, width)
    unit = (rows - mean) * inv
    d_in = rows_back(upstream[:length], norm_ref[0:1, :], unit, inv, width)
    out_ref[...] = dmid_ref[:length] + d_in


def layer_out_body(count, *refs):
    branch = add_terms(refs[:count])
    middle_ref, keep_ref, norm_ref, out_ref = refs[count:]
    out = middle_ref[...] + keep_ref[...] * (branch + norm_ref[5:6, :])
    out_ref[...] = out[: out_ref.shape[0]].astype(BF)


def rope_tables(coords):
    half_dim = HD // 2
    index_j = jnp.arange(half_dim // 2).astype(F32)
    frequency = jnp.repeat(jnp.exp(index_j * (-2.0 * math.log(10000.0) / half_dim)), 2)
    spots = jnp.arange(GRID_SIDE)
    angles = (spots.astype(F32) * 0.5)[:, None] * frequency
    lane_half = jnp.arange(LANES) // half_dim % 2
    tables = jnp.stack([jnp.cos(angles), jnp.sin(angles)])
    tables = jnp.tile(tables, (1, 1, LANES // half_dim))
    tables = jnp.concatenate([tables * (lane_half == half) for half in range(2)], axis=1)
    chosen = jnp.concatenate(
        [(coords[half][:, None] == spots).astype(F32) for half in range(2)], axis=1
    )
    both = jnp.dot(
        chosen,
        jnp.concatenate([tables[0], tables[1]], axis=1),
        precision=lax.Precision.HIGHEST,
    )
    return both[:, :LANES], both[:, LANES:]


def pad_to(value, axis, size):
    widths = [(0, 0)] * value.ndim
    widths[axis] = (0, size - value.shape[axis])
    return jnp.pad(value, widths)


def ceil_to(value, unit):
    return -(-value // unit) * unit


def on_device(
    n_dp,
    n_tp,
    tokens,
    cotangent,
    w_qkv,
    w_o,
    w_gu,
    w_down,
    norm_params,
    head_params,
    ffn_params,
    token_mask,
    empty_flag,
    coords,
):
    tp_index = lax.axis_index("tensor")
    own_rows, width = tokens.shape[1:]
    local = w_qkv.shape[2]
    units = w_gu.shape[2]
    heads = local // HD
    rows = ceil_to(own_rows, 16)
    seq = rows * n_tp
    lanes = ceil_to(units, LANES)
    step_rows = 2 * rows if n_tp % 2 == 0 else rows
    steps = seq // step_rows
    offsets = ring_offsets(n_tp)
    order = (jnp.array(offsets, jnp.int32) + tp_index) % n_tp
    place = {offset % n_tp: at for at, offset in enumerate(offsets)}
    own = whole((rows, width))

    normed = call(
        first_norm_body,
        (tokens[0], norm_params),
        [whole((own_rows, width)), whole(norm_params.shape)],
        [sds((rows, width), BF)],
        [own],
        (1,),
        us=1.2,
    )[0]
    normed_parts = ring_gather(normed, n_tp)

    ups = n_tp // 2
    arrivals = [[0]]
    for s in range(1, ups + 1):
        arrivals.append(sorted({place[-s % n_tp], place[s % n_tp]}))
    leaving = sorted({place[ups % n_tp], place[-1 % n_tp]})
    staying = [at for at in range(n_tp) if at not in leaving]
    leavings = [group for group in (leaving, staying) if group]

    slots = jnp.concatenate([token_mask, coords[0]], axis=0).reshape(3, n_tp, own_rows)
    slots = pad_to(slots, 2, rows)
    slots = jnp.stack(
        [lax.dynamic_index_in_dim(slots, order[at], 1, keepdims=False) for at in range(n_tp)], 1
    )
    mask = slots[0]
    bias = jnp.where(mask > 0, 0.0, -1e30).astype(F32)
    bias_row, bias_col = bias.reshape(1, seq), bias.reshape(seq, 1)
    keep = (mask[0].astype(F32) * (1.0 - empty_flag[0].astype(F32)))[:, None]
    cos_all, sin_all = rope_tables(slots[1:].reshape(2, seq))

    head_local = lax.dynamic_slice_in_dim(head_params, tp_index * local, local, 1)
    ffn_local = pad_to(
        lax.dynamic_slice_in_dim(ffn_params, tp_index * units, units, 1), 1, lanes
    )
    lane_at = jnp.arange(lanes)
    unit_row = ((lane_at < units) & (tp_index * units + lane_at < FF)).astype(F32)[None]

    tokens_own = pad_to(tokens[0], 0, rows)
    dy_own = pad_to(cotangent[0], 0, rows)
    d_low = (keep * dy_own.astype(F32)).astype(BF)

    w_order = dp_order(n_dp)
    full_qkv = put_back(w_order, dp_gather(w_qkv, n_dp), 1)
    filled = ()
    for turn, group in enumerate(arrivals):
        if turn > 1:
            normed_parts[group[0]] = after(normed_parts[group[0]], filled[0])
        filled = call(
            functools.partial(project_body, len(group)),
            (
                jnp.array(group, jnp.int32),
                *(normed_parts[at] for at in group),
                full_qkv,
                head_local,
                cos_all,
                sin_all,
            ),
            [own] * len(group)
            + [whole(full_qkv.shape), whole(head_local.shape)]
            + [pl.BlockSpec((rows, LANES), lambda s, place, *_: (place[s], 0))] * 2,
            [sds((n_tp, rows, local), BF)] * 3,
            [placed((rows, local))] * 3,
            (len(group),),
            scratch=[pltpu.VMEM((rows, width), BF)],
            prefetch=1,
            held=filled,
            us=2.0 * len(group),
        )
    query, key, value = (part.reshape(seq, local) for part in filled)
    d_low_late = after(d_low, normed_parts[-1], normed_parts[ups])
    d_low_first = [ring_up(d_low_late, n_tp), ring_down(d_low_late, n_tp)]
    strip = pl.BlockSpec((step_rows, local), lambda s, *_: (s, 0))
    mixed_heads, lse = call(
        attend_body,
        (order, query, key, value, bias_row),
        [strip, whole((seq, local)), whole((seq, local)), whole((1, seq))],
        [sds((n_tp, rows, local), BF), sds((steps, heads, step_rows), F32)],
        [whole((n_tp, rows, local)), lead((heads, step_rows))],
        (steps,),
        prefetch=1,
        us=10,
    )
    mixed_heads = after(mixed_heads, *d_low_first)
    mixed = lax.all_to_all(mixed_heads, "tensor", split_axis=0, concat_axis=0, tiled=True)

    w_o_late = after(w_o, normed_parts[1])
    o_parts = call(
        lay_body,
        (order, *ring_gather(w_o_late, n_tp)),
        [whole(w_o.shape)] * n_tp,
        [sds((n_tp,) + w_o.shape[::-1], BF)],
        [whole((n_tp,) + w_o.shape[::-1])],
        (1,),
        prefetch=1,
        us=0.7,
    )[0]
    o_parts = jnp.concatenate([o_parts[at] for at in range(n_tp)], axis=1)
    full_o = put_back(w_order, dp_gather(o_parts, n_dp), 0)
    w_ffn = pad_to(jnp.concatenate([w_gu, w_down.T[None]], axis=0), 2, lanes)
    w_ffn = dp_gather(after(w_ffn, normed_parts[1]), n_dp, mixed)

    inner_low, middle, normed_two = call(
        middle_body,
        (mixed, tokens_own, keep, full_o, norm_params, head_params),
        [
            whole(mixed.shape),
            own,
            whole((rows, 1)),
            whole(full_o.shape),
            whole(norm_params.shape),
            whole(head_params.shape),
        ],
        [sds((rows, width), BF), sds((rows, width), F32), sds((rows, width), BF)],
        [own] * 3,
        (1,),
        us=3,
    )
    two_parts = ring_gather(normed_two, n_tp)
    full_ffn = put_back(w_order, [after(part, normed_two) for part in w_ffn], 1)
    d_low_parts = gather_rest(d_low, d_low_first, n_tp, mixed)

    hidden_shape = (n_tp, rows, lanes)
    gu_block = pl.BlockSpec((2, width, lanes), lambda *_: (0, 0, 0))
    down_block = pl.BlockSpec((1, width, lanes), lambda *_: (2, 0, 0))
    d_ffn = [None] * n_tp
    near = [at for group in arrivals[:2] for at in group]
    for group in [near] + arrivals[2:]:
        outs = call(
            functools.partial(d_ffn_body, len(group)),
            (*(d_low_parts[at] for at in group), full_ffn),
            [own] * len(group) + [down_block],
            [sds((rows, lanes), F32)] * len(group),
            [whole((rows, lanes))] * len(group),
            (len(group),),
            scratch=[pltpu.VMEM((rows, width), BF)],
            us=1.4 * len(group),
        )
        for at, part in zip(group, outs):
            d_ffn[at] = part
    hidden_block = placed((rows, lanes))
    filled = ()
    for turn, group in enumerate(arrivals):
        if turn > 1:
            two_parts[group[0]] = after(two_parts[group[0]], filled[0])
        filled = call(
            functools.partial(ffn_body, len(group)),
            (
                jnp.array(group, jnp.int32),
                order,
                *(two_parts[at] for at in group),
                *(d_ffn[at] for at in group),
                full_ffn,
                ffn_local,
                unit_row,
            ),
            [own] * len(group)
            + [whole((rows, lanes))] * len(group)
            + [gu_block, whole(ffn_local.shape), whole(unit_row.shape)],
            [sds(hidden_shape, F32)] * 2 + [sds((n_tp, 4, rows), F32)],
            [hidden_block] * 2 + [ordered((4, rows))],
            (len(group),),
            scratch=[pltpu.VMEM((rows, width), BF), pltpu.VMEM((rows, lanes), F32)],
            prefetch=2,
            held=filled,
            us=1.2 + 2.2 * len(group),
        )
    gate, up, stats = filled
    stats = jnp.swapaxes(sum_shifts(stats, n_tp), 1, 2)
    filled, ffn_sums, d_two_parts = (), 0.0, [None] * n_tp
    for group in leavings:
        outs = call(
            functools.partial(ffn_back_body, len(group)),
            (
                jnp.array(group, jnp.int32),
                order,
                gate,
                up,
                *(d_ffn[at] for at in group),
                stats,
                full_ffn,
                ffn_local,
                unit_row,
            ),
            [hidden_block] * 2
            + [whole((rows, lanes))] * len(group)
            + [
                ordered((rows, 4)),
                gu_block,
                whole(ffn_local.shape),
                whole(unit_row.shape),
            ],
            [sds(hidden_shape, BF)] * 3
            + [sds((4, lanes), F32)]
            + [sds((rows, width), BF)] * len(group),
            [hidden_block] * 3 + [whole((4, lanes))] + [own] * len(group),
            (len(group),),
            scratch=[pltpu.VMEM((rows, lanes), F32)],
            prefetch=2,
            held=filled,
            us=3.7 * len(group),
        )
        filled = outs[:3]
        ffn_sums = ffn_sums + outs[3]
        for at, piece in zip(group, outs[4:]):
            d_two_parts[at] = piece
    ffn_low, d_gate, d_up = filled
    d_two_first = scatter_first(d_two_parts, n_tp)
    d_two_first = [after(d_two_first[0], *d_two_first[1:])] + d_two_first[1:]
    d_two_terms = scatter_rest(d_two_parts, d_two_first, n_tp)
    branch_parts = call(
        functools.partial(down_body, n_tp),
        (ffn_low, full_ffn),
        [lead((rows, lanes)), down_block],
        [sds((rows, width), BF)] * n_tp,
        [own] * n_tp,
        (n_tp,),
        us=2.8,
    )

    d_two_terms[0] = after(d_two_terms[0], *branch_parts)

    parity = (lax.axis_index("dp") % 2).astype(jnp.int32)[None]
    block = width // n_dp
    hidden_rows = [part.reshape(seq, lanes) for part in (d_gate, d_up, ffn_low)]
    grad_ffn = product([two_parts, d_low_parts], [hidden_rows[:2], hidden_rows[2:]], parity, block)
    grad_ffn = pair_sum(grad_ffn, n_dp)


    n_terms = len(d_two_terms)
    d_middle, d_branch, d_mixed_rows, mid_sums = call(
        functools.partial(middle_back_body, n_terms),
        (*d_two_terms, middle, dy_own, d_low, keep, mixed, full_o, norm_params, head_params),
        [own] * n_terms
        + [own] * 3
        + [
            whole((rows, 1)),
            whole(mixed.shape),
            whole(full_o.shape),
            whole(norm_params.shape),
            whole(head_params.shape),
        ],
        [
            sds((rows, width), F32),
            sds((rows, width), BF),
            sds((n_tp, rows, local), BF),
            sds((8, width), F32),
        ],
        [own, own, whole((n_tp, rows, local)), whole((8, width))],
        (1,),
        us=3.6,
    )
    d_mixed = lax.all_to_all(d_mixed_rows, "tensor", split_axis=0, concat_axis=0, tiled=True)
    d_mixed = after(d_mixed, grad_ffn)
    grad_ffn = dp_scatter(grad_ffn, n_dp)
    branch_parts = [after(part, d_mixed) for part in branch_parts]
    branch_first = scatter_first(branch_parts, n_tp)

    table = pl.BlockSpec((step_rows, LANES), lambda s, *_: (s, 0))
    all_rows = whole((seq, local))
    d_query, d_key, d_value, head_sums = call(
        attend_back_body,
        (
            order,
            query,
            d_mixed,
            lse,
            key,
            value,
            bias_col,
            cos_all,
            sin_all,
            cos_all,
            sin_all,
        ),
        [
            strip,
            whole(d_mixed.shape),
            lead((heads, step_rows)),
            all_rows,
            all_rows,
            whole((seq, 1)),
            table,
            table,
            whole((seq, LANES)),
            whole((seq, LANES)),
        ],
        [sds((seq, local), BF)] * 3 + [sds((8, local), F32)],
        [strip, all_rows, all_rows, whole((8, local))],
        (steps,),
        scratch=[pltpu.VMEM((seq, local), F32)] * 2,
        prefetch=1,
        us=24,
    )
    d_query = after(d_query, *branch_first)
    chunk = pl.BlockSpec((rows, local), lambda s, place, *_: (place[s], 0))
    d_one_parts = [None] * n_tp
    for group in leavings:
        outs = call(
            functools.partial(spread_back_body, len(group)),
            (jnp.array(group, jnp.int32), d_query, d_key, d_value, full_qkv),
            [chunk] * 3 + [whole(full_qkv.shape)],
            [sds((rows, width), BF)] * len(group),
            [own] * len(group),
            (len(group),),
            prefetch=1,
            us=1.0 * len(group),
        )
        for at, piece in zip(group, outs):
            d_one_parts[at] = piece
    d_proj = [after(part, *[d_one_parts[at] for at in leaving]) for part in (d_query, d_key, d_value)]
    *grad_late, along_normed = product(
        [normed_parts, [d_branch]], [d_proj, [inner_low]], parity, block, full_qkv
    )
    along_normed = along_normed.reshape(-1)
    shift_one = sum(
        jnp.sum(full_qkv[at].astype(F32) * head_sums[at : at + 1], axis=1) for at in range(3)
    )
    grad_late = pair_sum(grad_late, n_dp)

    d_one_first = scatter_first(d_one_parts, n_tp)
    arrived = [after(d_one_first[0], grad_late, grad_ffn)] + d_one_first[1:]
    sent = []
    d_one_terms = scatter_rest(d_one_parts, arrived, n_tp, sent)

    small = [along_normed, shift_one, mid_sums[:6].reshape(-1)]
    small += [head_sums[0], head_sums[2], ffn_sums[:, :units].reshape(-1)]
    small = jnp.concatenate(small)
    small_len = small.shape[0]
    small = pad_to(small, 0, ceil_to(small_len, 8 * LANES)).reshape(-1, LANES)
    small = sum_over(after(small, grad_ffn), "dp", n_dp)
    small_sum = small
    grad_late = dp_scatter(after(grad_late, small), n_dp)
    late_parts = grad_late
    small = after(small, *sent)
    small = [part.reshape(-1) for part in gather_small(small, n_tp)]
    head_at = 8 * width
    ffn_at = head_at + 2 * local
    norm_sums = sum_alike([part[:head_at] for part in small]).reshape(8, width)
    head_bias = jnp.zeros((2, width), F32)
    ffn_total = jnp.zeros((4, n_tp * units), F32)
    for s, part in enumerate(small):
        owner = (tp_index - s) % n_tp
        head_bias = lax.dynamic_update_slice(
            head_bias, part[head_at:ffn_at].reshape(2, local), (0, owner * local)
        )
        ffn_total = lax.dynamic_update_slice(
            ffn_total, part[ffn_at:small_len].reshape(4, units), (0, owner * units)
        )
    gain_one = (norm_sums[0:1] - norm_params[1:2] * norm_sums[1:2]) / norm_params[0:1]
    norm_total = jnp.concatenate([gain_one, norm_sums[1:6]], axis=0)
    head_total = jnp.concatenate([head_bias, norm_sums[6:8]], axis=0)

    grad_early = sum_parts(grad_ffn)
    grad_late = sum_parts(grad_late)
    grad_o = grad_late[:, 3 * local :].astype(BF).reshape(-1, n_tp, local).swapaxes(0, 1)
    grad_o = swap_sum(grad_o, n_tp).T
    grad_gu = jnp.stack([grad_early[:, :units], grad_early[:, lanes : lanes + units]])
    grad_down = grad_early[:, 2 * lanes : 2 * lanes + units].T
    grad_qkv = grad_late[:, : 3 * local].reshape(-1, 3, local).swapaxes(0, 1)

    branch_first = [after(branch_first[0], small_sum)] + branch_first[1:]
    branch_terms = scatter_rest(branch_parts, branch_first, n_tp)
    branch_terms[1] = after(branch_terms[1], late_parts)
    layer_out = call(
        functools.partial(layer_out_body, n_terms),
        (*branch_terms, middle, keep, norm_params),
        [own] * n_terms + [own, whole((rows, 1)), whole(norm_params.shape)],
        [sds((own_rows, width), BF)],
        [whole((own_rows, width))],
        (1,),
        us=2,
    )[0]
    d_one_terms[0] = after(d_one_terms[0], grad_late, norm_total, ffn_total)
    d_tokens = call(
        functools.partial(first_back_body, n_terms),
        (*d_one_terms, tokens[0], d_middle, norm_params),
        [own] * n_terms + [whole((own_rows, width)), own, whole(norm_params.shape)],
        [sds((own_rows, width), F32)],
        [whole((own_rows, width))],
        (1,),
        us=1.5,
    )[0]

    return (
        layer_out[None],
        d_tokens[None],
        grad_qkv,
        grad_o,
        grad_gu,
        grad_down,
        norm_total,
        head_total,
        ffn_total,
    )


def solution(mesh):
    placed = (
        P("dp", "tensor", None),
        P("dp", "tensor", None),
        P(None, "dp", "tensor"),
        P("tensor", "dp"),
        P(None, "dp", "tensor"),
        P("tensor", "dp"),
        P(),
        P(),
        P(),
        P("dp", None),
        P("dp"),
        P("dp", None, None),
    )
    return jax.shard_map(
        functools.partial(on_device, mesh.shape["dp"], mesh.shape["tensor"]),
        mesh=mesh,
        in_specs=placed,
        out_specs=(
            P("dp", "tensor", None),
            P("dp", "tensor", None),
            P(None, "dp", "tensor"),
            P("tensor", "dp"),
            P(None, "dp", "tensor"),
            P("tensor", "dp"),
            P(),
            P(),
            P(),
        ),
        check_vma=False,
    )
```

```python
import functools
import math

import jax
import jax.numpy as jnp
from jax import lax
from jax.experimental import pallas as pl
from jax.experimental.pallas import tpu as pltpu
from jax.sharding import PartitionSpec as P

FF = 2730
HD = 64
FF_PAD = 2736
GRID_SIDE = 32
LANES = 128
EPS = 1e-06
VMEM_LIMIT = 44 * 2**20
COST_SCALE = 4.0
BF = jnp.bfloat16
F32 = jnp.float32
NT = (((1,), (1,)), ((), ()))
TN = (((0,), (0,)), ((), ()))


def ring_up(value, size):
    return lax.ppermute(value, "tensor", [(j, (j + 1) % size) for j in range(size)])


def ring_down(value, size):
    return lax.ppermute(value, "tensor", [(j, (j - 1) % size) for j in range(size)])


def ring_offsets(size):
    ups = size // 2
    return [0] + [-s for s in range(1, ups + 1)] + [s for s in range(1, size - ups)]


def gather_rest(own, first, size, late=None):
    ups = size // 2
    downs = size - 1 - ups
    upper, lower = first[:1], first[1:]
    for s in range(1, ups):
        up_now = upper[-1] if late is None else after(upper[-1], late)
        upper.append(ring_up(up_now, size))
        if s < downs:
            down_now = lower[-1] if late is None else after(lower[-1], late)
            lower.append(ring_down(down_now, size))
    return [own] + upper + lower


def ring_gather(own, size):
    return gather_rest(own, [ring_up(own, size), ring_down(own, size)], size)


def after(value, *others):
    return lax.optimization_barrier((value,) + others)[0]


def sum_shifts(value, size):
    total = value
    for s in range(1, size):
        total = total + lax.ppermute(
            value, "tensor", [(j, (j + s) % size) for j in range(size)]
        )
    return total


def gather_small(value, size):
    return [value] + [
        lax.ppermute(value, "tensor", [(j, (j + s) % size) for j in range(size)])
        for s in range(1, size)
    ]


def sum_alike(terms):
    while len(terms) > 1 and len(terms) % 2 == 0:
        half = len(terms) // 2
        terms = [terms[s] + terms[s + half] for s in range(half)]
    return functools.reduce(jnp.add, terms)


def swap_sum(blocks, size):
    index = lax.axis_index("tensor")

    def block_for(s):
        return lax.dynamic_index_in_dim(blocks, (index + s) % size, 0, keepdims=False)

    total = block_for(0).astype(F32)
    for s in range(1, size):
        came = lax.ppermute(block_for(s), "tensor", [(j, (j + s) % size) for j in range(size)])
        total = total + came.astype(F32)
    return total


def add_low(left, right):
    return (left.astype(F32) + right.astype(F32)).astype(BF)


def scatter_first(pieces, size):
    place = {offset % size: at for at, offset in enumerate(ring_offsets(size))}
    ups = size // 2
    arrived = []
    if size > 1:
        arrived.append(ring_up(pieces[place[ups % size]], size))
    if ups == size - 1 - ups:
        arrived.append(ring_down(pieces[place[-ups % size]], size))
    elif size > 2:
        arrived.append(ring_down(pieces[place[(1 - ups) % size]], size))
    return arrived


def scatter_rest(pieces, arrived, size, sent=None):
    place = {offset % size: at for at, offset in enumerate(ring_offsets(size))}
    ups = size // 2
    downs = size - 1 - ups
    up_now = arrived[0]
    for s in range(ups - 1, 0, -1):
        up_now = add_low(up_now, pieces[place[s]])
        if sent is not None:
            sent.append(up_now)
        up_now = ring_up(up_now, size)
    terms = [pieces[0], up_now]
    if downs:
        down_now = arrived[1]
        for s in range(downs - 1, 0, -1):
            down_now = ring_down(add_low(down_now, pieces[place[-s % size]]), size)
        terms.append(down_now)
    return terms


def dp_bits(size):
    bits = []
    step = 2
    while step < size:
        bits.append(step)
        step *= 2
    return bits + ([1] if size > 1 else [])


def flip(value, bit, size):
    return lax.ppermute(value, "dp", [(j, j ^ bit) for j in range(size)])


def dp_gather(block, size, late=None):
    stacked = block[None]
    bits = dp_bits(size)
    for bit in bits[:-1]:
        other = flip(stacked, bit, size)
        if late is not None and bit == bits[-2]:
            other = after(other, late)
        stacked = jnp.concatenate([stacked, other], axis=0)
    return [stacked] + [flip(stacked, bit, size) for bit in bits[-1:]]


def dp_order(size):
    order = [0]
    for bit in dp_bits(size):
        order = order + [at ^ bit for at in order]
    return jnp.array(order, jnp.int32) ^ lax.axis_index("dp")


def pair_sum(halves, size):
    kept, away = halves
    return add_low(kept, flip(away, 1, size))


def dp_scatter(merged, size):
    groups = [[j for j in range(size) if j % 2 == c] for c in range(2)]
    return lax.all_to_all(
        merged, "dp", split_axis=0, concat_axis=0, tiled=True, axis_index_groups=groups
    )


def sum_parts(parts):
    return jnp.sum(parts.astype(F32), axis=0)


def sum_over(value, axis, size):
    copies = jnp.broadcast_to(value[None], (size,) + value.shape)
    return jnp.sum(lax.all_to_all(copies, axis, split_axis=0, concat_axis=0, tiled=True), axis=0)


def whole(shape):
    return pl.BlockSpec(shape, lambda *_: (0,) * len(shape))


def lead(shape):
    return pl.BlockSpec((1,) + shape, lambda s, *_: (s,) + (0,) * len(shape))


def placed(shape):
    return pl.BlockSpec((1,) + shape, lambda s, place, *_: (place[s],) + (0,) * len(shape))


def ordered(shape):
    return pl.BlockSpec(
        (1,) + shape, lambda s, place, order: (order[place[s]],) + (0,) * len(shape)
    )


def call(
    body, args, specs, outs, out_specs, grid, scratch=(), prefetch=0, held=(), us=1.0
):
    first_held = len(args)
    args = tuple(args) + tuple(held)
    specs = list(specs) + [pl.BlockSpec(memory_space=pl.ANY)] * len(held)
    return pl.pallas_call(
        body,
        out_shape=outs,
        grid_spec=pltpu.PrefetchScalarGridSpec(
            num_scalar_prefetch=prefetch,
            grid=grid,
            in_specs=specs,
            out_specs=out_specs,
            scratch_shapes=list(scratch),
        ),
        input_output_aliases={first_held + at: at for at in range(len(held))},
        compiler_params=pltpu.CompilerParams(vmem_limit_bytes=VMEM_LIMIT),
        cost_estimate=pl.CostEstimate(
            flops=int(us * COST_SCALE * 1e9), bytes_accessed=1, transcendentals=0
        ),
    )(*args)


def sds(shape, dtype):
    return jax.ShapeDtypeStruct(shape, dtype)


def row_stats(rows, count):
    mean = jnp.sum(rows, axis=1, keepdims=True) / count
    power = jnp.sum(rows * rows, axis=1, keepdims=True) / count
    return mean, lax.rsqrt(power - mean * mean + EPS)


def rows_back(upstream, gain, unit, inv, count):
    scaled = upstream * gain
    first = jnp.sum(scaled, axis=1, keepdims=True) / count
    second = jnp.sum(scaled * unit, axis=1, keepdims=True) / count
    return inv * (scaled - first - unit * second)


def down_sum(rows):
    return jnp.sum(rows, axis=0, keepdims=True)


def put_back_body(count, near, *refs):
    in_refs, out_ref = refs[1:-1], refs[-1]
    for at in range(count):

        @pl.when(pl.program_id(0) // near == at)
        def _():
            out_ref[...] = in_refs[at][(0,) * (len(in_refs[at].shape) - len(out_ref.shape))]


def put_back(order, stacks, axis):
    count, near, block = len(stacks), stacks[0].shape[0], stacks[0].shape[1:]
    size = count * near
    shape = tuple(n * size if at == axis else n for at, n in enumerate(block))
    if block[axis] % (LANES if axis == len(block) - 1 else 16):
        stacked = jnp.concatenate(stacks, axis=0)
        placed = jnp.zeros_like(stacked).at[order].set(stacked)
        return jnp.moveaxis(placed, 0, axis).reshape(shape)

    def taken(at):
        return pl.BlockSpec(
            (1,) + block,
            lambda r, order: (jnp.clip(r - at * near, 0, near - 1),) + (0,) * len(block),
        )

    return call(
        functools.partial(put_back_body, count, near),
        (order, *stacks),
        [taken(at) for at in range(count)],
        [sds(shape, stacks[0].dtype)],
        [
            pl.BlockSpec(
                block,
                lambda r, order: tuple(order[r] if at == axis else 0 for at in range(len(block))),
            )
        ],
        (size,),
        prefetch=1,
        us=size * math.prod(block) / 2**19,
    )[0]


def first_norm_body(tokens_ref, norm_ref, normed_ref):
    rows = tokens_ref[...].astype(F32)
    length, width = rows.shape
    mean, inv = row_stats(rows, width)
    normed_ref[:length] = ((rows - mean) * inv * norm_ref[0:1, :] + norm_ref[1:2, :]).astype(BF)
    normed_ref[length:] = jnp.zeros((normed_ref.shape[0] - length, width), BF)


def lay_body(order_ref, *refs):
    out_ref = refs[-1]
    for at, ref in enumerate(refs[:-1]):
        piece = ref[...].astype(F32).T.astype(BF)
        out_ref[order_ref[at]] = piece


def spread(table, width):
    return table if width == LANES else jnp.concatenate([table] * (width // LANES), axis=1)


def turn_pairs(rows):
    width = rows.shape[1]
    even = lax.broadcasted_iota(jnp.int32, (1, width), 1) % 2 == 0
    return jnp.where(even, -pltpu.roll(rows, width - 1, 1), pltpu.roll(rows, 1, 1))


def pick(held, chunk_refs):
    for at, ref in enumerate(chunk_refs):

        @pl.when(pl.program_id(0) == at)
        def _():
            held[...] = ref[...]

    return held[...]


def project_body(count, place_ref, *refs):
    chunk_refs = refs[:count]
    w_ref, head_ref, cos_ref, sin_ref = refs[count : count + 4]
    q_ref, k_ref, v_ref, held = refs[-4:]
    rows = pick(held, chunk_refs)
    width = w_ref.shape[2]
    cosine, sine = spread(cos_ref[...], width), spread(sin_ref[...], width)
    query = jnp.dot(rows, w_ref[0], preferred_element_type=F32) + head_ref[0:1, :]
    key = jnp.dot(rows, w_ref[1], preferred_element_type=F32)
    value = jnp.dot(rows, w_ref[2], preferred_element_type=F32) + head_ref[1:2, :]
    query_low = (query * cosine + turn_pairs(query) * sine).astype(BF)
    q_ref[0] = (query_low.astype(F32) * HD ** (-0.5)).astype(BF)
    k_ref[0] = (key * cosine + turn_pairs(key) * sine).astype(BF)
    v_ref[0] = value.astype(BF)


def head_lanes(width, head):
    lane = lax.broadcasted_iota(jnp.int32, (1, width), 1)
    return (lane >= head * HD) & (lane < (head + 1) * HD)


def attend_body(order_ref, q_ref, k_ref, v_ref, bias_ref, mixed_ref, lse_ref):
    query, keys, values, bias = q_ref[...], k_ref[...], v_ref[...], bias_ref[...]
    length, width = query.shape
    total = jnp.zeros((length, width), F32)
    for head in range(width // HD):
        mine = head_lanes(width, head)
        query_h = jnp.where(mine, query, jnp.zeros_like(query))
        scores = lax.dot_general(query_h, keys, NT, preferred_element_type=F32) + bias
        row_max = jnp.max(scores, axis=1, keepdims=True)
        exp_score = jnp.exp(scores - row_max)
        row_total = jnp.sum(exp_score, axis=1, keepdims=True)
        out = jnp.dot(exp_score.astype(BF), values, preferred_element_type=F32)
        total = jnp.where(mine, out * (1.0 / row_total), total)
        lse_ref[0, head : head + 1, :] = (row_max + jnp.log(row_total)).reshape(1, length)
    rows = mixed_ref.shape[1]
    for part in range(length // rows):
        at = order_ref[pl.program_id(0) * (length // rows) + part]
        mixed_ref[at] = total[part * rows : (part + 1) * rows].astype(BF)


def attend_back_body(
    order_ref,
    q_ref,
    dmix_ref,
    lse_ref,
    k_ref,
    v_ref,
    bias_ref,
    cos_ref,
    sin_ref,
    coss_ref,
    sins_ref,
    dq_ref,
    dk_ref,
    dv_ref,
    sums_ref,
    dk_sum,
    dv_sum,
):
    step = pl.program_id(0)

    @pl.when(step == 0)
    def _():
        dk_sum[...] = jnp.zeros_like(dk_sum)
        dv_sum[...] = jnp.zeros_like(dv_sum)
        sums_ref[...] = jnp.zeros_like(sums_ref)

    query, keys, values, bias = q_ref[...], k_ref[...], v_ref[...], bias_ref[...]
    length, width = query.shape
    rows = dmix_ref.shape[1]
    parts = length // rows
    d_mixed = jnp.concatenate([dmix_ref[order_ref[step * parts + p]] for p in range(parts)], axis=0)
    total = jnp.zeros((length, width), F32)
    for head in range(width // HD):
        mine = head_lanes(width, head)
        zero = jnp.zeros_like(query)
        query_h, d_mixed_h = jnp.where(mine, query, zero), jnp.where(mine, d_mixed, zero)
        scores = lax.dot_general(keys, query_h, NT, preferred_element_type=F32) + bias
        probs = jnp.exp(scores - lse_ref[0, head : head + 1, :])
        d_probs = lax.dot_general(values, d_mixed_h, NT, preferred_element_type=F32)
        d_scores = (probs * (d_probs - down_sum(probs * d_probs))).astype(BF)
        dv_sum[...] += jnp.dot(probs.astype(BF), d_mixed_h, preferred_element_type=F32)
        dk_sum[...] += jnp.dot(d_scores, query_h, preferred_element_type=F32)
        d_query = lax.dot_general(d_scores, keys, TN, preferred_element_type=F32)
        total = jnp.where(mine, d_query, total)
    total = total * HD ** (-0.5)
    cosine, sine = spread(cos_ref[...], width), spread(sin_ref[...], width)
    d_query_pre = (total * cosine - turn_pairs(total) * sine).astype(BF)
    dq_ref[...] = d_query_pre
    sums_ref[0:1, :] += down_sum(d_query_pre.astype(F32))

    @pl.when(step == pl.num_programs(0) - 1)
    def _():
        d_key = dk_sum[...]
        all_cos, all_sin = spread(coss_ref[...], width), spread(sins_ref[...], width)
        d_key_pre = (d_key * all_cos - turn_pairs(d_key) * all_sin).astype(BF)
        dk_ref[...] = d_key_pre
        sums_ref[1:2, :] = down_sum(d_key_pre.astype(F32))
        d_value_pre = dv_sum[...].astype(BF)
        dv_ref[...] = d_value_pre
        sums_ref[2:3, :] = down_sum(d_value_pre.astype(F32))


def mixed_rows(mixed_ref):
    parts = mixed_ref.shape[0]
    return jnp.concatenate([mixed_ref[p] for p in range(parts)], axis=1).astype(F32)


def middle_body(
    mixed_ref, tokens_ref, keep_ref, w_ref, norm_ref, head_ref, inner_ref, middle_ref, normed_ref
):
    mixed = mixed_rows(mixed_ref)
    mean, inv = row_stats(mixed, mixed.shape[1])
    inner = ((mixed - mean) * inv * head_ref[2:3, :] + head_ref[3:4, :]).astype(BF)
    inner_ref[...] = inner
    branch = lax.dot_general(inner, w_ref[...], NT, preferred_element_type=F32)
    branch += norm_ref[4:5, :]
    middle = tokens_ref[...].astype(F32) + keep_ref[...] * branch
    middle_ref[...] = middle
    mean, inv = row_stats(middle, middle.shape[1])
    normed_ref[...] = ((middle - mean) * inv * norm_ref[2:3, :] + norm_ref[3:4, :]).astype(BF)


def sigmoid(gate):
    return 1.0 / (1.0 + jnp.exp(-gate))


def d_ffn_body(count, *refs):
    w_ref, out_refs, held = refs[count], refs[count + 1 : -1], refs[-1]
    out = jnp.dot(pick(held, refs[:count]), w_ref[0], preferred_element_type=F32)
    for at in range(count):

        @pl.when(pl.program_id(0) == at)
        def _():
            out_refs[at][...] = out


def ffn_body(count, place_ref, order_ref, *refs):
    w_gu_ref, ffn_ref, unit_ref = refs[2 * count : 2 * count + 3]
    gate_ref, up_ref, stats_ref, held, d_held = refs[-5:]
    rows = pick(held, refs[:count])
    d_ffn = pick(d_held, refs[count : 2 * count])
    gate = jnp.dot(rows, w_gu_ref[0], preferred_element_type=F32) + ffn_ref[0:1, :]
    up = jnp.dot(rows, w_gu_ref[1], preferred_element_type=F32) + ffn_ref[1:2, :]
    gate_ref[0], up_ref[0] = gate, up
    unit = unit_ref[...]
    hidden = gate * sigmoid(gate) * up
    masked = hidden * unit
    scaled = d_ffn * ffn_ref[2:3, :] * unit
    length = rows.shape[0]
    for at, term in enumerate((masked, masked * hidden, scaled, scaled * hidden)):
        stats_ref[0, at : at + 1, :] = jnp.sum(term, axis=1, keepdims=True).reshape(1, length)


def ffn_back_body(count, place_ref, order_ref, *refs):
    gate_ref, up_ref = refs[:2]
    stats_ref, w_gu_ref, ffn_ref, unit_ref = refs[2 + count : 6 + count]
    low_ref, dgate_ref, dup_ref, sums_ref = refs[-5 - count : -1 - count]
    out_refs = refs[-1 - count : -1]
    d_ffn = pick(refs[-1], refs[2 : 2 + count])
    step = pl.program_id(0)

    @pl.when(step == 0)
    def _():
        sums_ref[...] = jnp.zeros_like(sums_ref)

    gate, up, unit = gate_ref[0], up_ref[0], unit_ref[...]
    gain = ffn_ref[2:3, :]
    stats = stats_ref[0]
    mean = stats[:, 0:1] / FF
    inv = lax.rsqrt(stats[:, 1:2] / FF - mean * mean + EPS)
    first = stats[:, 2:3]
    second = inv * (stats[:, 3:4] - mean * first)
    sig = sigmoid(gate)
    silu = gate * sig
    unit_value = (silu * up - mean) * inv
    low_ref[0] = (unit * (unit_value * gain + ffn_ref[3:4, :])).astype(BF)
    d_hidden = unit * inv * (d_ffn * gain * unit - first / FF - unit_value * (second / FF))
    d_gate = (d_hidden * up * sig * (1.0 + gate * (1.0 - sig))).astype(BF)
    d_up = (d_hidden * silu).astype(BF)
    dgate_ref[0], dup_ref[0] = d_gate, d_up
    d_masked = d_ffn * unit
    sums_ref[0:1, :] += down_sum(d_gate.astype(F32))
    sums_ref[1:2, :] += down_sum(d_up.astype(F32))
    sums_ref[2:3, :] += down_sum(d_masked * unit_value)
    sums_ref[3:4, :] += down_sum(d_masked)
    out = lax.dot_general(d_gate, w_gu_ref[0], NT, preferred_element_type=F32)
    out += lax.dot_general(d_up, w_gu_ref[1], NT, preferred_element_type=F32)
    for at in range(count):

        @pl.when(step == at)
        def _():
            out_refs[at][...] = out.astype(BF)


def down_body(count, low_ref, w_ref, *out_refs):
    out = lax.dot_general(low_ref[0], w_ref[0], NT, preferred_element_type=F32)
    for at in range(count):

        @pl.when(pl.program_id(0) == at)
        def _():
            out_refs[at][...] = out.astype(BF)


def spread_back_body(count, place_ref, dq_ref, dk_ref, dv_ref, w_ref, *out_refs):
    out = lax.dot_general(dq_ref[...], w_ref[0], NT, preferred_element_type=F32)
    out += lax.dot_general(dk_ref[...], w_ref[1], NT, preferred_element_type=F32)
    out += lax.dot_general(dv_ref[...], w_ref[2], NT, preferred_element_type=F32)
    for at in range(count):

        @pl.when(pl.program_id(0) == at)
        def _():
            out_refs[at][...] = out.astype(BF)


def product_body(n_left, sizes, block, parity_ref, *refs):
    lefts, at = [], 0
    for count in n_left:
        lefts.append(jnp.concatenate([ref[...] for ref in refs[at : at + count]], axis=0))
        at += count
    rights = []
    for size in sizes:
        rights.append([ref[...] for ref in refs[at : at + size]])
        at += size
    w_refs = refs[at:-3] if len(refs) - at > 2 else []
    kept_ref, away_ref = refs[at + len(w_refs) : at + len(w_refs) + 2]
    parity = parity_ref[0]
    column, along = 0, 0.0
    for left, group in zip(lefts, rights):
        for right in group:
            out = lax.dot_general(left, right, TN, preferred_element_type=F32)
            width = right.shape[1]
            if w_refs and column < w_refs[0].shape[0] * w_refs[0].shape[2]:
                part = w_refs[0][column // width].astype(F32)
                along = along + jnp.sum(out * part, axis=1, keepdims=True)
            low = out.astype(BF)
            for pair in range(out.shape[0] // (2 * block)):
                first = low[2 * pair * block : (2 * pair + 1) * block]
                second = low[(2 * pair + 1) * block : (2 * pair + 2) * block]
                mine = jnp.where(parity == 0, first, second)
                other = jnp.where(parity == 0, second, first)
                kept_ref[pair, :, column : column + width] = mine
                away_ref[pair, :, column : column + width] = other
            column += width
    if w_refs:
        refs[-1][0] = along.reshape(1, along.shape[0])


def product(lefts, rights, parity, block, weights=None):
    width = lefts[0][0].shape[1]
    step = max(256, 2 * block)
    pairs = step // (2 * block)
    columns = sum(right.shape[1] for group in rights for right in group)
    args = [left for group in lefts for left in group]
    specs = [
        pl.BlockSpec((left.shape[0], step), lambda m, *_: (0, m)) for group in lefts for left in group
    ]
    for group in rights:
        args += group
        specs += [whole(right.shape) for right in group]
    outs = [sds((width // (2 * block), block, columns), BF)] * 2
    out_specs = [pl.BlockSpec((pairs, block, columns), lambda m, *_: (m, 0, 0))] * 2
    if weights is not None:
        args.append(weights)
        specs.append(
            pl.BlockSpec((weights.shape[0], step, weights.shape[2]), lambda m, *_: (0, m, 0))
        )
        outs.append(sds((width // step, 1, step), F32))
        out_specs.append(lead((1, step)))
    return call(
        functools.partial(
            product_body, [len(g) for g in lefts], [len(g) for g in rights], block
        ),
        (parity, *args),
        specs,
        outs,
        out_specs,
        (width // step,),
        prefetch=1,
        us=columns / 250,
    )


def add_terms(term_refs):
    total = term_refs[0][...].astype(F32)
    for ref in term_refs[1:]:
        total += ref[...].astype(F32)
    return total


def middle_back_body(count, *refs):
    upstream = add_terms(refs[:count])
    middle_ref, dy_ref, low_ref, keep_ref, mixed_ref, w_ref, norm_ref, head_ref = refs[
        count : count + 8
    ]
    dmid_ref, dbranch_ref, dmix_ref, sums_ref = refs[count + 8 :]
    middle = middle_ref[...]
    width = middle.shape[1]
    mean, inv = row_stats(middle, width)
    unit = (middle - mean) * inv
    d_middle = dy_ref[...].astype(F32) + rows_back(upstream, norm_ref[2:3, :], unit, inv, width)
    dmid_ref[...] = d_middle
    sums_ref[0:1, :] = down_sum(upstream * unit)
    sums_ref[1:2, :] = down_sum(upstream)
    d_branch = (keep_ref[...] * d_middle).astype(BF)
    dbranch_ref[...] = d_branch
    sums_ref[2:3, :] = down_sum(d_branch.astype(F32))
    sums_ref[3:4, :] = down_sum(low_ref[...].astype(F32))
    d_inner = jnp.dot(d_branch, w_ref[...], preferred_element_type=F32)
    mixed = mixed_rows(mixed_ref)
    mean, inv = row_stats(mixed, width)
    unit = (mixed - mean) * inv
    d_mixed = rows_back(d_inner, head_ref[2:3, :], unit, inv, width).astype(BF)
    part = mixed_ref.shape[2]
    for at in range(mixed_ref.shape[0]):
        dmix_ref[at] = d_mixed[:, at * part : (at + 1) * part]
    sums_ref[4:5, :] = down_sum(d_inner * unit)
    sums_ref[5:6, :] = down_sum(d_inner)
    sums_ref[6:8, :] = jnp.zeros((2, width), F32)


def first_back_body(count, *refs):
    upstream = add_terms(refs[:count])
    tokens_ref, dmid_ref, norm_ref, out_ref = refs[count:]
    rows = tokens_ref[...].astype(F32)
    length, width = rows.shape
    mean, inv = row_stats(rows, width)
    unit = (rows - mean) * inv
    d_in = rows_back(upstream[:length], norm_ref[0:1, :], unit, inv, width)
    out_ref[...] = dmid_ref[:length] + d_in


def layer_out_body(count, *refs):
    branch = add_terms(refs[:count])
    middle_ref, keep_ref, norm_ref, out_ref = refs[count:]
    out = middle_ref[...] + keep_ref[...] * (branch + norm_ref[5:6, :])
    out_ref[...] = out[: out_ref.shape[0]].astype(BF)


def rope_tables(coords):
    half_dim = HD // 2
    index_j = jnp.arange(half_dim // 2).astype(F32)
    frequency = jnp.repeat(jnp.exp(index_j * (-2.0 * math.log(10000.0) / half_dim)), 2)
    spots = jnp.arange(GRID_SIDE)
    angles = (spots.astype(F32) * 0.5)[:, None] * frequency
    lane_half = jnp.arange(LANES) // half_dim % 2
    tables = jnp.stack([jnp.cos(angles), jnp.sin(angles)])
    tables = jnp.tile(tables, (1, 1, LANES // half_dim))
    tables = jnp.concatenate([tables * (lane_half == half) for half in range(2)], axis=1)
    chosen = jnp.concatenate(
        [(coords[half][:, None] == spots).astype(F32) for half in range(2)], axis=1
    )
    both = jnp.dot(
        chosen,
        jnp.concatenate([tables[0], tables[1]], axis=1),
        precision=lax.Precision.HIGHEST,
    )
    return both[:, :LANES], both[:, LANES:]


def pad_to(value, axis, size):
    widths = [(0, 0)] * value.ndim
    widths[axis] = (0, size - value.shape[axis])
    return jnp.pad(value, widths)


def ceil_to(value, unit):
    return -(-value // unit) * unit


def on_device(
    n_dp,
    n_tp,
    tokens,
    cotangent,
    w_qkv,
    w_o,
    w_gu,
    w_down,
    norm_params,
    head_params,
    ffn_params,
    token_mask,
    empty_flag,
    coords,
):
    tp_index = lax.axis_index("tensor")
    own_rows, width = tokens.shape[1:]
    local = w_qkv.shape[2]
    units = w_gu.shape[2]
    heads = local // HD
    rows = ceil_to(own_rows, 16)
    seq = rows * n_tp
    lanes = ceil_to(units, LANES)
    step_rows, steps = seq, 1
    offsets = ring_offsets(n_tp)
    order = (jnp.array(offsets, jnp.int32) + tp_index) % n_tp
    place = {offset % n_tp: at for at, offset in enumerate(offsets)}
    own = whole((rows, width))

    normed = call(
        first_norm_body,
        (tokens[0], norm_params),
        [whole((own_rows, width)), whole(norm_params.shape)],
        [sds((rows, width), BF)],
        [own],
        (1,),
        us=1.2,
    )[0]
    normed_parts = ring_gather(normed, n_tp)

    ups = n_tp // 2
    arrivals = [[0]]
    for s in range(1, ups + 1):
        arrivals.append(sorted({place[-s % n_tp], place[s % n_tp]}))
    leaving = sorted({place[ups % n_tp], place[-1 % n_tp]})
    staying = [at for at in range(n_tp) if at not in leaving]
    leavings = [group for group in (leaving, staying) if group]

    slots = jnp.concatenate([token_mask, coords[0]], axis=0).reshape(3, n_tp, own_rows)
    slots = pad_to(slots, 2, rows)
    slots = jnp.stack(
        [lax.dynamic_index_in_dim(slots, order[at], 1, keepdims=False) for at in range(n_tp)], 1
    )
    mask = slots[0]
    bias = jnp.where(mask > 0, 0.0, -1e30).astype(F32)
    bias_row, bias_col = bias.reshape(1, seq), bias.reshape(seq, 1)
    keep = (mask[0].astype(F32) * (1.0 - empty_flag[0].astype(F32)))[:, None]
    cos_all, sin_all = rope_tables(slots[1:].reshape(2, seq))

    head_local = lax.dynamic_slice_in_dim(head_params, tp_index * local, local, 1)
    ffn_local = pad_to(
        lax.dynamic_slice_in_dim(ffn_params, tp_index * units, units, 1), 1, lanes
    )
    lane_at = jnp.arange(lanes)
    unit_row = ((lane_at < units) & (tp_index * units + lane_at < FF)).astype(F32)[None]

    tokens_own = pad_to(tokens[0], 0, rows)
    dy_own = pad_to(cotangent[0], 0, rows)
    d_low = (keep * dy_own.astype(F32)).astype(BF)

    w_order = dp_order(n_dp)
    full_qkv = put_back(w_order, dp_gather(w_qkv, n_dp), 1)
    filled = ()
    for turn, group in enumerate(arrivals):
        if turn > 1:
            normed_parts[group[0]] = after(normed_parts[group[0]], filled[0])
        filled = call(
            functools.partial(project_body, len(group)),
            (
                jnp.array(group, jnp.int32),
                *(normed_parts[at] for at in group),
                full_qkv,
                head_local,
                cos_all,
                sin_all,
            ),
            [own] * len(group)
            + [whole(full_qkv.shape), whole(head_local.shape)]
            + [pl.BlockSpec((rows, LANES), lambda s, place, *_: (place[s], 0))] * 2,
            [sds((n_tp, rows, local), BF)] * 3,
            [placed((rows, local))] * 3,
            (len(group),),
            scratch=[pltpu.VMEM((rows, width), BF)],
            prefetch=1,
            held=filled,
            us=2.0 * len(group),
        )
    query, key, value = (part.reshape(seq, local) for part in filled)
    d_low_late = after(d_low, normed_parts[-1], normed_parts[ups])
    d_low_first = [ring_up(d_low_late, n_tp), ring_down(d_low_late, n_tp)]
    strip = pl.BlockSpec((step_rows, local), lambda s, *_: (s, 0))
    mixed_heads, lse = call(
        attend_body,
        (order, query, key, value, bias_row),
        [strip, whole((seq, local)), whole((seq, local)), whole((1, seq))],
        [sds((n_tp, rows, local), BF), sds((steps, heads, step_rows), F32)],
        [whole((n_tp, rows, local)), lead((heads, step_rows))],
        (steps,),
        prefetch=1,
        us=10,
    )
    w_o_late = after(w_o, normed_parts[1])
    o_parts = call(
        lay_body,
        (order, *ring_gather(w_o_late, n_tp)),
        [whole(w_o.shape)] * n_tp,
        [sds((n_tp,) + w_o.shape[::-1], BF)],
        [whole((n_tp,) + w_o.shape[::-1])],
        (1,),
        prefetch=1,
        us=0.7,
    )[0]
    o_parts = jnp.concatenate([o_parts[at] for at in range(n_tp)], axis=1)
    full_o = put_back(w_order, dp_gather(o_parts, n_dp), 0)
    w_ffn = pad_to(jnp.concatenate([w_gu, w_down.T[None]], axis=0), 2, lanes)
    w_ffn = dp_gather(after(w_ffn, normed_parts[1]), n_dp)
    mixed_heads = after(mixed_heads, full_o, *d_low_first)
    mixed = lax.all_to_all(mixed_heads, "tensor", split_axis=0, concat_axis=0, tiled=True)

    inner_low, middle, normed_two = call(
        middle_body,
        (mixed, tokens_own, keep, full_o, norm_params, head_params),
        [
            whole(mixed.shape),
            own,
            whole((rows, 1)),
            whole(full_o.shape),
            whole(norm_params.shape),
            whole(head_params.shape),
        ],
        [sds((rows, width), BF), sds((rows, width), F32), sds((rows, width), BF)],
        [own] * 3,
        (1,),
        us=3,
    )
    two_parts = ring_gather(normed_two, n_tp)
    full_ffn = put_back(w_order, [after(part, normed_two) for part in w_ffn], 1)
    d_low_parts = gather_rest(d_low, d_low_first, n_tp, mixed)

    hidden_shape = (n_tp, rows, lanes)
    gu_block = pl.BlockSpec((2, width, lanes), lambda *_: (0, 0, 0))
    down_block = pl.BlockSpec((1, width, lanes), lambda *_: (2, 0, 0))
    d_ffn = [None] * n_tp
    near = [at for group in arrivals[:2] for at in group]
    for group in [near] + arrivals[2:]:
        outs = call(
            functools.partial(d_ffn_body, len(group)),
            (*(d_low_parts[at] for at in group), full_ffn),
            [own] * len(group) + [down_block],
            [sds((rows, lanes), F32)] * len(group),
            [whole((rows, lanes))] * len(group),
            (len(group),),
            scratch=[pltpu.VMEM((rows, width), BF)],
            us=1.4 * len(group),
        )
        for at, part in zip(group, outs):
            d_ffn[at] = part
    hidden_block = placed((rows, lanes))
    filled = ()
    for turn, group in enumerate(arrivals):
        if turn > 1:
            two_parts[group[0]] = after(two_parts[group[0]], filled[0])
        filled = call(
            functools.partial(ffn_body, len(group)),
            (
                jnp.array(group, jnp.int32),
                order,
                *(two_parts[at] for at in group),
                *(d_ffn[at] for at in group),
                full_ffn,
                ffn_local,
                unit_row,
            ),
            [own] * len(group)
            + [whole((rows, lanes))] * len(group)
            + [gu_block, whole(ffn_local.shape), whole(unit_row.shape)],
            [sds(hidden_shape, F32)] * 2 + [sds((n_tp, 4, rows), F32)],
            [hidden_block] * 2 + [ordered((4, rows))],
            (len(group),),
            scratch=[pltpu.VMEM((rows, width), BF), pltpu.VMEM((rows, lanes), F32)],
            prefetch=2,
            held=filled,
            us=1.2 + 2.2 * len(group),
        )
    gate, up, stats = filled
    stats = jnp.swapaxes(sum_shifts(stats, n_tp), 1, 2)
    filled, ffn_sums, d_two_parts = (), 0.0, [None] * n_tp
    for group in leavings:
        outs = call(
            functools.partial(ffn_back_body, len(group)),
            (
                jnp.array(group, jnp.int32),
                order,
                gate,
                up,
                *(d_ffn[at] for at in group),
                stats,
                full_ffn,
                ffn_local,
                unit_row,
            ),
            [hidden_block] * 2
            + [whole((rows, lanes))] * len(group)
            + [
                ordered((rows, 4)),
                gu_block,
                whole(ffn_local.shape),
                whole(unit_row.shape),
            ],
            [sds(hidden_shape, BF)] * 3
            + [sds((4, lanes), F32)]
            + [sds((rows, width), BF)] * len(group),
            [hidden_block] * 3 + [whole((4, lanes))] + [own] * len(group),
            (len(group),),
            scratch=[pltpu.VMEM((rows, lanes), F32)],
            prefetch=2,
            held=filled,
            us=3.7 * len(group),
        )
        filled = outs[:3]
        ffn_sums = ffn_sums + outs[3]
        for at, piece in zip(group, outs[4:]):
            d_two_parts[at] = piece
    ffn_low, d_gate, d_up = filled
    d_two_first = scatter_first(d_two_parts, n_tp)
    d_two_first = [after(d_two_first[0], *d_two_first[1:])] + d_two_first[1:]
    d_two_terms = scatter_rest(d_two_parts, d_two_first, n_tp)
    branch_parts = call(
        functools.partial(down_body, n_tp),
        (ffn_low, full_ffn),
        [lead((rows, lanes)), down_block],
        [sds((rows, width), BF)] * n_tp,
        [own] * n_tp,
        (n_tp,),
        us=2.8,
    )

    d_two_terms[0] = after(d_two_terms[0], *branch_parts)

    parity = (lax.axis_index("dp") % 2).astype(jnp.int32)[None]
    block = width // n_dp
    hidden_rows = [part.reshape(seq, lanes) for part in (d_gate, d_up, ffn_low)]
    grad_ffn = product([two_parts, d_low_parts], [hidden_rows[:2], hidden_rows[2:]], parity, block)
    grad_ffn = pair_sum(grad_ffn, n_dp)


    n_terms = len(d_two_terms)
    d_middle, d_branch, d_mixed_rows, mid_sums = call(
        functools.partial(middle_back_body, n_terms),
        (*d_two_terms, middle, dy_own, d_low, keep, mixed, full_o, norm_params, head_params),
        [own] * n_terms
        + [own] * 3
        + [
            whole((rows, 1)),
            whole(mixed.shape),
            whole(full_o.shape),
            whole(norm_params.shape),
            whole(head_params.shape),
        ],
        [
            sds((rows, width), F32),
            sds((rows, width), BF),
            sds((n_tp, rows, local), BF),
            sds((8, width), F32),
        ],
        [own, own, whole((n_tp, rows, local)), whole((8, width))],
        (1,),
        us=3.6,
    )
    d_mixed = lax.all_to_all(d_mixed_rows, "tensor", split_axis=0, concat_axis=0, tiled=True)
    d_mixed = after(d_mixed, grad_ffn)
    grad_ffn = dp_scatter(grad_ffn, n_dp)
    branch_parts = [after(part, d_mixed) for part in branch_parts]
    branch_first = scatter_first(branch_parts, n_tp)

    table = pl.BlockSpec((step_rows, LANES), lambda s, *_: (s, 0))
    all_rows = whole((seq, local))
    d_query, d_key, d_value, head_sums = call(
        attend_back_body,
        (
            order,
            query,
            d_mixed,
            lse,
            key,
            value,
            bias_col,
            cos_all,
            sin_all,
            cos_all,
            sin_all,
        ),
        [
            strip,
            whole(d_mixed.shape),
            lead((heads, step_rows)),
            all_rows,
            all_rows,
            whole((seq, 1)),
            table,
            table,
            whole((seq, LANES)),
            whole((seq, LANES)),
        ],
        [sds((seq, local), BF)] * 3 + [sds((8, local), F32)],
        [strip, all_rows, all_rows, whole((8, local))],
        (steps,),
        scratch=[pltpu.VMEM((seq, local), F32)] * 2,
        prefetch=1,
        us=24,
    )
    d_query = after(d_query, *branch_first)
    chunk = pl.BlockSpec((rows, local), lambda s, place, *_: (place[s], 0))
    d_one_parts = [None] * n_tp
    for group in leavings:
        outs = call(
            functools.partial(spread_back_body, len(group)),
            (jnp.array(group, jnp.int32), d_query, d_key, d_value, full_qkv),
            [chunk] * 3 + [whole(full_qkv.shape)],
            [sds((rows, width), BF)] * len(group),
            [own] * len(group),
            (len(group),),
            prefetch=1,
            us=1.0 * len(group),
        )
        for at, piece in zip(group, outs):
            d_one_parts[at] = piece
    d_proj = [after(part, *[d_one_parts[at] for at in leaving]) for part in (d_query, d_key, d_value)]
    *grad_late, along_normed = product(
        [normed_parts, [d_branch]], [d_proj, [inner_low]], parity, block, full_qkv
    )
    along_normed = along_normed.reshape(-1)
    shift_one = sum(
        jnp.sum(full_qkv[at].astype(F32) * head_sums[at : at + 1], axis=1) for at in range(3)
    )
    grad_late = pair_sum(grad_late, n_dp)

    d_one_first = scatter_first(d_one_parts, n_tp)
    arrived = [after(d_one_first[0], grad_late, grad_ffn)] + d_one_first[1:]
    sent = []
    d_one_terms = scatter_rest(d_one_parts, arrived, n_tp, sent)

    small = [along_normed, shift_one, mid_sums[:6].reshape(-1)]
    small += [head_sums[0], head_sums[2], ffn_sums[:, :units].reshape(-1)]
    small = jnp.concatenate(small)
    small_len = small.shape[0]
    small = pad_to(small, 0, ceil_to(small_len, 8 * LANES)).reshape(-1, LANES)
    small = sum_over(after(small, grad_ffn), "dp", n_dp)
    small_sum = small
    grad_late = dp_scatter(after(grad_late, small), n_dp)
    late_parts = grad_late
    small = after(small, *sent)
    small = [part.reshape(-1) for part in gather_small(small, n_tp)]
    head_at = 8 * width
    ffn_at = head_at + 2 * local
    norm_sums = sum_alike([part[:head_at] for part in small]).reshape(8, width)
    head_bias = jnp.zeros((2, width), F32)
    ffn_total = jnp.zeros((4, n_tp * units), F32)
    for s, part in enumerate(small):
        owner = (tp_index - s) % n_tp
        head_bias = lax.dynamic_update_slice(
            head_bias, part[head_at:ffn_at].reshape(2, local), (0, owner * local)
        )
        ffn_total = lax.dynamic_update_slice(
            ffn_total, part[ffn_at:small_len].reshape(4, units), (0, owner * units)
        )
    gain_one = (norm_sums[0:1] - norm_params[1:2] * norm_sums[1:2]) / norm_params[0:1]
    norm_total = jnp.concatenate([gain_one, norm_sums[1:6]], axis=0)
    head_total = jnp.concatenate([head_bias, norm_sums[6:8]], axis=0)

    grad_early = sum_parts(grad_ffn)
    grad_late = sum_parts(grad_late)
    grad_o = grad_late[:, 3 * local :].astype(BF).reshape(-1, n_tp, local).swapaxes(0, 1)
    grad_o = swap_sum(grad_o, n_tp).T
    grad_gu = jnp.stack([grad_early[:, :units], grad_early[:, lanes : lanes + units]])
    grad_down = grad_early[:, 2 * lanes : 2 * lanes + units].T
    grad_qkv = grad_late[:, : 3 * local].reshape(-1, 3, local).swapaxes(0, 1)

    branch_first = [after(branch_first[0], small_sum)] + branch_first[1:]
    branch_terms = scatter_rest(branch_parts, branch_first, n_tp)
    branch_terms[1] = after(branch_terms[1], late_parts)
    layer_out = call(
        functools.partial(layer_out_body, n_terms),
        (*branch_terms, middle, keep, norm_params),
        [own] * n_terms + [own, whole((rows, 1)), whole(norm_params.shape)],
        [sds((own_rows, width), BF)],
        [whole((own_rows, width))],
        (1,),
        us=2,
    )[0]
    d_one_terms[0] = after(d_one_terms[0], grad_late, norm_total, ffn_total)
    d_tokens = call(
        functools.partial(first_back_body, n_terms),
        (*d_one_terms, tokens[0], d_middle, norm_params),
        [own] * n_terms + [whole((own_rows, width)), own, whole(norm_params.shape)],
        [sds((own_rows, width), F32)],
        [whole((own_rows, width))],
        (1,),
        us=1.5,
    )[0]

    return (
        layer_out[None],
        d_tokens[None],
        grad_qkv,
        grad_o,
        grad_gu,
        grad_down,
        norm_total,
        head_total,
        ffn_total,
    )


def solution(mesh):
    placed = (
        P("dp", "tensor", None),
        P("dp", "tensor", None),
        P(None, "dp", "tensor"),
        P("tensor", "dp"),
        P(None, "dp", "tensor"),
        P("tensor", "dp"),
        P(),
        P(),
        P(),
        P("dp", None),
        P("dp"),
        P("dp", None, None),
    )
    return jax.shard_map(
        functools.partial(on_device, mesh.shape["dp"], mesh.shape["tensor"]),
        mesh=mesh,
        in_specs=placed,
        out_specs=(
            P("dp", "tensor", None),
            P("dp", "tensor", None),
            P(None, "dp", "tensor"),
            P("tensor", "dp"),
            P(None, "dp", "tensor"),
            P("tensor", "dp"),
            P(),
            P(),
            P(),
        ),
        check_vma=False,
    )
```

```python
import functools
import math

import jax
import jax.numpy as jnp
from jax import lax
from jax.experimental import pallas as pl
from jax.experimental.pallas import tpu as pltpu
from jax.sharding import PartitionSpec as P

FF = 2730
HD = 64
FF_PAD = 2736
GRID_SIDE = 32
LANES = 128
EPS = 1e-06
VMEM_LIMIT = 44 * 2**20
COST_SCALE = 4.0
BF = jnp.bfloat16
F32 = jnp.float32
NT = (((1,), (1,)), ((), ()))
TN = (((0,), (0,)), ((), ()))


def ring_up(value, size):
    return lax.ppermute(value, "tensor", [(j, (j + 1) % size) for j in range(size)])


def ring_down(value, size):
    return lax.ppermute(value, "tensor", [(j, (j - 1) % size) for j in range(size)])


def ring_offsets(size):
    ups = size // 2
    return [0] + [-s for s in range(1, ups + 1)] + [s for s in range(1, size - ups)]


def gather_rest(own, first, size, late=None):
    ups = size // 2
    downs = size - 1 - ups
    upper, lower = first[:1], first[1:]
    for s in range(1, ups):
        up_now = upper[-1] if late is None else after(upper[-1], late)
        upper.append(ring_up(up_now, size))
        if s < downs:
            down_now = lower[-1] if late is None else after(lower[-1], late)
            lower.append(ring_down(down_now, size))
    return [own] + upper + lower


def ring_gather(own, size):
    return gather_rest(own, [ring_up(own, size), ring_down(own, size)], size)


def after(value, *others):
    return lax.optimization_barrier((value,) + others)[0]


def sum_shifts(value, size):
    total = value
    for s in range(1, size):
        total = total + lax.ppermute(
            value, "tensor", [(j, (j + s) % size) for j in range(size)]
        )
    return total


def gather_small(value, size):
    return [value] + [
        lax.ppermute(value, "tensor", [(j, (j + s) % size) for j in range(size)])
        for s in range(1, size)
    ]


def sum_alike(terms):
    while len(terms) > 1 and len(terms) % 2 == 0:
        half = len(terms) // 2
        terms = [terms[s] + terms[s + half] for s in range(half)]
    return functools.reduce(jnp.add, terms)


def swap_sum(blocks, size):
    index = lax.axis_index("tensor")

    def block_for(s):
        return lax.dynamic_index_in_dim(blocks, (index + s) % size, 0, keepdims=False)

    total = block_for(0).astype(F32)
    for s in range(1, size):
        came = lax.ppermute(block_for(s), "tensor", [(j, (j + s) % size) for j in range(size)])
        total = total + came.astype(F32)
    return total


def add_low(left, right):
    return (left.astype(F32) + right.astype(F32)).astype(BF)


def scatter_first(pieces, size):
    place = {offset % size: at for at, offset in enumerate(ring_offsets(size))}
    ups = size // 2
    arrived = []
    if size > 1:
        arrived.append(ring_up(pieces[place[ups % size]], size))
    if ups == size - 1 - ups:
        arrived.append(ring_down(pieces[place[-ups % size]], size))
    elif size > 2:
        arrived.append(ring_down(pieces[place[(1 - ups) % size]], size))
    return arrived


def scatter_rest(pieces, arrived, size, sent=None):
    place = {offset % size: at for at, offset in enumerate(ring_offsets(size))}
    ups = size // 2
    downs = size - 1 - ups
    up_now = arrived[0]
    for s in range(ups - 1, 0, -1):
        up_now = add_low(up_now, pieces[place[s]])
        if sent is not None:
            sent.append(up_now)
        up_now = ring_up(up_now, size)
    terms = [pieces[0], up_now]
    if downs:
        down_now = arrived[1]
        for s in range(downs - 1, 0, -1):
            down_now = ring_down(add_low(down_now, pieces[place[-s % size]]), size)
        terms.append(down_now)
    return terms


def dp_bits(size):
    bits = []
    step = 2
    while step < size:
        bits.append(step)
        step *= 2
    return bits + ([1] if size > 1 else [])


def flip(value, bit, size):
    return lax.ppermute(value, "dp", [(j, j ^ bit) for j in range(size)])


def dp_gather(block, size, late=None):
    stacked = block[None]
    bits = dp_bits(size)
    for bit in bits[:-1]:
        other = flip(stacked, bit, size)
        if late is not None and bit == bits[-2]:
            other = after(other, late)
        stacked = jnp.concatenate([stacked, other], axis=0)
    return [stacked] + [flip(stacked, bit, size) for bit in bits[-1:]]


def dp_order(size):
    order = [0]
    for bit in dp_bits(size):
        order = order + [at ^ bit for at in order]
    return jnp.array(order, jnp.int32) ^ lax.axis_index("dp")


def pair_sum(halves, size):
    kept, away = halves
    return add_low(kept, flip(away, 1, size))


def dp_scatter(merged, size):
    groups = [[j for j in range(size) if j % 2 == c] for c in range(2)]
    return lax.all_to_all(
        merged, "dp", split_axis=0, concat_axis=0, tiled=True, axis_index_groups=groups
    )


def sum_parts(parts):
    return jnp.sum(parts.astype(F32), axis=0)


def sum_over(value, axis, size):
    copies = jnp.broadcast_to(value[None], (size,) + value.shape)
    return jnp.sum(lax.all_to_all(copies, axis, split_axis=0, concat_axis=0, tiled=True), axis=0)


def whole(shape):
    return pl.BlockSpec(shape, lambda *_: (0,) * len(shape))


def lead(shape):
    return pl.BlockSpec((1,) + shape, lambda s, *_: (s,) + (0,) * len(shape))


def placed(shape):
    return pl.BlockSpec((1,) + shape, lambda s, place, *_: (place[s],) + (0,) * len(shape))


def ordered(shape):
    return pl.BlockSpec(
        (1,) + shape, lambda s, place, order: (order[place[s]],) + (0,) * len(shape)
    )


def call(
    body, args, specs, outs, out_specs, grid, scratch=(), prefetch=0, held=(), us=1.0
):
    first_held = len(args)
    args = tuple(args) + tuple(held)
    specs = list(specs) + [pl.BlockSpec(memory_space=pl.ANY)] * len(held)
    return pl.pallas_call(
        body,
        out_shape=outs,
        grid_spec=pltpu.PrefetchScalarGridSpec(
            num_scalar_prefetch=prefetch,
            grid=grid,
            in_specs=specs,
            out_specs=out_specs,
            scratch_shapes=list(scratch),
        ),
        input_output_aliases={first_held + at: at for at in range(len(held))},
        compiler_params=pltpu.CompilerParams(vmem_limit_bytes=VMEM_LIMIT),
        cost_estimate=pl.CostEstimate(
            flops=int(us * COST_SCALE * 1e9), bytes_accessed=1, transcendentals=0
        ),
    )(*args)


def sds(shape, dtype):
    return jax.ShapeDtypeStruct(shape, dtype)


def row_stats(rows, count):
    mean = jnp.sum(rows, axis=1, keepdims=True) / count
    power = jnp.sum(rows * rows, axis=1, keepdims=True) / count
    return mean, lax.rsqrt(power - mean * mean + EPS)


def rows_back(upstream, gain, unit, inv, count):
    scaled = upstream * gain
    first = jnp.sum(scaled, axis=1, keepdims=True) / count
    second = jnp.sum(scaled * unit, axis=1, keepdims=True) / count
    return inv * (scaled - first - unit * second)


def down_sum(rows):
    return jnp.sum(rows, axis=0, keepdims=True)


def put_back_body(count, near, *refs):
    in_refs, out_ref = refs[1:-1], refs[-1]
    for at in range(count):

        @pl.when(pl.program_id(0) // near == at)
        def _():
            out_ref[...] = in_refs[at][(0,) * (len(in_refs[at].shape) - len(out_ref.shape))]


def put_back(order, stacks, axis):
    count, near, block = len(stacks), stacks[0].shape[0], stacks[0].shape[1:]
    size = count * near
    shape = tuple(n * size if at == axis else n for at, n in enumerate(block))
    if block[axis] % (LANES if axis == len(block) - 1 else 16):
        stacked = jnp.concatenate(stacks, axis=0)
        placed = jnp.zeros_like(stacked).at[order].set(stacked)
        return jnp.moveaxis(placed, 0, axis).reshape(shape)

    def taken(at):
        return pl.BlockSpec(
            (1,) + block,
            lambda r, order: (jnp.clip(r - at * near, 0, near - 1),) + (0,) * len(block),
        )

    return call(
        functools.partial(put_back_body, count, near),
        (order, *stacks),
        [taken(at) for at in range(count)],
        [sds(shape, stacks[0].dtype)],
        [
            pl.BlockSpec(
                block,
                lambda r, order: tuple(order[r] if at == axis else 0 for at in range(len(block))),
            )
        ],
        (size,),
        prefetch=1,
        us=size * math.prod(block) / 2**19,
    )[0]


def first_norm_body(tokens_ref, norm_ref, normed_ref):
    rows = tokens_ref[...].astype(F32)
    length, width = rows.shape
    mean, inv = row_stats(rows, width)
    normed_ref[:length] = ((rows - mean) * inv * norm_ref[0:1, :] + norm_ref[1:2, :]).astype(BF)
    normed_ref[length:] = jnp.zeros((normed_ref.shape[0] - length, width), BF)


def lay_body(order_ref, *refs):
    out_ref = refs[-1]
    for at, ref in enumerate(refs[:-1]):
        piece = ref[...].astype(F32).T.astype(BF)
        out_ref[order_ref[at]] = piece


def spread(table, width):
    return table if width == LANES else jnp.concatenate([table] * (width // LANES), axis=1)


def turn_pairs(rows):
    width = rows.shape[1]
    even = lax.broadcasted_iota(jnp.int32, (1, width), 1) % 2 == 0
    return jnp.where(even, -pltpu.roll(rows, width - 1, 1), pltpu.roll(rows, 1, 1))


def pick(held, chunk_refs):
    for at, ref in enumerate(chunk_refs):

        @pl.when(pl.program_id(0) == at)
        def _():
            held[...] = ref[...]

    return held[...]


def project_body(count, place_ref, *refs):
    chunk_refs = refs[:count]
    w_ref, head_ref, cos_ref, sin_ref = refs[count : count + 4]
    q_ref, k_ref, v_ref, held = refs[-4:]
    rows = pick(held, chunk_refs)
    width = w_ref.shape[2]
    cosine, sine = spread(cos_ref[...], width), spread(sin_ref[...], width)
    query = jnp.dot(rows, w_ref[0], preferred_element_type=F32) + head_ref[0:1, :]
    key = jnp.dot(rows, w_ref[1], preferred_element_type=F32)
    value = jnp.dot(rows, w_ref[2], preferred_element_type=F32) + head_ref[1:2, :]
    query_low = (query * cosine + turn_pairs(query) * sine).astype(BF)
    q_ref[0] = (query_low.astype(F32) * HD ** (-0.5)).astype(BF)
    k_ref[0] = (key * cosine + turn_pairs(key) * sine).astype(BF)
    v_ref[0] = value.astype(BF)


def head_lanes(width, head):
    lane = lax.broadcasted_iota(jnp.int32, (1, width), 1)
    return (lane >= head * HD) & (lane < (head + 1) * HD)


def attend_body(order_ref, q_ref, k_ref, v_ref, bias_ref, mixed_ref, lse_ref):
    query, keys, values, bias = q_ref[...], k_ref[...], v_ref[...], bias_ref[...]
    length, width = query.shape
    total = jnp.zeros((length, width), F32)
    for head in range(width // HD):
        mine = head_lanes(width, head)
        query_h = jnp.where(mine, query, jnp.zeros_like(query))
        scores = lax.dot_general(query_h, keys, NT, preferred_element_type=F32) + bias
        row_max = jnp.max(scores, axis=1, keepdims=True)
        exp_score = jnp.exp(scores - row_max)
        row_total = jnp.sum(exp_score, axis=1, keepdims=True)
        out = jnp.dot(exp_score.astype(BF), values, preferred_element_type=F32)
        total = jnp.where(mine, out * (1.0 / row_total), total)
        lse_ref[0, head : head + 1, :] = (row_max + jnp.log(row_total)).reshape(1, length)
    rows = mixed_ref.shape[1]
    for part in range(length // rows):
        at = order_ref[pl.program_id(0) * (length // rows) + part]
        mixed_ref[at] = total[part * rows : (part + 1) * rows].astype(BF)


def attend_back_body(
    order_ref,
    q_ref,
    dmix_ref,
    lse_ref,
    k_ref,
    v_ref,
    bias_ref,
    cos_ref,
    sin_ref,
    coss_ref,
    sins_ref,
    dq_ref,
    dk_ref,
    dv_ref,
    sums_ref,
    dk_sum,
    dv_sum,
):
    step = pl.program_id(0)

    @pl.when(step == 0)
    def _():
        dk_sum[...] = jnp.zeros_like(dk_sum)
        dv_sum[...] = jnp.zeros_like(dv_sum)
        sums_ref[...] = jnp.zeros_like(sums_ref)

    query, keys, values, bias = q_ref[...], k_ref[...], v_ref[...], bias_ref[...]
    length, width = query.shape
    rows = dmix_ref.shape[1]
    parts = length // rows
    d_mixed = jnp.concatenate([dmix_ref[order_ref[step * parts + p]] for p in range(parts)], axis=0)
    total = jnp.zeros((length, width), F32)
    for head in range(width // HD):
        mine = head_lanes(width, head)
        zero = jnp.zeros_like(query)
        query_h, d_mixed_h = jnp.where(mine, query, zero), jnp.where(mine, d_mixed, zero)
        scores = lax.dot_general(keys, query_h, NT, preferred_element_type=F32) + bias
        probs = jnp.exp(scores - lse_ref[0, head : head + 1, :])
        d_probs = lax.dot_general(values, d_mixed_h, NT, preferred_element_type=F32)
        d_scores = (probs * (d_probs - down_sum(probs * d_probs))).astype(BF)
        dv_sum[...] += jnp.dot(probs.astype(BF), d_mixed_h, preferred_element_type=F32)
        dk_sum[...] += jnp.dot(d_scores, query_h, preferred_element_type=F32)
        d_query = lax.dot_general(d_scores, keys, TN, preferred_element_type=F32)
        total = jnp.where(mine, d_query, total)
    total = total * HD ** (-0.5)
    cosine, sine = spread(cos_ref[...], width), spread(sin_ref[...], width)
    d_query_pre = (total * cosine - turn_pairs(total) * sine).astype(BF)
    dq_ref[...] = d_query_pre
    sums_ref[0:1, :] += down_sum(d_query_pre.astype(F32))

    @pl.when(step == pl.num_programs(0) - 1)
    def _():
        d_key = dk_sum[...]
        all_cos, all_sin = spread(coss_ref[...], width), spread(sins_ref[...], width)
        d_key_pre = (d_key * all_cos - turn_pairs(d_key) * all_sin).astype(BF)
        dk_ref[...] = d_key_pre
        sums_ref[1:2, :] = down_sum(d_key_pre.astype(F32))
        d_value_pre = dv_sum[...].astype(BF)
        dv_ref[...] = d_value_pre
        sums_ref[2:3, :] = down_sum(d_value_pre.astype(F32))


def mixed_rows(mixed_ref):
    parts = mixed_ref.shape[0]
    return jnp.concatenate([mixed_ref[p] for p in range(parts)], axis=1).astype(F32)


def middle_body(
    mixed_ref, tokens_ref, keep_ref, w_ref, norm_ref, head_ref, inner_ref, middle_ref, normed_ref
):
    mixed = mixed_rows(mixed_ref)
    mean, inv = row_stats(mixed, mixed.shape[1])
    inner = ((mixed - mean) * inv * head_ref[2:3, :] + head_ref[3:4, :]).astype(BF)
    inner_ref[...] = inner
    branch = lax.dot_general(inner, w_ref[...], NT, preferred_element_type=F32)
    branch += norm_ref[4:5, :]
    middle = tokens_ref[...].astype(F32) + keep_ref[...] * branch
    middle_ref[...] = middle
    mean, inv = row_stats(middle, middle.shape[1])
    normed_ref[...] = ((middle - mean) * inv * norm_ref[2:3, :] + norm_ref[3:4, :]).astype(BF)


def sigmoid(gate):
    return 1.0 / (1.0 + jnp.exp(-gate))


def d_ffn_body(count, *refs):
    w_ref, out_refs, held = refs[count], refs[count + 1 : -1], refs[-1]
    out = jnp.dot(pick(held, refs[:count]), w_ref[0], preferred_element_type=F32)
    for at in range(count):

        @pl.when(pl.program_id(0) == at)
        def _():
            out_refs[at][...] = out


def ffn_body(count, place_ref, order_ref, *refs):
    w_gu_ref, ffn_ref, unit_ref = refs[2 * count : 2 * count + 3]
    gate_ref, up_ref, stats_ref, held, d_held = refs[-5:]
    rows = pick(held, refs[:count])
    d_ffn = pick(d_held, refs[count : 2 * count])
    gate = jnp.dot(rows, w_gu_ref[0], preferred_element_type=F32) + ffn_ref[0:1, :]
    up = jnp.dot(rows, w_gu_ref[1], preferred_element_type=F32) + ffn_ref[1:2, :]
    gate_ref[0], up_ref[0] = gate, up
    unit = unit_ref[...]
    hidden = gate * sigmoid(gate) * up
    masked = hidden * unit
    scaled = d_ffn * ffn_ref[2:3, :] * unit
    length = rows.shape[0]
    for at, term in enumerate((masked, masked * hidden, scaled, scaled * hidden)):
        stats_ref[0, at : at + 1, :] = jnp.sum(term, axis=1, keepdims=True).reshape(1, length)
    stats_ref[0, 4:8, :] = jnp.zeros((4, length), F32)


def ffn_back_body(count, place_ref, order_ref, *refs):
    gate_ref, up_ref = refs[:2]
    stats_ref, w_gu_ref, ffn_ref, unit_ref = refs[2 + count : 6 + count]
    low_ref, dgate_ref, dup_ref, sums_ref = refs[-5 - count : -1 - count]
    out_refs = refs[-1 - count : -1]
    d_ffn = pick(refs[-1], refs[2 : 2 + count])
    step = pl.program_id(0)

    @pl.when(step == 0)
    def _():
        sums_ref[...] = jnp.zeros_like(sums_ref)

    gate, up, unit = gate_ref[0], up_ref[0], unit_ref[...]
    gain = ffn_ref[2:3, :]
    stats = stats_ref[0]
    mean = stats[:, 0:1] / FF
    inv = lax.rsqrt(stats[:, 1:2] / FF - mean * mean + EPS)
    first = stats[:, 2:3]
    second = inv * (stats[:, 3:4] - mean * first)
    sig = sigmoid(gate)
    silu = gate * sig
    unit_value = (silu * up - mean) * inv
    low_ref[0] = (unit * (unit_value * gain + ffn_ref[3:4, :])).astype(BF)
    d_hidden = unit * inv * (d_ffn * gain * unit - first / FF - unit_value * (second / FF))
    d_gate = (d_hidden * up * sig * (1.0 + gate * (1.0 - sig))).astype(BF)
    d_up = (d_hidden * silu).astype(BF)
    dgate_ref[0], dup_ref[0] = d_gate, d_up
    d_masked = d_ffn * unit
    sums_ref[0:1, :] += down_sum(d_gate.astype(F32))
    sums_ref[1:2, :] += down_sum(d_up.astype(F32))
    sums_ref[2:3, :] += down_sum(d_masked * unit_value)
    sums_ref[3:4, :] += down_sum(d_masked)
    out = lax.dot_general(d_gate, w_gu_ref[0], NT, preferred_element_type=F32)
    out += lax.dot_general(d_up, w_gu_ref[1], NT, preferred_element_type=F32)
    for at in range(count):

        @pl.when(step == at)
        def _():
            out_refs[at][...] = out.astype(BF)


def down_body(count, low_ref, w_ref, *out_refs):
    out = lax.dot_general(low_ref[0], w_ref[0], NT, preferred_element_type=F32)
    for at in range(count):

        @pl.when(pl.program_id(0) == at)
        def _():
            out_refs[at][...] = out.astype(BF)


def spread_back_body(count, place_ref, dq_ref, dk_ref, dv_ref, w_ref, *out_refs):
    out = lax.dot_general(dq_ref[...], w_ref[0], NT, preferred_element_type=F32)
    out += lax.dot_general(dk_ref[...], w_ref[1], NT, preferred_element_type=F32)
    out += lax.dot_general(dv_ref[...], w_ref[2], NT, preferred_element_type=F32)
    for at in range(count):

        @pl.when(pl.program_id(0) == at)
        def _():
            out_refs[at][...] = out.astype(BF)


def product_body(n_left, sizes, block, parity_ref, *refs):
    lefts, at = [], 0
    for count in n_left:
        lefts.append(jnp.concatenate([ref[...] for ref in refs[at : at + count]], axis=0))
        at += count
    rights = []
    for size in sizes:
        rights.append([ref[...] for ref in refs[at : at + size]])
        at += size
    w_refs = refs[at:-3] if len(refs) - at > 2 else []
    kept_ref, away_ref = refs[at + len(w_refs) : at + len(w_refs) + 2]
    parity = parity_ref[0]
    column, along = 0, 0.0
    for left, group in zip(lefts, rights):
        for right in group:
            out = lax.dot_general(left, right, TN, preferred_element_type=F32)
            width = right.shape[1]
            if w_refs and column < w_refs[0].shape[0] * w_refs[0].shape[2]:
                part = w_refs[0][column // width].astype(F32)
                along = along + jnp.sum(out * part, axis=1, keepdims=True)
            low = out.astype(BF)
            for pair in range(out.shape[0] // (2 * block)):
                first = low[2 * pair * block : (2 * pair + 1) * block]
                second = low[(2 * pair + 1) * block : (2 * pair + 2) * block]
                mine = jnp.where(parity == 0, first, second)
                other = jnp.where(parity == 0, second, first)
                kept_ref[pair, :, column : column + width] = mine
                away_ref[pair, :, column : column + width] = other
            column += width
    if w_refs:
        refs[-1][0] = along.reshape(1, along.shape[0])


def product(lefts, rights, parity, block, weights=None):
    width = lefts[0][0].shape[1]
    step = max(256, 2 * block)
    pairs = step // (2 * block)
    columns = sum(right.shape[1] for group in rights for right in group)
    args = [left for group in lefts for left in group]
    specs = [
        pl.BlockSpec((left.shape[0], step), lambda m, *_: (0, m)) for group in lefts for left in group
    ]
    for group in rights:
        args += group
        specs += [whole(right.shape) for right in group]
    outs = [sds((width // (2 * block), block, columns), BF)] * 2
    out_specs = [pl.BlockSpec((pairs, block, columns), lambda m, *_: (m, 0, 0))] * 2
    if weights is not None:
        args.append(weights)
        specs.append(
            pl.BlockSpec((weights.shape[0], step, weights.shape[2]), lambda m, *_: (0, m, 0))
        )
        outs.append(sds((width // step, 1, step), F32))
        out_specs.append(lead((1, step)))
    return call(
        functools.partial(
            product_body, [len(g) for g in lefts], [len(g) for g in rights], block
        ),
        (parity, *args),
        specs,
        outs,
        out_specs,
        (width // step,),
        prefetch=1,
        us=columns / 250,
    )


def add_terms(term_refs):
    total = term_refs[0][...].astype(F32)
    for ref in term_refs[1:]:
        total += ref[...].astype(F32)
    return total


def middle_back_body(count, *refs):
    upstream = add_terms(refs[:count])
    middle_ref, dy_ref, low_ref, keep_ref, mixed_ref, w_ref, norm_ref, head_ref = refs[
        count : count + 8
    ]
    dmid_ref, dbranch_ref, dmix_ref, sums_ref = refs[count + 8 :]
    middle = middle_ref[...]
    width = middle.shape[1]
    mean, inv = row_stats(middle, width)
    unit = (middle - mean) * inv
    d_middle = dy_ref[...].astype(F32) + rows_back(upstream, norm_ref[2:3, :], unit, inv, width)
    dmid_ref[...] = d_middle
    sums_ref[0:1, :] = down_sum(upstream * unit)
    sums_ref[1:2, :] = down_sum(upstream)
    d_branch = (keep_ref[...] * d_middle).astype(BF)
    dbranch_ref[...] = d_branch
    sums_ref[2:3, :] = down_sum(d_branch.astype(F32))
    sums_ref[3:4, :] = down_sum(low_ref[...].astype(F32))
    d_inner = jnp.dot(d_branch, w_ref[...], preferred_element_type=F32)
    mixed = mixed_rows(mixed_ref)
    mean, inv = row_stats(mixed, width)
    unit = (mixed - mean) * inv
    d_mixed = rows_back(d_inner, head_ref[2:3, :], unit, inv, width).astype(BF)
    part = mixed_ref.shape[2]
    for at in range(mixed_ref.shape[0]):
        dmix_ref[at] = d_mixed[:, at * part : (at + 1) * part]
    sums_ref[4:5, :] = down_sum(d_inner * unit)
    sums_ref[5:6, :] = down_sum(d_inner)
    sums_ref[6:8, :] = jnp.zeros((2, width), F32)


def first_back_body(count, *refs):
    upstream = add_terms(refs[:count])
    tokens_ref, dmid_ref, norm_ref, out_ref = refs[count:]
    rows = tokens_ref[...].astype(F32)
    length, width = rows.shape
    mean, inv = row_stats(rows, width)
    unit = (rows - mean) * inv
    d_in = rows_back(upstream[:length], norm_ref[0:1, :], unit, inv, width)
    out_ref[...] = dmid_ref[:length] + d_in


def layer_out_body(count, *refs):
    branch = add_terms(refs[:count])
    middle_ref, keep_ref, norm_ref, out_ref = refs[count:]
    out = middle_ref[...] + keep_ref[...] * (branch + norm_ref[5:6, :])
    out_ref[...] = out[: out_ref.shape[0]].astype(BF)


def rope_tables(coords):
    half_dim = HD // 2
    index_j = jnp.arange(half_dim // 2).astype(F32)
    frequency = jnp.repeat(jnp.exp(index_j * (-2.0 * math.log(10000.0) / half_dim)), 2)
    spots = jnp.arange(GRID_SIDE)
    angles = (spots.astype(F32) * 0.5)[:, None] * frequency
    lane_half = jnp.arange(LANES) // half_dim % 2
    tables = jnp.stack([jnp.cos(angles), jnp.sin(angles)])
    tables = jnp.tile(tables, (1, 1, LANES // half_dim))
    tables = jnp.concatenate([tables * (lane_half == half) for half in range(2)], axis=1)
    chosen = jnp.concatenate(
        [(coords[half][:, None] == spots).astype(F32) for half in range(2)], axis=1
    )
    both = jnp.dot(
        chosen,
        jnp.concatenate([tables[0], tables[1]], axis=1),
        precision=lax.Precision.HIGHEST,
    )
    return both[:, :LANES], both[:, LANES:]


def pad_to(value, axis, size):
    widths = [(0, 0)] * value.ndim
    widths[axis] = (0, size - value.shape[axis])
    return jnp.pad(value, widths)


def ceil_to(value, unit):
    return -(-value // unit) * unit


def on_device(
    n_dp,
    n_tp,
    tokens,
    cotangent,
    w_qkv,
    w_o,
    w_gu,
    w_down,
    norm_params,
    head_params,
    ffn_params,
    token_mask,
    empty_flag,
    coords,
):
    tp_index = lax.axis_index("tensor")
    own_rows, width = tokens.shape[1:]
    local = w_qkv.shape[2]
    units = w_gu.shape[2]
    heads = local // HD
    rows = ceil_to(own_rows, 16)
    seq = rows * n_tp
    lanes = ceil_to(units, LANES)
    step_rows, steps = seq, 1
    offsets = ring_offsets(n_tp)
    order = (jnp.array(offsets, jnp.int32) + tp_index) % n_tp
    place = {offset % n_tp: at for at, offset in enumerate(offsets)}
    own = whole((rows, width))

    normed = call(
        first_norm_body,
        (tokens[0], norm_params),
        [whole((own_rows, width)), whole(norm_params.shape)],
        [sds((rows, width), BF)],
        [own],
        (1,),
        us=1.2,
    )[0]
    normed_parts = ring_gather(normed, n_tp)

    ups = n_tp // 2
    arrivals = [[0]]
    for s in range(1, ups + 1):
        arrivals.append(sorted({place[-s % n_tp], place[s % n_tp]}))
    leaving = sorted({place[ups % n_tp], place[-1 % n_tp]})
    staying = [at for at in range(n_tp) if at not in leaving]
    leavings = [group for group in (leaving, staying) if group]

    slots = jnp.concatenate([token_mask, coords[0]], axis=0).reshape(3, n_tp, own_rows)
    slots = pad_to(slots, 2, rows)
    slots = jnp.stack(
        [lax.dynamic_index_in_dim(slots, order[at], 1, keepdims=False) for at in range(n_tp)], 1
    )
    mask = slots[0]
    bias = jnp.where(mask > 0, 0.0, -1e30).astype(F32)
    bias_row, bias_col = bias.reshape(1, seq), bias.reshape(seq, 1)
    keep = (mask[0].astype(F32) * (1.0 - empty_flag[0].astype(F32)))[:, None]
    cos_all, sin_all = rope_tables(slots[1:].reshape(2, seq))

    head_local = lax.dynamic_slice_in_dim(head_params, tp_index * local, local, 1)
    ffn_local = pad_to(
        lax.dynamic_slice_in_dim(ffn_params, tp_index * units, units, 1), 1, lanes
    )
    lane_at = jnp.arange(lanes)
    unit_row = ((lane_at < units) & (tp_index * units + lane_at < FF)).astype(F32)[None]

    tokens_own = pad_to(tokens[0], 0, rows)
    dy_own = pad_to(cotangent[0], 0, rows)
    d_low = (keep * dy_own.astype(F32)).astype(BF)

    w_order = dp_order(n_dp)
    full_qkv = put_back(w_order, dp_gather(w_qkv, n_dp), 1)
    filled = ()
    for turn, group in enumerate(arrivals):
        if turn > 1:
            normed_parts[group[0]] = after(normed_parts[group[0]], filled[0])
        filled = call(
            functools.partial(project_body, len(group)),
            (
                jnp.array(group, jnp.int32),
                *(normed_parts[at] for at in group),
                full_qkv,
                head_local,
                cos_all,
                sin_all,
            ),
            [own] * len(group)
            + [whole(full_qkv.shape), whole(head_local.shape)]
            + [pl.BlockSpec((rows, LANES), lambda s, place, *_: (place[s], 0))] * 2,
            [sds((n_tp, rows, local), BF)] * 3,
            [placed((rows, local))] * 3,
            (len(group),),
            scratch=[pltpu.VMEM((rows, width), BF)],
            prefetch=1,
            held=filled,
            us=2.0 * len(group),
        )
    query, key, value = (part.reshape(seq, local) for part in filled)
    d_low_late = after(d_low, normed_parts[-1], normed_parts[ups])
    d_low_first = [ring_up(d_low_late, n_tp), ring_down(d_low_late, n_tp)]
    strip = pl.BlockSpec((step_rows, local), lambda s, *_: (s, 0))
    mixed_heads, lse = call(
        attend_body,
        (order, query, key, value, bias_row),
        [strip, whole((seq, local)), whole((seq, local)), whole((1, seq))],
        [sds((n_tp, rows, local), BF), sds((steps, heads, step_rows), F32)],
        [whole((n_tp, rows, local)), lead((heads, step_rows))],
        (steps,),
        prefetch=1,
        us=10,
    )
    w_o_late = after(w_o, normed_parts[1])
    o_parts = call(
        lay_body,
        (order, *ring_gather(w_o_late, n_tp)),
        [whole(w_o.shape)] * n_tp,
        [sds((n_tp,) + w_o.shape[::-1], BF)],
        [whole((n_tp,) + w_o.shape[::-1])],
        (1,),
        prefetch=1,
        us=0.7,
    )[0]
    o_parts = jnp.concatenate([o_parts[at] for at in range(n_tp)], axis=1)
    full_o = put_back(w_order, dp_gather(o_parts, n_dp), 0)
    w_ffn = pad_to(jnp.concatenate([w_gu, w_down.T[None]], axis=0), 2, lanes)
    w_ffn = dp_gather(after(w_ffn, normed_parts[1]), n_dp)
    mixed_heads = after(mixed_heads, full_o, *d_low_first)
    mixed = lax.all_to_all(mixed_heads, "tensor", split_axis=0, concat_axis=0, tiled=True)

    inner_low, middle, normed_two = call(
        middle_body,
        (mixed, tokens_own, keep, full_o, norm_params, head_params),
        [
            whole(mixed.shape),
            own,
            whole((rows, 1)),
            whole(full_o.shape),
            whole(norm_params.shape),
            whole(head_params.shape),
        ],
        [sds((rows, width), BF), sds((rows, width), F32), sds((rows, width), BF)],
        [own] * 3,
        (1,),
        us=3,
    )
    two_parts = ring_gather(normed_two, n_tp)
    full_ffn = put_back(w_order, [after(part, normed_two) for part in w_ffn], 1)
    d_low_parts = gather_rest(d_low, d_low_first, n_tp, mixed)

    hidden_shape = (n_tp, rows, lanes)
    gu_block = pl.BlockSpec((2, width, lanes), lambda *_: (0, 0, 0))
    down_block = pl.BlockSpec((1, width, lanes), lambda *_: (2, 0, 0))
    d_ffn = [None] * n_tp
    near = [at for group in arrivals[:2] for at in group]
    for group in [near] + arrivals[2:]:
        outs = call(
            functools.partial(d_ffn_body, len(group)),
            (*(d_low_parts[at] for at in group), full_ffn),
            [own] * len(group) + [down_block],
            [sds((rows, lanes), F32)] * len(group),
            [whole((rows, lanes))] * len(group),
            (len(group),),
            scratch=[pltpu.VMEM((rows, width), BF)],
            us=1.4 * len(group),
        )
        for at, part in zip(group, outs):
            d_ffn[at] = part
    hidden_block = placed((rows, lanes))
    filled = ()
    for turn, group in enumerate(arrivals):
        if turn > 1:
            two_parts[group[0]] = after(two_parts[group[0]], filled[0])
        filled = call(
            functools.partial(ffn_body, len(group)),
            (
                jnp.array(group, jnp.int32),
                order,
                *(two_parts[at] for at in group),
                *(d_ffn[at] for at in group),
                full_ffn,
                ffn_local,
                unit_row,
            ),
            [own] * len(group)
            + [whole((rows, lanes))] * len(group)
            + [gu_block, whole(ffn_local.shape), whole(unit_row.shape)],
            [sds(hidden_shape, F32)] * 2 + [sds((n_tp, 8, rows), F32)],
            [hidden_block] * 2 + [ordered((8, rows))],
            (len(group),),
            scratch=[pltpu.VMEM((rows, width), BF), pltpu.VMEM((rows, lanes), F32)],
            prefetch=2,
            held=filled,
            us=1.2 + 2.2 * len(group),
        )
    gate, up, stats = filled
    stats = jnp.swapaxes(sum_shifts(stats, n_tp), 1, 2)
    filled, ffn_sums, d_two_parts = (), 0.0, [None] * n_tp
    for group in leavings:
        outs = call(
            functools.partial(ffn_back_body, len(group)),
            (
                jnp.array(group, jnp.int32),
                order,
                gate,
                up,
                *(d_ffn[at] for at in group),
                stats,
                full_ffn,
                ffn_local,
                unit_row,
            ),
            [hidden_block] * 2
            + [whole((rows, lanes))] * len(group)
            + [
                ordered((rows, 8)),
                gu_block,
                whole(ffn_local.shape),
                whole(unit_row.shape),
            ],
            [sds(hidden_shape, BF)] * 3
            + [sds((4, lanes), F32)]
            + [sds((rows, width), BF)] * len(group),
            [hidden_block] * 3 + [whole((4, lanes))] + [own] * len(group),
            (len(group),),
            scratch=[pltpu.VMEM((rows, lanes), F32)],
            prefetch=2,
            held=filled,
            us=3.7 * len(group),
        )
        filled = outs[:3]
        ffn_sums = ffn_sums + outs[3]
        for at, piece in zip(group, outs[4:]):
            d_two_parts[at] = piece
    ffn_low, d_gate, d_up = filled
    d_two_first = scatter_first(d_two_parts, n_tp)
    d_two_first = [after(d_two_first[0], *d_two_first[1:])] + d_two_first[1:]
    d_two_terms = scatter_rest(d_two_parts, d_two_first, n_tp)
    branch_parts = call(
        functools.partial(down_body, n_tp),
        (ffn_low, full_ffn),
        [lead((rows, lanes)), down_block],
        [sds((rows, width), BF)] * n_tp,
        [own] * n_tp,
        (n_tp,),
        us=2.8,
    )

    parity = (lax.axis_index("dp") % 2).astype(jnp.int32)[None]
    block = width // n_dp
    hidden_rows = [part.reshape(seq, lanes) for part in (d_gate, d_up, ffn_low)]
    grad_ffn = product([two_parts, d_low_parts], [hidden_rows[:2], hidden_rows[2:]], parity, block)
    grad_ffn = pair_sum(grad_ffn, n_dp)


    n_terms = len(d_two_terms)
    d_middle, d_branch, d_mixed_rows, mid_sums = call(
        functools.partial(middle_back_body, n_terms),
        (*d_two_terms, middle, dy_own, d_low, keep, mixed, full_o, norm_params, head_params),
        [own] * n_terms
        + [own] * 3
        + [
            whole((rows, 1)),
            whole(mixed.shape),
            whole(full_o.shape),
            whole(norm_params.shape),
            whole(head_params.shape),
        ],
        [
            sds((rows, width), F32),
            sds((rows, width), BF),
            sds((n_tp, rows, local), BF),
            sds((8, width), F32),
        ],
        [own, own, whole((n_tp, rows, local)), whole((8, width))],
        (1,),
        us=3.6,
    )
    d_mixed = lax.all_to_all(d_mixed_rows, "tensor", split_axis=0, concat_axis=0, tiled=True)
    d_mixed = after(d_mixed, grad_ffn)
    grad_ffn = dp_scatter(grad_ffn, n_dp)
    branch_parts = [after(part, d_mixed) for part in branch_parts]
    branch_first = scatter_first(branch_parts, n_tp)

    table = pl.BlockSpec((step_rows, LANES), lambda s, *_: (s, 0))
    all_rows = whole((seq, local))
    d_query, d_key, d_value, head_sums = call(
        attend_back_body,
        (
            order,
            query,
            d_mixed,
            lse,
            key,
            value,
            bias_col,
            cos_all,
            sin_all,
            cos_all,
            sin_all,
        ),
        [
            strip,
            whole(d_mixed.shape),
            lead((heads, step_rows)),
            all_rows,
            all_rows,
            whole((seq, 1)),
            table,
            table,
            whole((seq, LANES)),
            whole((seq, LANES)),
        ],
        [sds((seq, local), BF)] * 3 + [sds((8, local), F32)],
        [strip, all_rows, all_rows, whole((8, local))],
        (steps,),
        scratch=[pltpu.VMEM((seq, local), F32)] * 2,
        prefetch=1,
        us=24,
    )
    d_query = after(d_query, *branch_first)
    chunk = pl.BlockSpec((rows, local), lambda s, place, *_: (place[s], 0))
    d_one_parts = [None] * n_tp
    for group in leavings:
        outs = call(
            functools.partial(spread_back_body, len(group)),
            (jnp.array(group, jnp.int32), d_query, d_key, d_value, full_qkv),
            [chunk] * 3 + [whole(full_qkv.shape)],
            [sds((rows, width), BF)] * len(group),
            [own] * len(group),
            (len(group),),
            prefetch=1,
            us=1.0 * len(group),
        )
        for at, piece in zip(group, outs):
            d_one_parts[at] = piece
    d_proj = [after(part, *[d_one_parts[at] for at in leaving]) for part in (d_query, d_key, d_value)]
    *grad_late, along_normed = product(
        [normed_parts, [d_branch]], [d_proj, [inner_low]], parity, block, full_qkv
    )
    along_normed = along_normed.reshape(-1)
    shift_one = sum(
        jnp.sum(full_qkv[at].astype(F32) * head_sums[at : at + 1], axis=1) for at in range(3)
    )
    grad_late = pair_sum(grad_late, n_dp)

    d_one_first = scatter_first(d_one_parts, n_tp)
    arrived = [after(d_one_first[0], grad_late, grad_ffn)] + d_one_first[1:]
    sent = []
    d_one_terms = scatter_rest(d_one_parts, arrived, n_tp, sent)

    small = [along_normed, shift_one, mid_sums[:6].reshape(-1)]
    small += [head_sums[0], head_sums[2], ffn_sums[:, :units].reshape(-1)]
    small = jnp.concatenate(small)
    small_len = small.shape[0]
    small = pad_to(small, 0, ceil_to(small_len, 8 * LANES)).reshape(-1, LANES)
    small = sum_over(after(small, grad_ffn), "dp", n_dp)
    small_sum = small
    grad_late = dp_scatter(after(grad_late, small), n_dp)
    late_parts = grad_late
    small = after(small, *sent)
    small = [part.reshape(-1) for part in gather_small(small, n_tp)]
    head_at = 8 * width
    ffn_at = head_at + 2 * local
    norm_sums = sum_alike([part[:head_at] for part in small]).reshape(8, width)
    head_bias = jnp.zeros((2, width), F32)
    ffn_total = jnp.zeros((4, n_tp * units), F32)
    for s, part in enumerate(small):
        owner = (tp_index - s) % n_tp
        head_bias = lax.dynamic_update_slice(
            head_bias, part[head_at:ffn_at].reshape(2, local), (0, owner * local)
        )
        ffn_total = lax.dynamic_update_slice(
            ffn_total, part[ffn_at:small_len].reshape(4, units), (0, owner * units)
        )
    gain_one = (norm_sums[0:1] - norm_params[1:2] * norm_sums[1:2]) / norm_params[0:1]
    norm_total = jnp.concatenate([gain_one, norm_sums[1:6]], axis=0)
    head_total = jnp.concatenate([head_bias, norm_sums[6:8]], axis=0)

    grad_early = sum_parts(grad_ffn)
    grad_late = sum_parts(grad_late)
    grad_o = grad_late[:, 3 * local :].astype(BF).reshape(-1, n_tp, local).swapaxes(0, 1)
    grad_o = swap_sum(grad_o, n_tp).T
    grad_gu = jnp.stack([grad_early[:, :units], grad_early[:, lanes : lanes + units]])
    grad_down = grad_early[:, 2 * lanes : 2 * lanes + units].T
    grad_qkv = grad_late[:, : 3 * local].reshape(-1, 3, local).swapaxes(0, 1)

    branch_first = [after(branch_first[0], small_sum)] + branch_first[1:]
    branch_terms = scatter_rest(branch_parts, branch_first, n_tp)
    branch_terms[1] = after(branch_terms[1], late_parts)
    layer_out = call(
        functools.partial(layer_out_body, n_terms),
        (*branch_terms, middle, keep, norm_params),
        [own] * n_terms + [own, whole((rows, 1)), whole(norm_params.shape)],
        [sds((own_rows, width), BF)],
        [whole((own_rows, width))],
        (1,),
        us=2,
    )[0]
    d_one_terms[0] = after(d_one_terms[0], grad_late, norm_total, ffn_total)
    d_tokens = call(
        functools.partial(first_back_body, n_terms),
        (*d_one_terms, tokens[0], d_middle, norm_params),
        [own] * n_terms + [whole((own_rows, width)), own, whole(norm_params.shape)],
        [sds((own_rows, width), F32)],
        [whole((own_rows, width))],
        (1,),
        us=1.5,
    )[0]

    return (
        layer_out[None],
        d_tokens[None],
        grad_qkv,
        grad_o,
        grad_gu,
        grad_down,
        norm_total,
        head_total,
        ffn_total,
    )


def solution(mesh):
    placed = (
        P("dp", "tensor", None),
        P("dp", "tensor", None),
        P(None, "dp", "tensor"),
        P("tensor", "dp"),
        P(None, "dp", "tensor"),
        P("tensor", "dp"),
        P(),
        P(),
        P(),
        P("dp", None),
        P("dp"),
        P("dp", None, None),
    )
    return jax.shard_map(
        functools.partial(on_device, mesh.shape["dp"], mesh.shape["tensor"]),
        mesh=mesh,
        in_specs=placed,
        out_specs=(
            P("dp", "tensor", None),
            P("dp", "tensor", None),
            P(None, "dp", "tensor"),
            P("tensor", "dp"),
            P(None, "dp", "tensor"),
            P("tensor", "dp"),
            P(),
            P(),
            P(),
        ),
        check_vma=False,
    )
```
